128 devices in a mesh: dp: 16 (over y_hi, z, core), mp: 8 (over y_lo, x).
Axes of the slice: x: 4, y: 4 (y_hi: 2, y_lo: 2; y = y_hi * 2 + y_lo), z: 4, core: 2. Of those that a mesh axis runs over, the one named last changes fastest.
Arguments:
- latents: bfloat16 [32, 512, 1024], P('dp', 'mp'), may hold values from -6 to 6
- pixels: bfloat16 [32, 4096, 261], P('dp', 'mp'), may hold values from -6 to 6
- masks: int32 [32, 4096], P('dp', 'mp'), may hold values from 0 to 1, as said below
- cotangent: bfloat16 [32, 512, 1024], P('dp', 'mp'), may hold values from -6 to 6
- norm_latent: float32 [1024], replicated, may hold values from 0.5 to 1.5
- norm_pixel: float32 [261], replicated, may hold values from 0.5 to 1.5
- norm_feed: float32 [1024], replicated, may hold values from 0.5 to 1.5
- norm_self: float32 [1024], replicated, may hold values from 0.5 to 1.5
- norm_last: float32 [1024], replicated, may hold values from 0.5 to 1.5
- cross_query: bfloat16 [1024, 1024], P(None, 'mp'), may hold values from -0.1875 to 0.1875
- cross_key: bfloat16 [261, 1024], P(None, 'mp'), may hold values from -0.375 to 0.375
- cross_value: bfloat16 [261, 1024], P(None, 'mp'), may hold values from -0.375 to 0.375
- cross_out: bfloat16 [1024, 1024], P(None, 'mp'), may hold values from -0.75 to 0.75
- feed_in: bfloat16 [1024, 1024], P(None, 'mp'), may hold values from -0.1875 to 0.1875
- feed_out: bfloat16 [1024, 1024], P('mp'), may hold values from -0.1875 to 0.1875
- self_query: bfloat16 [1024, 1024], P(None, 'mp'), may hold values from -0.1875 to 0.1875
- self_key: bfloat16 [1024, 1024], P(None, 'mp'), may hold values from -0.1875 to 0.1875
- self_value: bfloat16 [1024, 1024], P(None, 'mp'), may hold values from -0.1875 to 0.1875
- self_out: bfloat16 [1024, 1024], P('mp'), may hold values from -0.75 to 0.75
- last_in: bfloat16 [1024, 1024], P(None, 'mp'), may hold values from -0.1875 to 0.1875
- last_out: bfloat16 [1024, 1024], P('mp'), may hold values from -0.1875 to 0.1875
Outputs:
- result: bfloat16 [32, 512, 1024], P('dp', 'mp')
- grad_latents: float32 [32, 512, 1024], P('dp', 'mp')
- grad_pixels: float32 [32, 4096, 261], P('dp', 'mp')
- grad_norm_latent: float32 [1024], replicated
- grad_norm_pixel: float32 [261], replicated
- grad_norm_feed: float32 [1024], replicated
- grad_norm_self: float32 [1024], replicated
- grad_norm_last: float32 [1024], replicated
- grad_cross_query: float32 [1024, 1024], P(None, 'mp')
- grad_cross_key: float32 [261, 1024], P(None, 'mp')
- grad_cross_value: float32 [261, 1024], P(None, 'mp')
- grad_cross_out: float32 [1024, 1024], P(None, 'mp')
- grad_feed_in: float32 [1024, 1024], P(None, 'mp')
- grad_feed_out: float32 [1024, 1024], P('mp')
- grad_self_query: float32 [1024, 1024], P(None, 'mp')
- grad_self_key: float32 [1024, 1024], P(None, 'mp')
- grad_self_value: float32 [1024, 1024], P(None, 'mp')
- grad_self_out: float32 [1024, 1024], P('mp')
- grad_last_in: float32 [1024, 1024], P(None, 'mp')
- grad_last_out: float32 [1024, 1024], P('mp')
The draws below stay inside these ranges and needn't reach their ends.
Inputs may be any that keep to these rules, and one draw needn't show every extreme that they name: `masks`: each item's kept slots form one rectangle of its 64 x 64 window (slot = row * 64 + column), both sides at least 32; some item keeps the full height of the window and some item exactly (32) squared slots.
All inputs are finite; a program needn't handle non-finite values.
Results may differ from the reference program's by a relative error of at most 0.035.
Values may be sent and summed in bfloat16 or wider, within the bound.
No kernel may reach another device: no remote copies, remote signals or barrier semaphores. Data moves between devices by JAX's collectives and lax.ppermute only.
A program may use at most 128 MiB of HBM per device.

```python
import jax
import jax.numpy as jnp
from jax import lax

D = 1024
C = 261
FF = 1024
HEADS = 8
NLAT = 512
SIDE = 64
SLOTS = 4096
ITEMS = 32


def draw_masks(key, part):
    key = jax.random.fold_in(key, 11)
    subkeys = jax.random.split(key, 5)
    half_side = SIDE // 2
    height = jax.random.randint(subkeys[0], (ITEMS,), half_side, SIDE + 1)
    breadth = jax.random.randint(subkeys[1], (ITEMS,), half_side, SIDE + 1)
    chosen = jax.random.permutation(subkeys[2], ITEMS)
    height = height.at[chosen[0]].set(SIDE)
    height = height.at[chosen[1]].set(half_side)
    breadth = breadth.at[chosen[1]].set(half_side)
    top_row = jax.random.randint(subkeys[3], (ITEMS,), 0, SIDE - height + 1)
    left_column = jax.random.randint(subkeys[4], (ITEMS,), 0, SIDE - breadth + 1)
    slot_ids = jnp.arange(SIDE * SIDE, dtype=jnp.int32)
    row_index = (slot_ids // SIDE)[None, :]
    column_index = (slot_ids % SIDE)[None, :]
    inside = (row_index >= top_row[:, None]) & (row_index < (top_row + height)[:, None])
    inside = inside & (column_index >= left_column[:, None]) & (column_index < (left_column + breadth)[:, None])
    return inside.astype(jnp.int32)


def levels(own_key, shape, shards, low, largest):
    gain = 1.0
    for dim, blocks in shards:
        draws = jax.random.uniform(jax.random.fold_in(jax.random.fold_in(own_key, 6), dim), (blocks,), jnp.float32, low / len(shards), largest / len(shards))
        gain = gain * jnp.repeat(jnp.exp(draws), shape[dim] // blocks).reshape((-1,) + (1,) * (len(shape) - 1 - dim))
    return gain


def noise(key, shape, deviation, reach, cuts=(), kind=jnp.bfloat16):
    drawn = deviation * jax.random.normal(key, shape, jnp.float32)
    if cuts:
        drawn = drawn * levels(key, shape, cuts, -0.22, 0.18)
    return jnp.clip(drawn, -reach, reach).astype(kind)


def setup_inputs(seed: int = 0) -> dict:
    streams_of = jax.random.split(jax.random.key(seed), 22)
    latents = noise(streams_of[0], (ITEMS, NLAT, D), 1.0, 6.0, ((0, 16), (1, 8)))
    pixels = noise(streams_of[1], (ITEMS, SLOTS, C), 1.0, 6.0, ((0, 16), (1, 8)))
    masks = draw_masks(jax.random.fold_in(streams_of[21], 71), 0)
    cotangent = noise(streams_of[3], (ITEMS, NLAT, D), 1.0, 6.0, ((0, 16), (1, 8)))
    norm_latent = jnp.clip(1.0 + 0.1 * jax.random.normal(streams_of[4], (D,), jnp.float32), 0.5, 1.5)
    norm_pixel = jnp.clip(1.0 + 0.1 * jax.random.normal(streams_of[5], (C,), jnp.float32), 0.5, 1.5)
    norm_feed = jnp.clip(1.0 + 0.1 * jax.random.normal(streams_of[6], (D,), jnp.float32), 0.5, 1.5)
    norm_self = jnp.clip(1.0 + 0.1 * jax.random.normal(streams_of[7], (D,), jnp.float32), 0.5, 1.5)
    norm_last = jnp.clip(1.0 + 0.1 * jax.random.normal(streams_of[8], (D,), jnp.float32), 0.5, 1.5)
    cross_query = noise(streams_of[9], (D, D), D ** -0.5, 0.1875, ((1, 8),))
    cross_key = noise(streams_of[10], (C, D), C ** -0.5, 0.375, ((1, 8),))
    cross_value = noise(streams_of[11], (C, D), C ** -0.5, 0.375, ((1, 8),))
    cross_out = noise(streams_of[12], (D, D), (D // 16) ** -0.5, 0.75, ((1, 8),))
    feed_in = noise(streams_of[13], (D, FF), D ** -0.5, 0.1875, ((1, 8),))
    feed_out = noise(streams_of[14], (FF, D), FF ** -0.5, 0.1875, ((0, 8),))
    self_query = noise(streams_of[15], (D, D), D ** -0.5, 0.1875, ((1, 8),))
    self_key = noise(streams_of[16], (D, D), D ** -0.5, 0.1875, ((1, 8),))
    self_value = noise(streams_of[17], (D, D), D ** -0.5, 0.1875, ((1, 8),))
    self_out = noise(streams_of[18], (D, D), (D // 16) ** -0.5, 0.75, ((0, 8),))
    last_in = noise(streams_of[19], (D, FF), D ** -0.5, 0.1875, ((1, 8),))
    last_out = noise(streams_of[20], (FF, D), FF ** -0.5, 0.1875, ((0, 8),))
    return {"latents": latents, "pixels": pixels, "masks": masks, "cotangent": cotangent, "norm_latent": norm_latent, "norm_pixel": norm_pixel, "norm_feed": norm_feed, "norm_self": norm_self, "norm_last": norm_last, "cross_query": cross_query, "cross_key": cross_key, "cross_value": cross_value, "cross_out": cross_out, "feed_in": feed_in, "feed_out": feed_out, "self_query": self_query, "self_key": self_key, "self_value": self_value, "self_out": self_out, "last_in": last_in, "last_out": last_out}


precise = lax.Precision.HIGHEST
epsilon = 1e-05
masked_score = -1e+30

@jax.custom_vjp
def low(v):
    return lax.optimization_barrier(v.astype(jnp.bfloat16)).astype(jnp.float32)

@jax.custom_vjp
def low_back(v):
    return v

def low_keep(v):
    return (low(v), None)

def low_pass(kept, grad):
    return (grad,)

def back_keep(v):
    return (v, None)

def back_low(kept, grad):
    return (low(grad),)
low.defvjp(low_keep, low_pass)
low_back.defvjp(back_keep, back_low)

def layer_norm(values, norm_gain):
    center = values - lax.optimization_barrier(jnp.mean(values, axis=-1, keepdims=True))
    spread = lax.optimization_barrier(jnp.mean(center * center, axis=-1, keepdims=True))
    return center * lax.rsqrt(spread + epsilon) * norm_gain

def round_both(values):
    return low(low_back(values))

def matmul_high(left_side, right_side):
    return jnp.dot(left_side, right_side, precision=precise)

def log_total(scores):
    peak_score = lax.optimization_barrier(jnp.max(scores, axis=-1, keepdims=True))
    return peak_score + jnp.log(lax.optimization_barrier(jnp.sum(jnp.exp(scores - peak_score), axis=-1, keepdims=True)))

def feed_branch(stream, norm_gain, weight_in, weight_out):
    hidden = low(layer_norm(stream, norm_gain))
    before = low_back(matmul_high(hidden, weight_in))
    active = low(jax.nn.gelu(before))
    return low_back(matmul_high(active, weight_out))

def cross_branch(latent_rows, pixel_rows, kept_slots, gain_latent, gain_pixel, weight_query, weight_key, weight_value, weight_out):
    inputs = low(layer_norm(pixel_rows, gain_pixel))
    normed = low(layer_norm(latent_rows, gain_latent))
    queries = round_both(matmul_high(normed, weight_query))
    key_rows = round_both(matmul_high(inputs, weight_key))
    values = round_both(matmul_high(inputs, weight_value))
    scores = low_back(matmul_high(queries, key_rows.T) * D ** (-0.5))
    scores = jnp.where(kept_slots[None, :] > 0, scores, masked_score)
    attention = jnp.exp(scores - log_total(scores))
    mixed_rows = round_both(matmul_high(low(attention), values))
    return low_back(matmul_high(mixed_rows, weight_out))

def self_branch(stream, norm_gain, weight_query, weight_key, weight_value, weight_out):
    hidden = low(layer_norm(stream, norm_gain))
    head_width = D // HEADS

    def split_heads(weight):
        return round_both(matmul_high(hidden, weight)).reshape(NLAT, HEADS, head_width)
    queries = split_heads(weight_query)
    key_rows = split_heads(weight_key)
    values = split_heads(weight_value)
    scores = low_back(jnp.einsum('qhe,khe->hqk', queries, key_rows, precision=precise) * head_width ** (-0.5))
    attention = jnp.exp(scores - log_total(scores))
    mixed_rows = round_both(jnp.einsum('hqk,khe->qhe', low(attention), values, precision=precise)).reshape(NLAT, D)
    return low_back(matmul_high(mixed_rows, weight_out))

def one_item(latent_rows, pixel_rows, kept_slots, weights):
    gain_latent, gain_pixel, gain_feed, gain_self, gain_last, cross_q, cross_k, cross_v, cross_o, feed_w1, feed_w2, self_q, self_k, self_v, self_o, last_w1, last_w2 = weights
    state_one = latent_rows + cross_branch(latent_rows, pixel_rows, kept_slots, gain_latent, gain_pixel, cross_q, cross_k, cross_v, cross_o)
    state_two = state_one + feed_branch(state_one, gain_feed, feed_w1, feed_w2)
    state_three = state_two + self_branch(state_two, gain_self, self_q, self_k, self_v, self_o)
    return state_three + feed_branch(state_three, gain_last, last_w1, last_w2)

def reference(latents, pixels, masks, cotangent, norm_latent, norm_pixel, norm_feed, norm_self, norm_last, cross_query, cross_key, cross_value, cross_out, feed_in, feed_out, self_query, self_key, self_value, self_out, last_in, last_out):
    floats = [weight.astype(jnp.float32) for weight in (norm_latent, norm_pixel, norm_feed, norm_self, norm_last, cross_query, cross_key, cross_value, cross_out, feed_in, feed_out, self_query, self_key, self_value, self_out, last_in, last_out)]

    def forward(latent_all, pixel_all, *weights):

        def per_item(operands):
            return one_item(operands[0], operands[1], operands[2], weights)
        return lax.map(jax.checkpoint(per_item), (latent_all, pixel_all, masks))
    result, pullback = jax.vjp(forward, latents.astype(jnp.float32), pixels.astype(jnp.float32), *floats)
    gradients = pullback(cotangent.astype(jnp.float32))
    return (result.astype(jnp.bfloat16), gradients[0], gradients[1], gradients[2], gradients[3], gradients[4], gradients[5], gradients[6], gradients[7], gradients[8], gradients[9], gradients[10], gradients[11], gradients[12], gradients[13], gradients[14], gradients[15], gradients[16], gradients[17], gradients[18])
```

```python
import jax
import jax.numpy as jnp
from jax import lax
from jax.sharding import PartitionSpec as P

D = 1024
C = 261
CP = 272
CH = 288
HALF = 144
HEADS = 8
HEAD = 128
MP = 8
ITEMS = 2
ROWS = 64
LOCAL = ITEMS * ROWS
SLOTS = 512
NLAT = 512
WIDE = 512
MEMBERS = 64
PART = 40
EPS = 1e-05
MASKED = -1e30
GELU_A = 0.044715
GELU_K = 0.7978845608028654

bf16 = jnp.bfloat16
f32 = jnp.float32

SWAP = [(i, i ^ 1) for i in range(16)]
CHIPS = [
    [(d * 2 + core) * MP + m for d in range(8) for m in range(MP)] for core in range(2)
]
COPIES = [[d * 2 + core for d in range(8)] for core in range(2)]


def dot(a, b):
    return lax.dot_general(a, b, (((1,), (0,)), ((), ())), preferred_element_type=f32)


def dot_t(a, b):
    return lax.dot_general(a, b, (((1,), (1,)), ((), ())), preferred_element_type=f32)


def t_dot(a, b):
    return dot(a.T, b)


def core_swap(x):
    return lax.ppermute(x, "dp", SWAP)


def exchange(x):
    return lax.all_to_all(x, "mp", 0, 0, tiled=True)


def to_all(x):
    return exchange(jnp.broadcast_to(x[None], (MP,) + x.shape))


def normal(v):
    center = v - jnp.mean(v, axis=-1, keepdims=True)
    spread = jnp.mean(center * center, axis=-1, keepdims=True)
    scale = lax.rsqrt(spread + EPS)
    return center * scale, scale


def normal_back(unit, scale, gain, upstream):
    grad_gain = jnp.sum(upstream * unit, axis=0, keepdims=True)
    grad_unit = upstream * gain
    inner = jnp.mean(grad_unit * unit, axis=-1, keepdims=True)
    grad = scale * (grad_unit - jnp.mean(grad_unit, axis=-1, keepdims=True) - unit * inner)
    return grad, grad_gain


def gelu_parts(v):
    square = v * v
    t = jnp.tanh(GELU_K * v * (1.0 + GELU_A * square))
    value = 0.5 * v * (1.0 + t)
    slope = 0.5 * (1.0 + t) + 0.5 * v * (1.0 - t * t) * GELU_K * (1.0 + 3.0 * GELU_A * square)
    return value, slope


def split3(v):
    high = v.astype(bf16)
    rest = v - high.astype(f32)
    middle = rest.astype(bf16)
    low = (rest - middle.astype(f32)).astype(bf16)
    return [high.astype(f32), middle.astype(f32), low.astype(f32)]


def join3(rows, start):
    return rows[start : start + 1] + rows[start + 1 : start + 2] + rows[start + 2 : start + 3]


def halves(core, own, other, axis):
    first = jnp.where(core == 0, own, other)
    second = jnp.where(core == 0, other, own)
    return jnp.concatenate([first, second], axis=axis)


def pick(core, v, own):
    take_low = core == 0 if own else core != 0
    return jnp.where(take_low, v[:, :WIDE], v[:, WIDE:])


def times_in(core, x, own, other):
    return dot_t(pick(core, x, True), own) + dot_t(pick(core, x, False), other)


def times_out(core, x, own, other):
    return halves(core, dot(x, own), dot(x, other), 1)


def feed_forward(core, stream, gain, win, wout):
    unit, scale = normal(stream)
    hidden = (unit * gain).astype(bf16)
    before = times_in(core, hidden, *win)
    active, slope = gelu_parts(before)
    active = active.astype(bf16)
    return times_out(core, active, *wout), (hidden, active, slope)


def feed_back(core, stream, gain, win, wout, saved, upstream):
    hidden, active, slope = saved
    dy = upstream.astype(bf16)
    grad_active = times_in(core, dy, *wout)
    grad_before = (grad_active * slope).astype(bf16)
    grad_hidden = times_out(core, grad_before, *win)
    unit, scale = normal(stream)
    grad, grad_gain = normal_back(unit, scale, gain, grad_hidden)
    return upstream + grad, grad_gain, dy, grad_before


def weight_grad(core, left, right):
    flipped = left.T
    own = dot(flipped, pick(core, right, True)).astype(bf16)
    other = dot(flipped, pick(core, right, False)).astype(bf16)
    return own.reshape(MP, HEAD, WIDE), other.reshape(MP, HEAD, WIDE)


def by_item(x):
    parts = x.reshape(MP, CP, ITEMS, ROWS)
    return [parts[:, :, i].transpose(1, 0, 2).reshape(CP, NLAT) for i in range(ITEMS)]


def by_peer(items):
    parts = jnp.stack([v.reshape(CP, MP, ROWS) for v in items], axis=2)
    return parts.transpose(1, 0, 2, 3).reshape(MP, CP, LOCAL)


def rows_of(x, item):
    return x.reshape(MP, ITEMS, ROWS, HEAD)[:, item].reshape(NLAT, HEAD)


def rows_back(items):
    return jnp.stack([v.reshape(MP, ROWS, HEAD) for v in items], axis=1).reshape(
        MP * LOCAL, HEAD
    )


def body(
    latents,
    pixels,
    masks,
    cotangent,
    norm_latent,
    norm_pixel,
    norm_feed,
    norm_self,
    norm_last,
    cross_query,
    cross_key,
    cross_value,
    cross_out,
    feed_in,
    feed_out,
    self_query,
    self_key,
    self_value,
    self_out,
    last_in,
    last_out,
):
    core = lax.axis_index("dp") % 2
    mine = lax.axis_index("mp")
    row_ids = lax.broadcasted_iota(jnp.int32, (CP, 1), 0)
    gain_latent, gain_feed, gain_self, gain_last = (
        g[None, :] for g in (norm_latent, norm_feed, norm_self, norm_last)
    )

    def own_half(x, keep):
        low, high = x[:, :WIDE], x[:, WIDE:]
        return jnp.where((core == 0) == keep, low, high)

    def gather_pack(weights):
        pack = jnp.stack([own_half(w, True) for w in weights])
        own = lax.all_gather(pack, "mp")
        other = core_swap(own)
        return [
            (own[:, j].reshape(D, WIDE), other[:, j].reshape(D, WIDE))
            for j in range(len(weights))
        ]

    win, wout = gather_pack([feed_in.T, feed_out])
    wself, last_win, last_wout = gather_pack([self_out, last_in.T, last_out])

    key_rows = jnp.pad(cross_key, ((0, CH - C), (0, 0)))
    value_rows = jnp.pad(cross_value, ((0, CH - C), (0, 0)))

    def core_rows(x):
        return jnp.where(core == 0, x[:HALF], x[HALF:])

    partial = dot_t(core_rows(key_rows), cross_query).astype(bf16)
    partial = partial.reshape(HALF, MP, HEAD).transpose(1, 0, 2)
    shared = jnp.broadcast_to(core_rows(value_rows)[None], (MP, HALF, HEAD))
    got = exchange(jnp.concatenate([partial, shared], axis=1))
    score_part = jnp.sum(got[:, :HALF].astype(f32), axis=0).astype(bf16)
    value_half = got[:, HALF:].transpose(1, 0, 2).reshape(HALF, D)
    mix_part = dot(value_half, cross_out).astype(bf16)
    got = to_all(jnp.concatenate([score_part, mix_part], axis=0))
    merged = got.reshape(MP, 2, HALF, HEAD).transpose(1, 2, 0, 3).reshape(2, HALF, D)
    merged = jnp.concatenate([merged, value_half[None]], axis=0)
    crossed = core_swap(merged)
    score_map, mix_map, value_full = (
        halves(core, merged[j], crossed[j], 0)[:CP] for j in range(3)
    )

    latent_rows = latents.reshape(LOCAL, D).astype(f32)
    latent_unit, latent_scale = normal(latent_rows)
    normed = (latent_unit * gain_latent).astype(bf16)
    asked = dot_t(score_map, normed) * (D**-0.5)
    asked = jnp.where(row_ids < C, asked, jnp.where(row_ids == C, 1.0, 0.0)).astype(bf16)
    asked_all = by_item(to_all(asked))

    pixel_rows = pixels.reshape(ITEMS * SLOTS, C).astype(f32)
    pixel_unit, pixel_scale = normal(pixel_rows)
    gain_pixel = norm_pixel[None, :]
    inputs = (pixel_unit * gain_pixel).astype(bf16)
    bias = jnp.where(masks.reshape(ITEMS * SLOTS, 1) > 0, 0.0, MASKED).astype(bf16)
    inputs = jnp.concatenate(
        [inputs, bias, jnp.zeros((ITEMS * SLOTS, CP - C - 1), bf16)], axis=1
    ).reshape(ITEMS, SLOTS, CP)

    sums = []
    for i in range(ITEMS):
        scores = dot(inputs[i], asked_all[i])
        peak = jnp.max(scores, axis=0, keepdims=True)
        weight = jnp.exp(scores - peak)
        total = jnp.sum(weight, axis=0, keepdims=True)
        mixed = t_dot(inputs[i], weight.astype(bf16))
        mixed = jnp.where(row_ids < C, mixed, 0.0)
        for offset, row in enumerate(split3(peak) + split3(total)):
            mixed = jnp.where(row_ids == C + 1 + offset, row, mixed)
        sums.append(mixed.astype(bf16))
    got = exchange(by_peer(sums)).astype(f32)
    peaks = [join3(got[s], C + 1) for s in range(MP)]
    totals = [join3(got[s], C + 4) for s in range(MP)]
    peak = peaks[0]
    for s in range(1, MP):
        peak = jnp.maximum(peak, peaks[s])
    total, mixed = 0.0, 0.0
    for s in range(MP):
        share = jnp.exp(peaks[s] - peak)
        total = total + share * totals[s]
        mixed = mixed + share * got[s]
    mixed = jnp.where(row_ids < C, mixed / total, 0.0)
    lse = peak + jnp.log(total)
    mixed_low = mixed.astype(bf16)

    state_one = latent_rows + t_dot(mixed_low, mix_map)
    branch, feed_saved = feed_forward(core, state_one, gain_feed, win, wout)
    state_two = state_one + branch
    self_unit, self_scale = normal(state_two)
    hidden = (self_unit * gain_self).astype(bf16)

    hidden_all = to_all(hidden).reshape(MP * LOCAL, D)
    queries, keys, values = (
        dot(hidden_all, w).astype(bf16) for w in (self_query, self_key, self_value)
    )
    head_scale = HEAD**-0.5
    outs, logs = [], []
    for i in range(ITEMS):
        q, k, v = rows_of(queries, i), rows_of(keys, i), rows_of(values, i)
        scores = dot_t(k, q) * head_scale
        top = jnp.max(scores, axis=0, keepdims=True)
        log = top + jnp.log(jnp.sum(jnp.exp(scores - top), axis=0, keepdims=True))
        attention = jnp.exp(scores - log).astype(bf16)
        outs.append(dot(v.T, attention).T.astype(bf16))
        logs.append(log)
    got = exchange(rows_back(outs).reshape(MP, LOCAL, HEAD))
    heads_out = got.transpose(1, 0, 2).reshape(LOCAL, D)
    state_three = state_two + times_out(core, heads_out, *wself)
    branch, last_saved = feed_forward(core, state_three, gain_last, last_win, last_wout)
    result = (state_three + branch).astype(bf16)

    upstream = cotangent.reshape(LOCAL, D).astype(f32)
    upstream, grad_gain_last, dy, grad_before = feed_back(
        core, state_three, gain_last, last_win, last_wout, last_saved, upstream
    )
    grad_last_out = weight_grad(core, last_saved[1], dy)
    grad_last_in = weight_grad(core, grad_before, last_saved[0])
    dy = upstream.astype(bf16)
    grad_heads = times_in(core, dy, *wself).astype(bf16)
    grad_self_out = weight_grad(core, heads_out, dy)

    got = exchange(grad_heads.reshape(LOCAL, MP, HEAD).transpose(1, 0, 2))
    grad_heads = got.reshape(MP * LOCAL, HEAD)
    dqs, dks, dvs = [], [], []
    for i in range(ITEMS):
        q, k, v = rows_of(queries, i), rows_of(keys, i), rows_of(values, i)
        g = rows_of(grad_heads, i)
        attention = jnp.exp(dot_t(k, q) * head_scale - logs[i])
        grad_attention = dot_t(v, g)
        delta = jnp.sum(attention * grad_attention, axis=0, keepdims=True)
        dvs.append(dot(attention.astype(bf16), g).astype(bf16))
        grad_scores = (attention * (grad_attention - delta)).astype(bf16)
        dks.append((dot(grad_scores, q) * head_scale).astype(bf16))
        dqs.append((dot(k.T, grad_scores).T * head_scale).astype(bf16))
    grad_query, grad_key, grad_value = rows_back(dqs), rows_back(dks), rows_back(dvs)
    grad_hidden = (
        dot_t(grad_query, self_query)
        + dot_t(grad_key, self_key)
        + dot_t(grad_value, self_value)
    )
    flipped = hidden_all.T
    grad_qkv = [dot(flipped, g) for g in (grad_query, grad_key, grad_value)]
    got = exchange(grad_hidden.astype(bf16).reshape(MP, LOCAL, D))
    grad_hidden = jnp.sum(got.astype(f32), axis=0)
    grad, grad_gain_self = normal_back(self_unit, self_scale, gain_self, grad_hidden)
    upstream = upstream + grad
    upstream, grad_gain_feed, dy, grad_before = feed_back(
        core, state_one, gain_feed, win, wout, feed_saved, upstream
    )
    grad_feed_out = weight_grad(core, feed_saved[1], dy)
    grad_feed_in = weight_grad(core, grad_before, feed_saved[0])
    dy = upstream.astype(bf16)
    grad_mixed = dot_t(mix_map, dy)
    delta = jnp.sum(grad_mixed * mixed, axis=0, keepdims=True)
    mix_sum = dot(mixed_low, dy)
    sent = jnp.where(row_ids < C, grad_mixed, 0.0)
    for offset, row in enumerate(split3(lse) + split3(delta)):
        sent = jnp.where(row_ids == C + 1 + offset, row, sent)
    told_all = by_item(to_all(sent.astype(bf16)))

    partials, grad_inputs = [], []
    for i in range(ITEMS):
        told = told_all[i].astype(f32)
        log, delta = join3(told, C + 1), join3(told, C + 4)
        grad_mixed_all = jnp.where(row_ids < C, told, 0.0).astype(bf16)
        attention = jnp.exp(dot(inputs[i], asked_all[i]) - log)
        grad_attention = dot(inputs[i], grad_mixed_all)
        grad_scores = (attention * (grad_attention - delta)).astype(bf16)
        grad_inputs.append(
            dot_t(grad_scores, asked_all[i]) + dot_t(attention.astype(bf16), grad_mixed_all)
        )
        partials.append(t_dot(inputs[i], grad_scores).astype(bf16))
    got = exchange(by_peer(partials))
    grad_asked = jnp.sum(got.astype(f32), axis=0) * (D**-0.5)
    grad_asked = jnp.where(row_ids < C, grad_asked, 0.0).astype(bf16)
    score_sum = dot(grad_asked, normed)
    grad_normed = t_dot(grad_asked, score_map)
    grad, grad_gain_latent = normal_back(latent_unit, latent_scale, gain_latent, grad_normed)
    grad_latents = upstream + grad
    grad_inputs = jnp.concatenate(grad_inputs, axis=0)[:, :C]
    grad_pixels, grad_gain_pixel = normal_back(
        pixel_unit, pixel_scale, gain_pixel, grad_inputs
    )

    gains = jnp.concatenate(
        [
            grad_gain_latent,
            grad_gain_feed,
            grad_gain_self,
            grad_gain_last,
            jnp.pad(grad_gain_pixel, ((0, 0), (0, D - C))),
        ],
        axis=0,
    )
    high = gains.astype(bf16)
    low = (gains - high.astype(f32)).astype(bf16)
    both = jnp.concatenate([high, low], axis=0)
    score_sum = jnp.concatenate([score_sum[:C].astype(bf16), both], axis=0)
    score_sum = jnp.pad(score_sum, ((0, MP * PART - C - 10), (0, 0)))
    mix_sum = jnp.pad(mix_sum.astype(bf16), ((0, MP * PART - CP), (0, 0)))
    kept = jnp.where(core == 0, score_sum, mix_sum)
    given = jnp.where(core == 0, mix_sum, score_sum)
    total = kept.astype(f32) + core_swap(given).astype(f32)
    total = total.astype(bf16).reshape(MP, PART, MP, HEAD).transpose(0, 2, 1, 3)
    got = lax.all_to_all(
        total.reshape(MEMBERS, PART, HEAD),
        ("dp", "mp"),
        0,
        0,
        tiled=True,
        axis_index_groups=CHIPS,
    )
    total = jnp.sum(got.astype(f32), axis=0).astype(bf16)
    got = lax.all_to_all(
        jnp.broadcast_to(total[None], (MEMBERS, PART, HEAD)),
        ("dp", "mp"),
        0,
        0,
        tiled=True,
        axis_index_groups=CHIPS,
    )
    total = got.reshape(MP, MP, PART, HEAD).transpose(0, 2, 1, 3).reshape(MP * PART, D)
    crossed = core_swap(total)
    score_sum = jnp.where(core == 0, total, crossed)
    mix_sum = jnp.where(core == 0, crossed, total)[:CP]
    both = score_sum[C : C + 10].astype(f32)
    gains = both[:5] + both[5:]
    score_sum = score_sum[:CP]
    out_rows = lax.all_to_all(
        cross_out.reshape(MP, HEAD, HEAD), "mp", 0, 0, tiled=True
    )
    out_rows = out_rows.transpose(1, 0, 2).reshape(HEAD, D)
    grad_cross_query = t_dot(score_sum, key_rows[:CP])
    grad_cross_key = dot(score_sum, cross_query)[:C]
    own_mix = lax.dynamic_slice_in_dim(mix_sum, mine * HEAD, HEAD, 1)
    grad_cross_out = t_dot(value_full, own_mix)
    grad_cross_value = dot_t(mix_sum, out_rows)[:C]

    def reduce_pack(pairs):
        own = jnp.stack([p[0] for p in pairs], axis=1)
        other = jnp.stack([p[1] for p in pairs], axis=1)
        pack = (own.astype(f32) + core_swap(other).astype(f32)).astype(bf16)
        pack = lax.psum_scatter(pack, "mp")
        pack = lax.psum(pack, "dp", axis_index_groups=COPIES)
        crossed = core_swap(pack)
        return [
            halves(core, pack[j], crossed[j], 1).astype(f32) for j in range(len(pairs))
        ]

    grad_self_out, grad_last_in, grad_last_out = reduce_pack(
        [grad_self_out, grad_last_in, grad_last_out]
    )
    grad_feed_in, grad_feed_out = reduce_pack([grad_feed_in, grad_feed_out])
    grad_qkv = lax.psum(jnp.stack(grad_qkv).astype(bf16), "dp").astype(f32)
    shape = (ITEMS, ROWS, D)
    return (
        result.reshape(shape),
        grad_latents.reshape(shape),
        grad_pixels.reshape(ITEMS, SLOTS, C),
        gains[0],
        gains[4, :C],
        gains[1],
        gains[2],
        gains[3],
        grad_cross_query,
        grad_cross_key,
        grad_cross_value,
        grad_cross_out,
        grad_feed_in.T,
        grad_feed_out,
        grad_qkv[0],
        grad_qkv[1],
        grad_qkv[2],
        grad_self_out,
        grad_last_in.T,
        grad_last_out,
    )


def solution(mesh):
    rows = P("dp", "mp", None)
    columns = P(None, "mp")
    depth = P("mp", None)
    return jax.shard_map(
        body,
        mesh=mesh,
        in_specs=(rows, rows, P("dp", "mp"), rows)
        + (P(),) * 5
        + (columns,) * 5
        + (depth,)
        + (columns,) * 3
        + (depth, columns, depth),
        out_specs=(rows,) * 3
        + (P(),) * 5
        + (columns,) * 5
        + (depth,)
        + (columns,) * 3
        + (depth, columns, depth),
        check_vma=False,
    )
```

```python
import functools

import jax
import jax.numpy as jnp
from jax import lax
from jax.experimental import pallas as pl
from jax.experimental.pallas import tpu as pltpu
from jax.sharding import PartitionSpec as P

D = 1024
C = 261
CP = 272
CH = 288
HALF = 144
HEADS = 8
HEAD = 128
MP = 8
ITEMS = 2
ROWS = 64
LOCAL = ITEMS * ROWS
SLOTS = 512
NLAT = 512
WIDE = 512
MEMBERS = 64
PART = 80
QUART = 4
LIMIT = 32 << 20
EPS = 1e-05
MASKED = -1e30
GELU_A = 0.044715
GELU_K = 0.7978845608028654

bf16 = jnp.bfloat16
f32 = jnp.float32

SWAP = [(i, i ^ 1) for i in range(16)]
CHIPS = [
    [(d * 2 + core) * MP + m for d in range(8) for m in range(MP)] for core in range(2)
]
DEPTH = [
    [((y * 4 + z) * 2 + c, (y * 4 + (z + k) % 4) * 2 + c) for y in range(2) for z in range(4) for c in range(2)]
    for k in range(4)
]
FAR = [(i, i ^ 8) for i in range(16)]
COPIES = [[d * 2 + core for d in range(8)] for core in range(2)]
ALONG_Z = [[(y * 4 + z) * 2 + core for z in range(4)] for y in range(2) for core in range(2)]


def dot(a, b):
    return lax.dot_general(a, b, (((1,), (0,)), ((), ())), preferred_element_type=f32)


def dot_t(a, b):
    return lax.dot_general(a, b, (((1,), (1,)), ((), ())), preferred_element_type=f32)


def t_dot(a, b):
    return dot(a.T, b)


def cost(micros):
    return pl.CostEstimate(
        flops=int(micros * 1e7), bytes_accessed=int(micros * 2e4), transcendentals=0
    )


class Arriving:
    def __init__(self, ref, copy):
        self.ref, self.copy, self.shape = ref, copy, ref.shape

    def settle(self):
        if self.copy is not None:
            self.copy.wait()
        self.copy = None

    def __getitem__(self, index):
        self.settle()
        return self.ref[index]


class Leaving:
    def __init__(self, ref, copy):
        self.ref, self.copy, self.shape, self.left = ref, copy, ref.shape, False

    def leave(self):
        if not self.left:
            self.copy.start()
        self.left = True

    def __getitem__(self, index):
        return self.ref[index]

    def __setitem__(self, index, value):
        self.ref[index] = value
        if index is Ellipsis:
            self.leave()


def run(kernel, micros, outs, *args, scratch=(), far=(), hot=(), hot_outs=(0,)):
    specs, homes = [], []
    for n, a in enumerate(args):
        if jnp.ndim(a) == 1 and a.dtype == jnp.int32:
            space = pltpu.SMEM
        elif n in hot:
            space = pltpu.VMEM
        else:
            space = pltpu.HBM
            if n not in far:
                homes.append(n)
        specs.append(pl.BlockSpec(memory_space=space))
    out_homes = [n for n in range(len(outs)) if n not in hot_outs]
    buffers = [pltpu.VMEM(args[n].shape, args[n].dtype) for n in homes]
    buffers += [pltpu.VMEM(*outs[n]) for n in out_homes]

    def wrapped(*refs):
        refs = list(refs)
        sems, refs = refs[-1], refs[:-1]
        given, refs = refs[: len(args)], refs[len(args) :]
        made, refs = refs[: len(outs)], refs[len(outs) :]
        own, refs = refs[: len(scratch)], refs[len(scratch) :]
        for k, n in enumerate(homes):
            copy = pltpu.make_async_copy(given[n], refs[k], sems.at[k])
            copy.start()
            given[n] = Arriving(refs[k], copy)
        for k, n in enumerate(out_homes, len(homes)):
            made[n] = Leaving(refs[k], pltpu.make_async_copy(refs[k], made[n], sems.at[k]))
        kernel(*given, *made, *own)
        for n in homes:
            given[n].settle()
        for n in out_homes:
            made[n].leave()
        for n in out_homes:
            made[n].copy.wait()

    return pl.pallas_call(
        wrapped,
        out_shape=[
            jax.ShapeDtypeStruct(*out) if n in hot_outs else pltpu.HBM(*out)
            for n, out in enumerate(outs)
        ],
        in_specs=specs,
        out_specs=[
            pl.BlockSpec(memory_space=pltpu.VMEM if n in hot_outs else pltpu.HBM)
            for n in range(len(outs))
        ],
        scratch_shapes=[
            *scratch,
            *buffers,
            pltpu.SemaphoreType.DMA((max(1, len(buffers)),)),
        ],
        compiler_params=pltpu.CompilerParams(vmem_limit_bytes=LIMIT),
        cost_estimate=cost(micros),
    )(
        *(
            pltpu.with_memory_space_constraint(a, pltpu.HBM) if n in homes or n in far else a
            for n, a in enumerate(args)
        )
    )


def after(x, *waits):
    x, *waits = lax.optimization_barrier((x, *waits))
    return x, waits


def core_swap(x):
    return lax.ppermute(x, "dp", SWAP)


def exchange(x):
    return lax.all_to_all(x, "mp", 0, 0, tiled=True)


def to_all(x):
    return exchange(jnp.broadcast_to(x[None], (MP,) + x.shape))


def grouped(x, axes, groups):
    return lax.all_to_all(x, axes, 0, 0, tiled=True, axis_index_groups=groups)


def grouped_all(x, axes, groups):
    return grouped(jnp.broadcast_to(x[None], (len(groups[0]),) + x.shape), axes, groups)


def added(x):
    return jnp.sum(x.astype(f32), axis=0).astype(bf16)


def normal(v):
    center = v - jnp.mean(v, axis=-1, keepdims=True)
    spread = jnp.mean(center * center, axis=-1, keepdims=True)
    scale = lax.rsqrt(spread + EPS)
    return center * scale, scale


def normal_back(unit, scale, gain, upstream):
    grad_gain = jnp.sum(upstream * unit, axis=0, keepdims=True)
    grad_unit = upstream * gain
    inner = jnp.mean(grad_unit * unit, axis=-1, keepdims=True)
    grad = scale * (grad_unit - jnp.mean(grad_unit, axis=-1, keepdims=True) - unit * inner)
    return grad, grad_gain


def gelu_parts(v):
    square = v * v
    t = jnp.tanh(GELU_K * v * (1.0 + GELU_A * square))
    value = 0.5 * v * (1.0 + t)
    slope = 0.5 * (1.0 + t) + 0.5 * v * (1.0 - t * t) * GELU_K * (1.0 + 3.0 * GELU_A * square)
    return value, slope


def split3(v):
    high = v.astype(bf16).astype(f32)
    middle = (v - high).astype(bf16).astype(f32)
    return [high, middle, v - high - middle]


def join3(rows, start):
    return rows[start : start + 1] + rows[start + 1 : start + 2] + rows[start + 2 : start + 3]


def halves(core, own, other, axis):
    first = jnp.where(core == 0, own, other)
    second = jnp.where(core == 0, other, own)
    return jnp.concatenate([first, second], axis=axis)


def pick(core, v, own):
    take_low = core == 0 if own else core != 0
    return jnp.where(take_low, v[:, :WIDE], v[:, WIDE:])


def pick_rows(core, v, own):
    take_low = core == 0 if own else core != 0
    return jnp.where(take_low, v[:HALF], v[HALF:])


def full_shape(count):
    return [
        pltpu.VMEM((count, MP, HEAD, D), bf16),
        pltpu.SemaphoreType.DMA((count, 2, QUART)),
    ]


def fetch_all(ids_ref, pieces, full_ref, sems):
    core = ids_ref[0]
    copies = []
    for j in range(full_ref.shape[0]):
        for side, ref in enumerate(pieces):
            half = core if side == 0 else 1 - core
            for q in range(QUART):
                columns = pl.ds(pl.multiple_of((half * QUART + q) * HEAD, HEAD), HEAD)
                copies.append(
                    pltpu.make_async_copy(
                        ref.at[q, :, j], full_ref.at[j, :, :, columns], sems.at[j, side, q]
                    )
                )
                copies[-1].start()
    return copies


def arrive(copies, j):
    for copy in copies[j * 2 * QUART : (j + 1) * 2 * QUART]:
        copy.wait()


def matrix(full_ref, j):
    return full_ref[j].reshape(D, D)


def times_in(x, full_ref, j):
    return dot_t(x, matrix(full_ref, j))


def times_out(x, full_ref, j):
    return dot(x, matrix(full_ref, j))


def store_blocks(ids_ref, grad, own_ref, other_ref, place):
    core = ids_ref[0]
    for first, ref in ((True, own_ref), (False, other_ref)):
        half = pick(core, grad, first).astype(bf16)
        for q in range(QUART):
            ref[q, place] = half[:, q * HEAD : (q + 1) * HEAD]


def stacked(own, got):
    return jnp.concatenate([own, got], axis=0)


def store_grad(left, right, own_ref, j, count):
    flipped = left.T
    for s in range(MP):
        grad = dot(flipped[s * HEAD : (s + 1) * HEAD], right).astype(bf16)
        for q in range(QUART):
            own_ref[q, s * count + j] = grad[:, q * HEAD : (q + 1) * HEAD]


def side_by_side(ref, start):
    return jnp.concatenate([ref[s, start : start + HALF] for s in range(MP)], axis=1)


def lane_halves():
    return lax.broadcasted_iota(jnp.int32, (1, HEAD), 1) < ROWS


def turned(x):
    return pltpu.roll(x, ROWS, 1)


def to_items(ref):
    low = lane_halves()
    items = [[], []]
    for p in range(0, MP, 2):
        a, b = ref[p].astype(f32), ref[p + 1].astype(f32)
        items[0].append(jnp.where(low, a, turned(b)))
        items[1].append(jnp.where(low, turned(a), b))
    return [jnp.concatenate(v, axis=1) for v in items]


def store_by_peer(ref, first, second):
    low = lane_halves()
    for p in range(0, MP, 2):
        x, y = (v[:, p * ROWS : (p + 2) * ROWS] for v in (first, second))
        ref[p] = jnp.where(low, x, turned(y)).astype(bf16)
        ref[p + 1] = jnp.where(low, turned(x), y).astype(bf16)


def with_tail(x, rows):
    ids = lax.broadcasted_iota(jnp.int32, (CP - 256, 1), 0) + 256
    tail = jnp.where(ids < C, x[256:CP], 0.0)
    for offset, row in enumerate(rows):
        tail = jnp.where(ids == C + 1 + offset, row, tail)
    return jnp.concatenate([x[:256], tail], axis=0)


def map_start_kernel(
    ids_ref,
    key_ref,
    query_ref,
    value_ref,
    feed_in_ref,
    feed_out_ref,
    self_out_ref,
    last_in_ref,
    last_out_ref,
    out_ref,
    sent_ref,
    pad_ref,
):
    core = ids_ref[0]
    span = pl.ds(pl.multiple_of((core * QUART + ids_ref[1]) * HEAD, HEAD), HEAD)
    tiles = [
        feed_in_ref[span, :].T,
        feed_out_ref[:, span],
        self_out_ref[:, span],
        last_in_ref[span, :].T,
        last_out_ref[:, span],
    ]
    pad_ref[...] = jnp.zeros(pad_ref.shape, f32)
    pad_ref[0, :C] = key_ref[...].astype(f32)
    pad_ref[1, :C] = value_ref[...].astype(f32)
    key = jnp.where(core == 0, pad_ref[0, :HALF], pad_ref[0, HALF:]).astype(bf16)
    value = jnp.where(core == 0, pad_ref[1, :HALF], pad_ref[1, HALF:]).astype(bf16)
    for s in range(MP):
        block = query_ref[s * HEAD : (s + 1) * HEAD]
        sent_ref[s, :HALF] = dot_t(key, block).astype(bf16)
        sent_ref[s, HALF:CH] = value
        for j, tile in enumerate(tiles):
            sent_ref[s, CH + j * HEAD : CH + (j + 1) * HEAD] = tile
        sent_ref[s, CH + 5 * HEAD :] = out_ref[s * HEAD : (s + 1) * HEAD]


def map_sum_kernel(got_ref, out_ref, sent_ref, value_ref, feed_ref, last_ref, rows_ref):
    for s in range(MP):
        for j in range(5):
            tile = got_ref[s, CH + j * HEAD : CH + (j + 1) * HEAD]
            if j < 2:
                feed_ref[s, j] = tile
            else:
                last_ref[s, j - 2] = tile
        rows_ref[s] = got_ref[s, CH + 5 * HEAD :]
    feed_ref.leave()
    score = got_ref[0, :HALF].astype(f32)
    for s in range(1, MP):
        score = score + got_ref[s, :HALF].astype(f32)
    value = side_by_side(got_ref, HALF)
    value_ref[...] = value
    score = score.astype(bf16)
    mix = dot(value, out_ref[...]).astype(bf16)
    for s in range(MP):
        sent_ref[s, :HALF] = score
        sent_ref[s, HALF:] = mix


def asked_kernel(core_ref, own_ref, other_ref, latent_ref, gain_ref, sent_ref, cross_ref):
    core = core_ref[0]
    unit, _ = normal(latent_ref[...].astype(f32))
    normed = (unit * gain_ref[...]).astype(bf16)
    cross_ref[...] = pick(core, normed, False)
    asked = halves(
        core, dot_t(side_by_side(own_ref, 0), normed), dot_t(side_by_side(other_ref, 0), normed), 0
    )
    ids = lax.broadcasted_iota(jnp.int32, (CP, 1), 0)
    asked = jnp.where(ids < C, asked[:CP] * (D**-0.5), jnp.where(ids == C, 1.0, 0.0))
    asked = asked.astype(bf16)
    for s in range(MP):
        sent_ref[s] = asked


def pixel_kernel(pixel_ref, mask_ref, gain_ref, rows_ref, flat_ref, pad_ref):
    unit, _ = normal(pixel_ref[...].astype(f32))
    pad_ref[...] = jnp.zeros(pad_ref.shape, f32)
    pad_ref[:, :C] = unit * gain_ref[...]
    flat = pad_ref[...].T[:CP]
    bias = jnp.where(mask_ref[...] > 0, 0.0, MASKED)
    bias = jnp.concatenate([bias[i : i + 1] for i in range(ITEMS)], axis=1)
    ids = lax.broadcasted_iota(jnp.int32, (CP, 1), 0)
    flat = jnp.where(ids == C, bias, flat)
    flat_ref[...] = flat.astype(bf16)
    lanes = lax.broadcasted_iota(jnp.int32, (1, CP), 1)
    rows_ref[...] = flat.T.astype(bf16)


def cross_kernel(rows_ref, flat_ref, asked_ref, sent_ref, items_ref):
    sums = []
    for i, asked in enumerate(to_items(asked_ref)):
        asked = asked.astype(bf16)
        items_ref[i] = asked
        slots = slice(i * SLOTS, (i + 1) * SLOTS)
        scores = dot(rows_ref[slots], asked)
        peak = jnp.max(scores, axis=0, keepdims=True)
        weight = jnp.exp(scores - peak)
        total = jnp.sum(weight, axis=0, keepdims=True)
        mixed = dot(flat_ref[:, slots], weight.astype(bf16))
        sums.append(with_tail(mixed, split3(peak) + split3(total)))
    store_by_peer(sent_ref, *sums)


def feed_forward(stream, gain, copies, full_ref, j, hidden_ref, active_ref, slope_ref):
    unit, _ = normal(stream)
    hidden = (unit * gain).astype(bf16)
    hidden_ref[...] = hidden
    arrive(copies, j)
    active, slope = gelu_parts(times_in(hidden, full_ref, j))
    active = active.astype(bf16)
    active_ref[...] = active
    slope_ref[...] = slope
    arrive(copies, j + 1)
    return times_out(active, full_ref, j + 1)


def state_kernel(ids_ref, got_ref, latent_ref, map_own, map_other, gain_feed, gain_self, *refs):
    pieces, refs = refs[:2], refs[2:]
    sent_ref, mixed_ref, lse_ref, one_ref, hidden_ref, active_ref, slope_ref, two_ref = refs[:8]
    low_ref, pack_ref, full_ref, sems = refs[8:]
    copies = fetch_all(ids_ref, pieces, full_ref, sems)
    core = ids_ref[0]
    got = [got_ref[s].astype(f32) for s in range(MP)]
    peaks = [join3(g, C + 1) for g in got]
    totals = [join3(g, C + 4) for g in got]
    peak = peaks[0]
    for s in range(1, MP):
        peak = jnp.maximum(peak, peaks[s])
    shares = [jnp.exp(p - peak) for p in peaks]
    total = shares[0] * totals[0]
    mixed = shares[0] * got[0]
    for s in range(1, MP):
        total = total + shares[s] * totals[s]
        mixed = mixed + shares[s] * got[s]
    ids = lax.broadcasted_iota(jnp.int32, (CP, 1), 0)
    mixed = jnp.where(ids < C, mixed / total, 0.0)
    lse_ref[...] = peak + jnp.log(total)
    mixed_ref[...] = mixed
    low_ref[...] = mixed.astype(bf16)
    mixed = jnp.concatenate([mixed, jnp.zeros((CH - CP, LOCAL), f32)], axis=0)
    one = latent_ref[...].astype(f32)
    for first, ref in ((True, map_own), (False, map_other)):
        part = pick_rows(core, mixed, first)
        one = one + dot(part.T.astype(bf16), side_by_side(ref, HALF))
    one_ref[...] = one
    two = one + feed_forward(
        one, gain_feed[...], copies, full_ref, 0, hidden_ref, active_ref, slope_ref
    )
    two_ref[...] = two
    pack_ref[...] = jnp.concatenate([active_ref[...], pick(core, hidden_ref[...], False)], axis=1)
    unit, _ = normal(two)
    hidden = (unit * gain_self[...]).astype(bf16)
    for s in range(MP):
        sent_ref[s] = hidden


def heads_kernel(all_ref, wq_ref, wk_ref, wv_ref, sent_ref, q_ref, k_ref, v_ref, log_ref):
    weight = jnp.concatenate([wq_ref[...], wk_ref[...], wv_ref[...]], axis=1)
    for s in range(MP):
        rows = dot(all_ref[s], weight).astype(bf16)
        for n, ref in enumerate((q_ref, k_ref, v_ref)):
            ref[s] = rows[:, n * HEAD : (n + 1) * HEAD].reshape(ITEMS, ROWS, HEAD)
    for i in range(ITEMS):
        q, k, v = (ref[:, i].reshape(NLAT, HEAD) for ref in (q_ref, k_ref, v_ref))
        scores = dot_t(k, q) * HEAD**-0.5
        top = jnp.max(scores, axis=0, keepdims=True)
        log = top + jnp.log(jnp.sum(jnp.exp(scores - top), axis=0, keepdims=True))
        log_ref[i : i + 1] = log
        attention = jnp.exp(scores - log).astype(bf16)
        out = dot(v.T, attention).T.astype(bf16)
        sent_ref[:, i] = out.reshape(MP, ROWS, HEAD)


def last_kernel(ids_ref, got_ref, two_ref, gain_ref, cotangent_ref, *refs):
    pieces, refs = refs[:2], refs[2:]
    sent_ref, up_ref, result_ref, heads_ref, hidden_ref, active_ref, before_ref = refs[:7]
    grad_gain_ref, pack_ref, full_ref, sems, slope_ref = refs[7:]
    core = ids_ref[0]
    copies = fetch_all(ids_ref, pieces, full_ref, sems)
    heads = jnp.concatenate([got_ref[s] for s in range(MP)], axis=1)
    heads_ref[...] = heads
    arrive(copies, 0)
    three = two_ref[...] + times_out(heads, full_ref, 0)
    branch = feed_forward(
        three, gain_ref[...], copies, full_ref, 1, hidden_ref, active_ref, slope_ref
    )
    result_ref[...] = (three + branch).astype(bf16)
    upstream = cotangent_ref[...]
    grad_active = times_in(upstream, full_ref, 2)
    grad_before = (grad_active * slope_ref[...]).astype(bf16)
    before_ref[...] = grad_before
    grad_hidden = times_out(grad_before, full_ref, 1)
    unit, scale = normal(three)
    grad, grad_gain = normal_back(unit, scale, gain_ref[...], grad_hidden)
    grad_gain_ref[...] = grad_gain
    up = upstream.astype(f32) + grad
    up_ref[...] = up
    dy = up.astype(bf16)
    grad_heads = times_in(dy, full_ref, 0).astype(bf16)
    for s in range(MP):
        sent_ref[s] = grad_heads[:, s * HEAD : (s + 1) * HEAD]
    rights = [pick(core, v, False) for v in (dy, hidden_ref[...], upstream)]
    lefts = [heads, grad_before, active_ref[...]]
    pack_ref[...] = jnp.concatenate(lefts + rights, axis=1)


def last_grads_kernel(
    ids_ref, heads_ref, up_ref, hidden_ref, active_ref, before_ref, upstream_ref, got_ref, own
):
    core = ids_ref[0]
    lefts = heads_ref, before_ref, active_ref
    rights = up_ref, hidden_ref, upstream_ref
    for j in range(3):
        got_left = got_ref[:, j * D : (j + 1) * D]
        got_right = got_ref[:, 3 * D + j * WIDE : 3 * D + (j + 1) * WIDE]
        right = pick(core, rights[j][...], True).astype(bf16)
        store_grad(stacked(lefts[j][...], got_left), stacked(right, got_right), own, j, 3)


def heads_grads_kernel(ids_ref, all_ref, dq_ref, dk_ref, dv_ref, own, other):
    rows = all_ref[...].reshape(MP * LOCAL, D)
    for n, ref in enumerate((dq_ref, dk_ref, dv_ref)):
        grad = dot(ref[...].reshape(MP * LOCAL, HEAD).T, rows)
        store_blocks(ids_ref, grad, own, other, n)


def heads_back_kernel(
    got_ref,
    q_ref,
    k_ref,
    v_ref,
    log_ref,
    wq_ref,
    wk_ref,
    wv_ref,
    sent_ref,
    dq_ref,
    dk_ref,
    dv_ref,
):
    scale = HEAD**-0.5
    for i in range(ITEMS):
        q, k, v, g = (ref[:, i].reshape(NLAT, HEAD) for ref in (q_ref, k_ref, v_ref, got_ref))
        attention = jnp.exp(dot_t(k, q) * scale - log_ref[i : i + 1])
        grad_attention = dot_t(v, g)
        delta = jnp.sum(attention * grad_attention, axis=0, keepdims=True)
        dv = dot(attention.astype(bf16), g)
        grad_scores = (attention * (grad_attention - delta)).astype(bf16)
        dk = dot(grad_scores, q) * scale
        dq = dot(k.T, grad_scores).T * scale
        for ref, grad in ((dq_ref, dq), (dk_ref, dk), (dv_ref, dv)):
            ref[:, i] = grad.astype(bf16).reshape(MP, ROWS, HEAD)
    weight = jnp.concatenate([wq_ref[...], wk_ref[...], wv_ref[...]], axis=1)
    for s in range(MP):
        rows = jnp.concatenate(
            [ref[s].reshape(LOCAL, HEAD) for ref in (dq_ref, dk_ref, dv_ref)], axis=1
        )
        sent_ref[s] = dot_t(rows, weight).astype(bf16)


def feed_back_kernel(
    ids_ref,
    got_ref,
    two_ref,
    one_ref,
    up_ref,
    slope_ref,
    mixed_ref,
    lse_ref,
    map_own,
    map_other,
    gain_feed,
    gain_self,
    *refs,
):
    pieces, refs = refs[:2], refs[2:]
    sent_ref, down_ref, before_ref, branch_ref, grad_self_ref, grad_feed_ref = refs[:6]
    pack_ref, full_ref, sems = refs[6:]
    copies = fetch_all(ids_ref, pieces, full_ref, sems)
    core = ids_ref[0]
    grad_hidden = got_ref[0].astype(f32)
    for s in range(1, MP):
        grad_hidden = grad_hidden + got_ref[s].astype(f32)
    unit, scale = normal(two_ref[...])
    grad, grad_gain = normal_back(unit, scale, gain_self[...], grad_hidden)
    grad_self_ref[...] = grad_gain
    upstream = up_ref[...] + grad
    dy = upstream.astype(bf16)
    branch_ref[...] = dy
    arrive(copies, 1)
    grad_active = times_in(dy, full_ref, 1)
    grad_before = (grad_active * slope_ref[...]).astype(bf16)
    before_ref[...] = grad_before
    arrive(copies, 0)
    grad_hidden = times_out(grad_before, full_ref, 0)
    unit, scale = normal(one_ref[...])
    grad, grad_gain = normal_back(unit, scale, gain_feed[...], grad_hidden)
    grad_feed_ref[...] = grad_gain
    upstream = upstream + grad
    down_ref[...] = upstream
    dy = upstream.astype(bf16)
    pack_ref[...] = jnp.concatenate(
        [before_ref[...], pick(core, branch_ref[...], False), pick(core, dy, False)], axis=1
    )
    grad_mixed = halves(
        core, dot_t(side_by_side(map_own, HALF), dy), dot_t(side_by_side(map_other, HALF), dy), 0
    )[:CP]
    delta = jnp.sum(grad_mixed * mixed_ref[...], axis=0, keepdims=True)
    sent = with_tail(grad_mixed, split3(lse_ref[...]) + split3(delta)).astype(bf16)
    for s in range(MP):
        sent_ref[s] = sent


def feed_grads_kernel(
    ids_ref,
    hidden_ref,
    active_ref,
    before_ref,
    branch_ref,
    down_ref,
    mixed_ref,
    got_mixed_ref,
    got_state_ref,
    got_ref,
    own,
    mix_ref,
):
    core = ids_ref[0]
    right = stacked(pick(core, hidden_ref[...], True), got_state_ref[:, D:])
    store_grad(stacked(before_ref[...], got_ref[:, :D]), right, own, 0, 2)
    right = stacked(pick(core, branch_ref[...], True), got_ref[:, D : D + WIDE])
    store_grad(stacked(active_ref[...], got_state_ref[:, :D]), right, own, 1, 2)
    right = stacked(pick(core, down_ref[...], True).astype(bf16), got_ref[:, D + WIDE :])
    mixed = jnp.concatenate([mixed_ref[...], got_mixed_ref[...]], axis=1)
    mix_ref[...] = dot(mixed, right)


def cross_back_kernel(rows_ref, flat_ref, items_ref, told_ref, sent_ref, grad_ref):
    ids = lax.broadcasted_iota(jnp.int32, (CP, 1), 0)
    partials = []
    for i, told in enumerate(to_items(told_ref)):
        slots = slice(i * SLOTS, (i + 1) * SLOTS)
        log, delta = join3(told, C + 1), join3(told, C + 4)
        told = jnp.where(ids < C, told, 0.0).astype(bf16)
        asked = items_ref[i]
        attention = jnp.exp(dot(rows_ref[slots], asked) - log)
        grad_attention = dot(rows_ref[slots], told)
        grad_scores = (attention * (grad_attention - delta)).astype(bf16)
        grad_ref[slots] = dot_t(grad_scores, asked) + dot_t(attention.astype(bf16), told)
        partials.append(dot(flat_ref[:, slots], grad_scores))
    store_by_peer(sent_ref, *partials)


def pixel_back_kernel(pixel_ref, grad_ref, gain_ref, out_ref, grad_gain_ref):
    unit, scale = normal(pixel_ref[...].astype(f32))
    grad, grad_gain = normal_back(unit, scale, gain_ref[...], grad_ref[:, :C])
    out_ref[...] = grad
    grad_gain_ref[:, :] = jnp.zeros(grad_gain_ref.shape, f32)
    grad_gain_ref[:, :C] = grad_gain


def latent_back_kernel(
    core_ref,
    got_ref,
    latent_ref,
    gain_ref,
    map_own,
    map_other,
    down_ref,
    feed_gain,
    self_gain,
    last_gain,
    pixel_gain,
    asked_ref,
    gains_ref,
    grad_ref,
    normed_ref,
    own_gains_ref,
):
    core = core_ref[0]
    asked = got_ref[0].astype(f32)
    for s in range(1, MP):
        asked = asked + got_ref[s].astype(f32)
    ids = lax.broadcasted_iota(jnp.int32, (CP, 1), 0)
    asked = jnp.where(ids < C, asked * (D**-0.5), 0.0)
    unit, scale = normal(latent_ref[...].astype(f32))
    normed = (unit * gain_ref[...]).astype(bf16)
    padded = jnp.concatenate([asked, jnp.zeros((CH - CP, LOCAL), f32)], axis=0)
    grad_normed = 0.0
    for first, ref in ((True, map_own), (False, map_other)):
        part = pick_rows(core, padded, first)
        grad_normed = grad_normed + dot(part.T.astype(bf16), side_by_side(ref, 0))
    grad, grad_gain = normal_back(unit, scale, gain_ref[...], grad_normed)
    grad_ref[...] = down_ref[...] + grad
    asked_ref[...] = asked.astype(bf16)
    normed_ref[...] = pick(core, normed, True)
    rows = [grad_gain, feed_gain[...], self_gain[...], last_gain[...], pixel_gain[...]]
    gains = jnp.concatenate(rows + [jnp.zeros((3, D), f32)], axis=0)
    own_gains_ref[...] = pick(core, gains, True)
    other = pick(core, gains, False)
    high = other.astype(bf16).astype(f32)
    gains_ref[...] = jnp.concatenate([high, other - high], axis=0).astype(bf16)


def total_kernel(
    asked_ref,
    got_asked_ref,
    gains_ref,
    normed_ref,
    got_normed_ref,
    own_gains_ref,
    mix_ref,
    tiles_ref,
    sent_ref,
):
    asked = jnp.concatenate([asked_ref[...], got_asked_ref[...]], axis=1)
    score = dot(asked, stacked(normed_ref[...], got_normed_ref[...]))
    got_gains = gains_ref[...].astype(f32)
    gains = own_gains_ref[...] + got_gains[:8] + got_gains[8:]
    high = gains.astype(bf16).astype(f32)
    low = gains - high
    ids = lax.broadcasted_iota(jnp.int32, (CP - 256, 1), 0) + 256
    tail = score[256:]
    for n in range(5):
        tail = jnp.where(ids == C + n, high[n : n + 1], tail)
        tail = jnp.where(ids == C + 5 + n, low[n : n + 1], tail)
    rest = jnp.zeros((MP * PART - 2 * CP, WIDE), f32)
    total = jnp.concatenate([mix_ref[...], score[:256], tail, rest], axis=0)
    for s in range(MP):
        for j in range(2):
            for h in range(2):
                block = (j * 2 + h) * HEAD
                rows = tiles_ref[s * 2 + j, h * ROWS : (h + 1) * ROWS]
                sent_ref[s, :ROWS, block : block + HEAD] = rows
        sent_ref[s, ROWS:] = total[s * PART : (s + 1) * PART].astype(bf16)


def spread_kernel(got_ref, sent_ref):
    total = got_ref[0].astype(f32)
    for s in range(1, MP):
        total = total + got_ref[s].astype(f32)
    total = total.astype(bf16)
    for s in range(MP):
        sent_ref[s] = total


def copies_kernel(got_ref, sent_ref, tiles_ref):
    total = got_ref[0, ROWS:].astype(f32)
    for s in range(1, MP):
        total = total + got_ref[s, ROWS:].astype(f32)
    total = total.astype(bf16)
    for s in range(MP):
        sent_ref[s] = total
    for q in range(QUART):
        rows = (got_ref[q, :ROWS].astype(f32) + got_ref[QUART + q, :ROWS].astype(f32)).astype(bf16)
        for j in range(2):
            for h in range(2):
                block = (j * 2 + h) * HEAD
                tiles_ref[q, j, h * ROWS : (h + 1) * ROWS] = rows[:, block : block + HEAD]


def cross_grads_kernel(
    ids_ref,
    own_ref,
    other_ref,
    key_ref,
    query_ref,
    value_own,
    value_other,
    out_rows_ref,
    grad_query_ref,
    grad_key_ref,
    grad_value_ref,
    grad_out_ref,
    *refs,
):
    gain_refs, pad_ref = refs[:5], refs[5]
    core, mine = ids_ref[0], ids_ref[2]
    pad_ref[...] = jnp.zeros(pad_ref.shape, f32)
    pad_ref[:C] = key_ref[...].astype(f32)
    key = pad_ref[...].astype(bf16)
    out_rows = jnp.concatenate([out_rows_ref[s] for s in range(MP)], axis=1)
    block = pl.ds(pl.multiple_of(lax.rem(mine, QUART) * HEAD, HEAD), HEAD)
    grad_key, grad_value = 0.0, 0.0
    gains = []
    for side, ref in enumerate((own_ref, other_ref)):
        half = core if side == 0 else 1 - core
        span = pl.ds(pl.multiple_of(half * WIDE, WIDE), WIDE)
        mix, score = ref[:CP], ref[CP : 2 * CP]
        grad_query_ref[span, :] = dot(score.T, key)
        grad_key = grad_key + dot(score, query_ref[span, :])
        grad_value = grad_value + dot_t(mix, pick(core, out_rows, side == 0))
        tail = score[256:].astype(f32)
        gains.append(tail[C - 256 : C - 251] + tail[C - 251 : C - 246])
    grad_key_ref[...] = grad_key[:C]
    grad_value_ref[...] = grad_value[:C]
    gains = halves(core, gains[0], gains[1], 1)
    for n, ref in enumerate(gain_refs):
        ref[...] = gains[n : n + 1, : ref.shape[1]]
    half = lax.div(mine, QUART)
    mix = jnp.where(half == core, own_ref[:CP, block], other_ref[:CP, block])
    mix = jnp.concatenate([mix, jnp.zeros((CH - CP, HEAD), bf16)], axis=0)
    grad_out_ref[...] = dot(value_own[...].T, pick_rows(core, mix, True)) + dot(
        value_other[...].T, pick_rows(core, mix, False)
    )


def finish_kernel(turned_outs, relative, ids_ref, own_ref, other_ref, *outs):
    core, depth = ids_ref[0], ids_ref[1]
    for side, ref in enumerate((own_ref, other_ref)):
        half = core if side == 0 else 1 - core
        for step in range(QUART):
            block = half * QUART + (lax.rem(depth + step, QUART) if relative else step)
            span = pl.ds(pl.multiple_of(block * HEAD, HEAD), HEAD)
            for j, out in enumerate(outs):
                piece = ref[step, j].astype(f32)
                if turned_outs[j]:
                    out[span, :] = piece.T
                else:
                    out[:, span] = piece


def body(
    latents,
    pixels,
    masks,
    cotangent,
    norm_latent,
    norm_pixel,
    norm_feed,
    norm_self,
    norm_last,
    cross_query,
    cross_key,
    cross_value,
    cross_out,
    feed_in,
    feed_out,
    self_query,
    self_key,
    self_value,
    self_out,
    last_in,
    last_out,
):
    core = lax.axis_index("dp") % 2
    mine = lax.axis_index("mp")
    depth = (lax.axis_index("dp") // 2) % QUART
    core_id = jnp.stack([core, depth, mine]).astype(jnp.int32)
    gain_latent, gain_pixel, gain_feed, gain_self, gain_last = (
        g[None, :] for g in (norm_latent, norm_pixel, norm_feed, norm_self, norm_last)
    )
    latent_rows = latents.reshape(LOCAL, D)
    pixel_rows = pixels.reshape(ITEMS * SLOTS, C)
    cotangent_rows = cotangent.reshape(LOCAL, D)
    row_f32, row_bf16 = ((LOCAL, D), f32), ((LOCAL, D), bf16)
    gain_row = ((1, D), f32)

    def come(x, step):
        return lax.ppermute(x, "dp", DEPTH[QUART - step])

    map_shape = ((MP, CH, HEAD), bf16)
    (sent,) = run(
        map_start_kernel,
        2,
        [((MP, CH + 6 * HEAD, HEAD), bf16)],
        core_id,
        cross_key,
        cross_query,
        cross_value,
        feed_in,
        feed_out,
        self_out,
        last_in,
        last_out,
        cross_out,
        scratch=[pltpu.VMEM((2, CH, HEAD), f32)],
    )
    pixel_in, pixel_flat = run(
        pixel_kernel,
        2,
        [((ITEMS * SLOTS, CP), bf16), ((CP, ITEMS * SLOTS), bf16)],
        pixel_rows,
        masks,
        gain_pixel,
        scratch=[pltpu.VMEM((ITEMS * SLOTS, 384), f32)],
        hot_outs=(),
    )
    got, (pixel_in, pixel_flat) = after(exchange(sent), pixel_in, pixel_flat)

    def along(x):
        return lax.all_gather(x, "dp", axis_index_groups=ALONG_Z)

    sent, value_half, feed_pack, last_pack, out_rows = run(
        map_sum_kernel,
        1,
        [
            map_shape,
            ((HALF, D), bf16),
            ((MP, 2, HEAD, HEAD), bf16),
            ((MP, 3, HEAD, HEAD), bf16),
            ((MP, HEAD, HEAD), bf16),
        ],
        got,
        cross_out,
        hot=(0,),
    )
    feed_pack = along(feed_pack)
    map_own = exchange(sent)
    map_other = core_swap(map_own)
    peer_shape = ((MP, CP, HEAD), bf16)
    sent, normed_other = run(
        asked_kernel,
        1,
        [peer_shape, ((LOCAL, WIDE), bf16)],
        core_id,
        map_own,
        map_other,
        latent_rows,
        gain_latent,
        hot=(1, 2),
    )
    asked_all, (feed_pack, got_normed) = after(
        exchange(sent), feed_pack, core_swap(normed_other)
    )
    feed_pieces = [feed_pack, core_swap(feed_pack)]
    last_pack, _ = after(last_pack, feed_pack)
    last_pack = along(last_pack)
    sent, asked_items = run(
        cross_kernel,
        3,
        [peer_shape, ((ITEMS, CP, NLAT), bf16)],
        pixel_in,
        pixel_flat,
        asked_all,
        hot=(2,),
    )
    sent, mixed, lse, state_one, feed_hidden, feed_active, feed_slope, state_two, *packs = run(
        state_kernel,
        4,
        [
            ((MP, LOCAL, D), bf16),
            ((CP, LOCAL), f32),
            ((1, LOCAL), f32),
            row_f32,
            row_bf16,
            row_bf16,
            row_f32,
            row_f32,
            ((CP, LOCAL), bf16),
            ((LOCAL, D + WIDE), bf16),
        ],
        core_id,
        exchange(sent),
        latent_rows,
        map_own,
        map_other,
        gain_feed,
        gain_self,
        *feed_pieces,
        scratch=full_shape(2),
        far=(7, 8),
        hot=(1,),
    )
    mixed_low, state_pack = packs
    hidden_all, (last_pack, got_mixed, got_state) = after(
        exchange(sent), last_pack, core_swap(mixed_low), core_swap(state_pack)
    )
    heads_shape = ((MP, ITEMS, ROWS, HEAD), bf16)
    sent, queries, keys, values, logs = run(
        heads_kernel,
        3,
        [heads_shape] * 4 + [((ITEMS, NLAT), f32)],
        hidden_all,
        self_query,
        self_key,
        self_value,
        hot=(0,),
    )
    sent, up, result, heads_out, last_hidden, last_active, last_before, grad_last, last_pack = run(
        last_kernel,
        6,
        [
            ((MP, LOCAL, HEAD), bf16),
            row_f32,
            row_bf16,
            row_bf16,
            row_bf16,
            row_bf16,
            row_bf16,
            gain_row,
            ((LOCAL, 3 * (D + WIDE)), bf16),
        ],
        core_id,
        exchange(sent).reshape(MP, LOCAL, HEAD),
        state_two,
        gain_last,
        cotangent_rows,
        last_pack,
        core_swap(last_pack),
        scratch=full_shape(3) + [pltpu.VMEM((LOCAL, D), f32)],
        far=(5, 6),
        hot=(1,),
    )

    def tiles(count):
        return ((QUART, count, HEAD, HEAD), bf16)

    def along_sum(x):
        count = x.shape[1]
        x = x.reshape(QUART * count * HEAD, HEAD)
        x = lax.psum_scatter(x, "dp", axis_index_groups=ALONG_Z, tiled=True)
        return x.reshape(count, HEAD, HEAD)

    (last_own,) = run(
        last_grads_kernel,
        3,
        [tiles(3 * MP)],
        core_id,
        heads_out,
        up,
        last_hidden,
        last_active,
        last_before,
        cotangent_rows,
        core_swap(last_pack),
        hot_outs=(),
    )
    grad_heads, (last_own,) = after(exchange(sent), last_own)
    grad_heads = grad_heads.reshape(MP, ITEMS, ROWS, HEAD)
    last_sum = along_sum(last_own)
    sent, dq, dk, dv = run(
        heads_back_kernel,
        4,
        [((MP, LOCAL, D), bf16)] + [heads_shape] * 3,
        grad_heads,
        queries,
        keys,
        values,
        logs,
        self_query,
        self_key,
        self_value,
        hot=(0,),
    )
    self_own, self_other = run(
        heads_grads_kernel, 2, [tiles(3)] * 2, core_id, hidden_all, dq, dk, dv, hot_outs=()
    )
    got, (self_own, self_other) = after(exchange(sent), self_own, core_swap(self_other))
    sent, down, feed_before, feed_branch, grad_self, grad_feed, feed_back = run(
        feed_back_kernel,
        4,
        [peer_shape, row_f32, row_bf16, row_bf16, gain_row, gain_row, ((LOCAL, 2 * D), bf16)],
        core_id,
        got,
        state_two,
        state_one,
        up,
        feed_slope,
        mixed,
        lse,
        map_own,
        map_other,
        gain_feed,
        gain_self,
        *feed_pieces,
        scratch=full_shape(2),
        far=(12, 13),
        hot=(1,),
    )
    feed_own, mix_own = run(
        feed_grads_kernel,
        2,
        [tiles(2 * MP), ((CP, WIDE), f32)],
        core_id,
        feed_hidden,
        feed_active,
        feed_before,
        feed_branch,
        down,
        mixed_low,
        got_mixed,
        got_state,
        core_swap(feed_back),
        hot_outs=(),
    )
    told_all, (feed_own, last_sum) = after(exchange(sent), feed_own, last_sum)
    self_join = (self_own.astype(f32) + self_other.astype(f32)).astype(bf16)
    feed_sum = along_sum(jnp.concatenate([feed_own, self_join], axis=1))
    sent, grad_pixel_in = run(
        cross_back_kernel,
        4,
        [peer_shape, ((ITEMS * SLOTS, CP), f32)],
        pixel_in,
        pixel_flat,
        asked_items,
        told_all,
        hot=(3,),
    )
    grad_pixels, grad_pixel = run(
        pixel_back_kernel,
        2,
        [((ITEMS * SLOTS, C), f32), gain_row],
        pixel_rows,
        grad_pixel_in,
        gain_pixel,
        hot_outs=(),
    )
    grad_pixels = grad_pixels.reshape(ITEMS, SLOTS, C).transpose(2, 0, 1)
    got, (grad_pixels,) = after(exchange(sent), grad_pixels)
    asked_low, other_gains, grad_latents, normed_own, own_gains = run(
        latent_back_kernel,
        2,
        [
            ((CP, LOCAL), bf16),
            ((16, WIDE), bf16),
            row_f32,
            ((LOCAL, WIDE), bf16),
            ((8, WIDE), f32),
        ],
        core_id,
        got,
        latent_rows,
        gain_latent,
        map_own,
        map_other,
        down,
        grad_feed,
        grad_self,
        grad_last,
        grad_pixel,
        hot=(1,),
        hot_outs=(0, 1),
    )
    (sent,) = run(
        total_kernel,
        1,
        [((MP, ROWS + PART, WIDE), bf16)],
        asked_low,
        core_swap(asked_low),
        core_swap(other_gains),
        normed_own,
        got_normed,
        own_gains,
        mix_own,
        feed_sum[: 2 * MP],
        hot=(0, 1, 2),
    )
    last_sum, _ = after(last_sum, feed_sum)
    last_sum = last_sum.reshape(MP * 3 * HEAD, HEAD)
    last_piece = lax.psum_scatter(last_sum, "mp", tiled=True).reshape(3, HEAD, HEAD)
    self_rest = feed_sum[2 * MP :]
    self_rest = added(jnp.stack([self_rest, lax.ppermute(self_rest, "dp", FAR)]))
    got, (self_rest,) = after(exchange(sent), self_rest)
    (sent,) = run(spread_kernel, 1, [((MP, ROWS + PART, WIDE), bf16)], got, hot=(0,))
    got, (last_piece,) = after(grouped(sent, "dp", COPIES), last_piece)
    sent, feed_own = run(
        copies_kernel,
        1,
        [((MP, PART, WIDE), bf16), ((QUART, 2, HEAD, HEAD), bf16)],
        got,
        hot=(0,),
    )
    feed_pair = feed_own, core_swap(feed_own)
    own = exchange(sent).reshape(MP * PART, WIDE)
    x = added(jnp.stack([last_piece, lax.ppermute(last_piece, "dp", FAR)]))
    x = jnp.concatenate([x, self_rest], axis=0)
    x = jnp.stack([x] + [come(x, step) for step in (1, 2, 3)])
    self_pair = x, core_swap(x)
    row_out, key_out = ((D, HEAD), f32), ((C, HEAD), f32)
    grad_cross_query, grad_cross_key, grad_cross_value, grad_cross_out, *gains = run(
        cross_grads_kernel,
        3,
        [row_out, key_out, key_out, row_out] + [gain_row] * 4 + [((1, C), f32)],
        core_id,
        own,
        core_swap(own),
        cross_key,
        cross_query,
        value_half,
        core_swap(value_half),
        out_rows,
        scratch=[pltpu.VMEM((CP, HEAD), f32)],
        hot=(1, 2),
        hot_outs=(),
    )

    def finish(pair, flips, relative):
        outs = [((D, HEAD) if flip else (HEAD, D), f32) for flip in flips]
        kernel = functools.partial(finish_kernel, flips, relative)
        return run(kernel, 2, outs, core_id, *pair, hot_outs=())

    flips = (False, True, False, True, True, True)
    grad_self_out, grad_last_in, grad_last_out, grad_sq, grad_sk, grad_sv = finish(
        self_pair, flips, True
    )
    grad_feed_in, grad_feed_out = finish(feed_pair, (True, False), False)
    shape = (ITEMS, ROWS, D)
    return (
        result.reshape(shape),
        grad_latents.reshape(shape),
        grad_pixels.transpose(1, 2, 0),
        gains[0][0],
        gains[4][0],
        gains[1][0],
        gains[2][0],
        gains[3][0],
        grad_cross_query,
        grad_cross_key,
        grad_cross_value,
        grad_cross_out,
        grad_feed_in,
        grad_feed_out,
        grad_sq,
        grad_sk,
        grad_sv,
        grad_self_out,
        grad_last_in,
        grad_last_out,
    )


def solution(mesh):
    rows = P("dp", "mp", None)
    columns = P(None, "mp")
    depth = P("mp", None)
    return jax.shard_map(
        body,
        mesh=mesh,
        in_specs=(rows, rows, P("dp", "mp"), rows)
        + (P(),) * 5
        + (columns,) * 5
        + (depth,)
        + (columns,) * 3
        + (depth, columns, depth),
        out_specs=(rows,) * 3
        + (P(),) * 5
        + (columns,) * 5
        + (depth,)
        + (columns,) * 3
        + (depth, columns, depth),
        check_vma=False,
    )
```

```python
import functools

import jax
import jax.numpy as jnp
from jax import lax
from jax.experimental import pallas as pl
from jax.experimental.pallas import tpu as pltpu
from jax.sharding import PartitionSpec as P

D = 1024
C = 261
CP = 272
CH = 288
HALF = 144
HEADS = 8
HEAD = 128
MP = 8
ITEMS = 2
ROWS = 64
LOCAL = ITEMS * ROWS
SLOTS = 512
NLAT = 512
WIDE = 512
MEMBERS = 64
PART = 80
QUART = 4
SHARE = QUART * PART
LIMIT = 24 << 20
EPS = 1e-05
MASKED = -1e30
GELU_A = 0.044715
GELU_K = 0.7978845608028654

bf16 = jnp.bfloat16
f32 = jnp.float32

SWAP = [(i, i ^ 1) for i in range(16)]
CHIPS = [
    [(d * 2 + core) * MP + m for d in range(8) for m in range(MP)] for core in range(2)
]
DEPTH = [
    [((y * 4 + z) * 2 + c, (y * 4 + (z + k) % 4) * 2 + c) for y in range(2) for z in range(4) for c in range(2)]
    for k in range(4)
]
FAR = [(i, i ^ 8) for i in range(16)]
NEAR = [(i, i ^ 4) for i in range(MP)]
OPPOSITE = [(i, i ^ 68) for i in range(128)]
ACROSS = [[(y * 4 + x, y * 4 + (x + k) % 4) for y in range(2) for x in range(4)] for k in range(4)]
COPIES = [[d * 2 + core for d in range(8)] for core in range(2)]
ALONG_Z = [[(y * 4 + z) * 2 + core for z in range(4)] for y in range(2) for core in range(2)]


def dot(a, b):
    return lax.dot_general(a, b, (((1,), (0,)), ((), ())), preferred_element_type=f32)


def dot_t(a, b):
    return lax.dot_general(a, b, (((1,), (1,)), ((), ())), preferred_element_type=f32)


def t_dot(a, b):
    return dot(a.T, b)


def cost(micros):
    return pl.CostEstimate(
        flops=int(micros * 1e7), bytes_accessed=int(micros * 2e4), transcendentals=0
    )


class Arriving:
    def __init__(self, ref, copy):
        self.ref, self.copy, self.shape = ref, copy, ref.shape

    def settle(self):
        if self.copy is not None:
            self.copy.wait()
        self.copy = None

    def __getitem__(self, index):
        self.settle()
        return self.ref[index]


class Leaving:
    def __init__(self, ref, copy):
        self.ref, self.copy, self.shape, self.left = ref, copy, ref.shape, False

    def leave(self):
        if not self.left:
            self.copy.start()
        self.left = True

    def __getitem__(self, index):
        return self.ref[index]

    def __setitem__(self, index, value):
        self.ref[index] = value
        if index is Ellipsis:
            self.leave()


def run(kernel, micros, outs, *args, scratch=(), far=(), pinned=(), loose=(), hot=(), hot_outs=(0,)):
    specs, homes = [], []
    for n, a in enumerate(args):
        if jnp.ndim(a) == 1 and a.dtype == jnp.int32:
            space = pltpu.SMEM
        elif n in hot:
            space = pltpu.VMEM
        elif n in far:
            space = pl.ANY
        elif n in pinned:
            space = pltpu.HBM
        else:
            space = pl.ANY if n in loose else pltpu.HBM
            homes.append(n)
        specs.append(pl.BlockSpec(memory_space=space))
    out_homes = [n for n in range(len(outs)) if n not in hot_outs]
    buffers = [pltpu.VMEM(args[n].shape, args[n].dtype) for n in homes]
    buffers += [pltpu.VMEM(*outs[n]) for n in out_homes]

    def wrapped(*refs):
        refs = list(refs)
        sems, refs = refs[-1], refs[:-1]
        given, refs = refs[: len(args)], refs[len(args) :]
        made, refs = refs[: len(outs)], refs[len(outs) :]
        own, refs = refs[: len(scratch)], refs[len(scratch) :]
        for k, n in enumerate(homes):
            copy = pltpu.make_async_copy(given[n], refs[k], sems.at[k])
            copy.start()
            given[n] = Arriving(refs[k], copy)
        for k, n in enumerate(out_homes, len(homes)):
            made[n] = Leaving(refs[k], pltpu.make_async_copy(refs[k], made[n], sems.at[k]))
        kernel(*given, *made, *own)
        for n in homes:
            given[n].settle()
        for n in out_homes:
            made[n].leave()
        for n in out_homes:
            made[n].copy.wait()

    return pl.pallas_call(
        wrapped,
        out_shape=[
            jax.ShapeDtypeStruct(*out) if n in hot_outs else pltpu.HBM(*out)
            for n, out in enumerate(outs)
        ],
        in_specs=specs,
        out_specs=[
            pl.BlockSpec(memory_space=pltpu.VMEM if n in hot_outs else pltpu.HBM)
            for n in range(len(outs))
        ],
        scratch_shapes=[
            *scratch,
            *buffers,
            pltpu.SemaphoreType.DMA((max(1, len(buffers)),)),
        ],
        compiler_params=pltpu.CompilerParams(vmem_limit_bytes=LIMIT),
        cost_estimate=cost(micros),
    )(
        *(
            pltpu.with_memory_space_constraint(a, pltpu.HBM)
            if n in pinned or (n in homes and n not in loose)
            else a
            for n, a in enumerate(args)
        )
    )


def after(x, *waits):
    x, *waits = lax.optimization_barrier((x, *waits))
    return x, waits


def core_swap(x):
    return lax.ppermute(x, "dp", SWAP)


def exchange(x):
    return lax.all_to_all(x, "mp", 0, 0, tiled=True)


def to_all(x):
    return exchange(jnp.broadcast_to(x[None], (MP,) + x.shape))


def grouped(x, axes, groups):
    return lax.all_to_all(x, axes, 0, 0, tiled=True, axis_index_groups=groups)


def grouped_all(x, axes, groups):
    return grouped(jnp.broadcast_to(x[None], (len(groups[0]),) + x.shape), axes, groups)


def added(x):
    return jnp.sum(x.astype(f32), axis=0).astype(bf16)


def normal(v):
    center = v - jnp.mean(v, axis=-1, keepdims=True)
    spread = jnp.mean(center * center, axis=-1, keepdims=True)
    scale = lax.rsqrt(spread + EPS)
    return center * scale, scale


def normal_back(unit, scale, gain, upstream):
    grad_gain = jnp.sum(upstream * unit, axis=0, keepdims=True)
    grad_unit = upstream * gain
    inner = jnp.mean(grad_unit * unit, axis=-1, keepdims=True)
    grad = scale * (grad_unit - jnp.mean(grad_unit, axis=-1, keepdims=True) - unit * inner)
    return grad, grad_gain


def gelu_parts(v):
    square = v * v
    t = jnp.tanh(GELU_K * v * (1.0 + GELU_A * square))
    value = 0.5 * v * (1.0 + t)
    slope = 0.5 * (1.0 + t) + 0.5 * v * (1.0 - t * t) * GELU_K * (1.0 + 3.0 * GELU_A * square)
    return value, slope


def split3(v):
    high = v.astype(bf16).astype(f32)
    middle = (v - high).astype(bf16).astype(f32)
    return [high, middle, v - high - middle]


def join3(rows, start):
    return rows[start : start + 1] + rows[start + 1 : start + 2] + rows[start + 2 : start + 3]


def halves(core, own, other, axis):
    first = jnp.where(core == 0, own, other)
    second = jnp.where(core == 0, other, own)
    return jnp.concatenate([first, second], axis=axis)


def pick(core, v, own):
    take_low = core == 0 if own else core != 0
    return jnp.where(take_low, v[:, :WIDE], v[:, WIDE:])


def pick_rows(core, v, own):
    take_low = core == 0 if own else core != 0
    return jnp.where(take_low, v[:HALF], v[HALF:])


def full_shape(count):
    return [
        pltpu.VMEM((count, MP, HEAD, D), bf16),
        pltpu.SemaphoreType.DMA((count, 2, QUART)),
    ]


def fetch_steps(ids_ref, pieces, full_ref, sems):
    core, depth = ids_ref[0], ids_ref[1]
    copies = []
    for j in range(full_ref.shape[0]):
        for n, ref in enumerate(pieces):
            side, step = n // QUART, n % QUART
            half = core if side == 0 else 1 - core
            block = half * QUART + lax.rem(depth + step, QUART)
            columns = pl.ds(pl.multiple_of(block * HEAD, HEAD), HEAD)
            copies.append(
                pltpu.make_async_copy(
                    ref.at[:, j], full_ref.at[j, :, :, columns], sems.at[j, side, step]
                )
            )
            copies[-1].start()
    return copies


def fetch_all(ids_ref, pieces, full_ref, sems, base):
    core = ids_ref[0]
    copies = []
    for j in range(full_ref.shape[0]):
        for side, ref in enumerate(pieces):
            half = core if side == 0 else 1 - core
            for q in range(QUART):
                columns = pl.ds(pl.multiple_of((half * QUART + q) * HEAD, HEAD), HEAD)
                copies.append(
                    pltpu.make_async_copy(
                        ref.at[q, :, base + j], full_ref.at[j, :, :, columns], sems.at[j, side, q]
                    )
                )
                copies[-1].start()
    return copies


def arrive(copies, j):
    for copy in copies[j * 2 * QUART : (j + 1) * 2 * QUART]:
        copy.wait()


def matrix(full_ref, j):
    return full_ref[j].reshape(D, D)


def times_in(x, full_ref, j):
    return dot_t(x, matrix(full_ref, j))


def times_out(x, full_ref, j):
    return dot(x, matrix(full_ref, j))


def store_blocks(ids_ref, grad, own_ref, other_ref, place):
    core, depth = ids_ref[0], ids_ref[1]
    for first, ref in ((True, own_ref), (False, other_ref)):
        half = pick(core, grad, first).astype(bf16)
        for q in range(QUART):
            step = lax.rem(q + QUART - depth, QUART)
            ref[step, place] = half[:, q * HEAD : (q + 1) * HEAD]


def stacked(own, got):
    return jnp.concatenate([own, got], axis=0)


def store_grad(left, right, own_ref, j, count):
    flipped = left.T
    for s in range(MP):
        grad = dot(flipped[s * HEAD : (s + 1) * HEAD], right).astype(bf16)
        for q in range(QUART):
            own_ref[q, s * count + j] = grad[:, q * HEAD : (q + 1) * HEAD]


def store_parts(ids_ref, left, right, right_ref, parts, j, count):
    right_ref[j] = right
    blocks = []
    for step in range(QUART):
        columns = pl.multiple_of(lax.rem(ids_ref[1] + step, QUART) * HEAD, HEAD)
        blocks.append(right_ref[j, :, pl.ds(columns, HEAD)])
    right = jnp.concatenate(blocks, axis=1)
    flipped = left.T
    for s in range(MP):
        grad = dot(flipped[s * HEAD : (s + 1) * HEAD], right).astype(bf16)
        for step, part in enumerate(parts):
            part[s * count + j] = grad[:, step * HEAD : (step + 1) * HEAD]


def as_row(column):
    return jnp.broadcast_to(column, (column.shape[0], HEAD)).T[:1]


def side_by_side(ref, start):
    return jnp.concatenate([ref[s, start : start + HALF] for s in range(MP)], axis=1)


def lane_halves():
    return lax.broadcasted_iota(jnp.int32, (1, HEAD), 1) < ROWS


def turned(x):
    return pltpu.roll(x, ROWS, 1)


def to_items(ref):
    low = lane_halves()
    items = [[], []]
    for p in range(0, MP, 2):
        a, b = ref[p].astype(f32), ref[p + 1].astype(f32)
        items[0].append(jnp.where(low, a, turned(b)))
        items[1].append(jnp.where(low, turned(a), b))
    return [jnp.concatenate(v, axis=1) for v in items]


def store_by_peer(ref, first, second):
    low = lane_halves()
    for p in range(0, MP, 2):
        x, y = (v[:, p * ROWS : (p + 2) * ROWS] for v in (first, second))
        ref[p] = jnp.where(low, x, turned(y)).astype(bf16)
        ref[p + 1] = jnp.where(low, turned(x), y).astype(bf16)


def with_tail(x, rows):
    ids = lax.broadcasted_iota(jnp.int32, (CP - 256, 1), 0) + 256
    tail = jnp.where(ids < C, x[256:CP], 0.0)
    for offset, row in enumerate(rows):
        tail = jnp.where(ids == C + 1 + offset, row, tail)
    return jnp.concatenate([x[:256], tail], axis=0)


def map_start_kernel(
    ids_ref,
    key_ref,
    query_ref,
    value_ref,
    feed_in_ref,
    feed_out_ref,
    out_ref,
    sent_ref,
    pad_ref,
):
    core = ids_ref[0]
    span = pl.ds(pl.multiple_of((core * QUART + ids_ref[1]) * HEAD, HEAD), HEAD)
    tiles = [feed_in_ref[span, :].T, feed_out_ref[:, span]]
    pad_ref[...] = jnp.zeros(pad_ref.shape, f32)
    pad_ref[0, :C] = key_ref[...].astype(f32)
    pad_ref[1, :C] = value_ref[...].astype(f32)
    key = jnp.where(core == 0, pad_ref[0, :HALF], pad_ref[0, HALF:]).astype(bf16)
    value = jnp.where(core == 0, pad_ref[1, :HALF], pad_ref[1, HALF:]).astype(bf16)
    for s in range(MP):
        block = query_ref[s * HEAD : (s + 1) * HEAD]
        sent_ref[s, :HALF] = dot_t(key, block).astype(bf16)
        sent_ref[s, HALF:CH] = value
        for j, tile in enumerate(tiles):
            sent_ref[s, CH + j * HEAD : CH + (j + 1) * HEAD] = tile
        rows = pl.ds(pl.multiple_of(s * HEAD + core * ROWS, ROWS), ROWS)
        sent_ref[s, CH + 2 * HEAD :] = out_ref[rows, :]


def tiles_kernel(
    ids_ref, self_out_ref, last_in_ref, last_out_ref, wq_ref, wk_ref, wv_ref, tiles_ref
):
    core = ids_ref[0]
    span = pl.ds(pl.multiple_of((core * QUART + ids_ref[1]) * HEAD, HEAD), HEAD)
    tiles_ref[0] = self_out_ref[:, span]
    tiles_ref[1] = last_in_ref[span, :].T
    tiles_ref[2] = last_out_ref[:, span]
    for n, ref in enumerate((wq_ref, wk_ref, wv_ref)):
        tiles_ref[3 + n] = ref[span, :].T


def map_sum_kernel(got_ref, out_ref, sent_ref, value_ref, feed_ref, rows_ref):
    for s in range(MP):
        for j in range(2):
            feed_ref[s, j] = got_ref[s, CH + j * HEAD : CH + (j + 1) * HEAD]
        rows_ref[s] = got_ref[s, CH + 2 * HEAD :]
    feed_ref.leave()
    score = got_ref[0, :HALF].astype(f32)
    for s in range(1, MP):
        score = score + got_ref[s, :HALF].astype(f32)
    value = side_by_side(got_ref, HALF)
    value_ref[...] = value
    score = score.astype(bf16)
    mix = dot(value, out_ref[...]).astype(bf16)
    for s in range(MP):
        sent_ref[s, :HALF] = score
        sent_ref[s, HALF:] = mix


def asked_kernel(core_ref, own_ref, other_ref, latent_ref, gain_ref, sent_ref, normed_ref):
    core = core_ref[0]
    unit, _ = normal(latent_ref[...].astype(f32))
    normed = (unit * gain_ref[...]).astype(bf16)
    normed_ref[...] = normed
    asked = halves(
        core, dot_t(side_by_side(own_ref, 0), normed), dot_t(side_by_side(other_ref, 0), normed), 0
    )
    ids = lax.broadcasted_iota(jnp.int32, (CP, 1), 0)
    asked = jnp.where(ids < C, asked[:CP] * (D**-0.5), jnp.where(ids == C, 1.0, 0.0))
    asked = asked.astype(bf16)
    for s in range(MP):
        sent_ref[s] = asked


def pixel_kernel(pixel_ref, mask_ref, gain_ref, rows_ref, flat_ref, pad_ref):
    unit, _ = normal(pixel_ref[...].astype(f32))
    pad_ref[...] = jnp.zeros(pad_ref.shape, f32)
    pad_ref[:, :C] = unit * gain_ref[...]
    flat = pad_ref[...].T[:CP]
    bias = jnp.where(mask_ref[...] > 0, 0.0, MASKED)
    bias = jnp.concatenate([bias[i : i + 1] for i in range(ITEMS)], axis=1)
    ids = lax.broadcasted_iota(jnp.int32, (CP, 1), 0)
    flat = jnp.where(ids == C, bias, flat)
    flat_ref[...] = flat.astype(bf16)
    lanes = lax.broadcasted_iota(jnp.int32, (1, CP), 1)
    rows_ref[...] = flat.T.astype(bf16)


def cross_kernel(rows_ref, flat_ref, asked_ref, sent_ref, items_ref):
    sums = []
    for i, asked in enumerate(to_items(asked_ref)):
        asked = asked.astype(bf16)
        items_ref[i] = asked
        slots = slice(i * SLOTS, (i + 1) * SLOTS)
        scores = dot(rows_ref[slots], asked)
        peak = jnp.max(scores, axis=0, keepdims=True)
        weight = jnp.exp(scores - peak)
        total = jnp.sum(weight, axis=0, keepdims=True)
        mixed = dot(flat_ref[:, slots], weight.astype(bf16))
        sums.append(with_tail(mixed, split3(peak) + split3(total)))
    store_by_peer(sent_ref, *sums)


def feed_forward(stream, gain, copies, full_ref, j, hidden_ref, active_ref, slope_ref):
    unit, _ = normal(stream)
    hidden = (unit * gain).astype(bf16)
    hidden_ref[...] = hidden
    arrive(copies, j)
    active, slope = gelu_parts(times_in(hidden, full_ref, j))
    active = active.astype(bf16)
    active_ref[...] = active
    slope_ref[...] = slope
    arrive(copies, j + 1)
    return times_out(active, full_ref, j + 1)


def state_kernel(ids_ref, got_ref, latent_ref, map_own, map_other, gain_feed, gain_self, *refs):
    pieces, refs = refs[: 2 * QUART], refs[2 * QUART :]
    sent_ref, mixed_ref, lse_ref, one_ref, hidden_ref, active_ref, slope_ref, two_ref = refs[:8]
    low_ref, pack_ref, full_ref, sems = refs[8:]
    copies = fetch_steps(ids_ref, pieces, full_ref, sems)
    core = ids_ref[0]
    got = [got_ref[s].astype(f32) for s in range(MP)]
    peaks = [join3(g, C + 1) for g in got]
    totals = [join3(g, C + 4) for g in got]
    peak = peaks[0]
    for s in range(1, MP):
        peak = jnp.maximum(peak, peaks[s])
    shares = [jnp.exp(p - peak) for p in peaks]
    total = shares[0] * totals[0]
    mixed = shares[0] * got[0]
    for s in range(1, MP):
        total = total + shares[s] * totals[s]
        mixed = mixed + shares[s] * got[s]
    ids = lax.broadcasted_iota(jnp.int32, (CP, 1), 0)
    mixed = jnp.where(ids < C, mixed / total, 0.0)
    lse_ref[...] = peak + jnp.log(total)
    mixed_ref[...] = mixed
    low_ref[...] = mixed.astype(bf16)
    mixed = jnp.concatenate([mixed, jnp.zeros((CH - CP, LOCAL), f32)], axis=0)
    one = latent_ref[...].astype(f32)
    for first, ref in ((True, map_own), (False, map_other)):
        part = pick_rows(core, mixed, first)
        one = one + dot(part.T.astype(bf16), side_by_side(ref, HALF))
    one_ref[...] = one
    two = one + feed_forward(
        one, gain_feed[...], copies, full_ref, 0, hidden_ref, active_ref, slope_ref
    )
    two_ref[...] = two
    pack_ref[...] = jnp.concatenate([active_ref[...], pick(core, hidden_ref[...], False)], axis=1)
    unit, _ = normal(two)
    hidden = (unit * gain_self[...]).astype(bf16)
    for s in range(MP):
        sent_ref[s] = hidden


def heads_kernel(all_ref, wq_ref, wk_ref, wv_ref, sent_ref, q_ref, k_ref, v_ref, log_ref):
    weight = jnp.concatenate([wq_ref[...], wk_ref[...], wv_ref[...]], axis=1)
    for s in range(MP):
        rows = dot(all_ref[s], weight).astype(bf16)
        for n, ref in enumerate((q_ref, k_ref, v_ref)):
            ref[s] = rows[:, n * HEAD : (n + 1) * HEAD].reshape(ITEMS, ROWS, HEAD)
    for i in range(ITEMS):
        q, k, v = (ref[:, i].reshape(NLAT, HEAD) for ref in (q_ref, k_ref, v_ref))
        scores = dot_t(k, q) * HEAD**-0.5
        top = jnp.max(scores, axis=0, keepdims=True)
        log = top + jnp.log(jnp.sum(jnp.exp(scores - top), axis=0, keepdims=True))
        log_ref[i : i + 1] = log
        attention = jnp.exp(scores - log).astype(bf16)
        out = dot(v.T, attention).T.astype(bf16)
        sent_ref[:, i] = out.reshape(MP, ROWS, HEAD)


def last_kernel(ids_ref, got_ref, two_ref, gain_ref, cotangent_ref, *refs):
    pieces, refs = refs[:2], refs[2:]
    sent_ref, up_ref, result_ref, heads_ref, hidden_ref, active_ref, before_ref = refs[:7]
    grad_gain_ref, pack_ref, full_ref, sems, slope_ref = refs[7:]
    core = ids_ref[0]
    copies = fetch_all(ids_ref, pieces, full_ref, sems, 0)
    heads = jnp.concatenate([got_ref[s] for s in range(MP)], axis=1)
    heads_ref[...] = heads
    arrive(copies, 0)
    three = two_ref[...] + times_out(heads, full_ref, 0)
    branch = feed_forward(
        three, gain_ref[...], copies, full_ref, 1, hidden_ref, active_ref, slope_ref
    )
    result_ref[...] = (three + branch).astype(bf16)
    upstream = cotangent_ref[...]
    grad_active = times_in(upstream, full_ref, 2)
    grad_before = (grad_active * slope_ref[...]).astype(bf16)
    before_ref[...] = grad_before
    grad_hidden = times_out(grad_before, full_ref, 1)
    unit, scale = normal(three)
    grad, grad_gain = normal_back(unit, scale, gain_ref[...], grad_hidden)
    grad_gain_ref[...] = grad_gain
    up = upstream.astype(f32) + grad
    up_ref[...] = up
    dy = up.astype(bf16)
    grad_heads = times_in(dy, full_ref, 0).astype(bf16)
    for s in range(MP):
        sent_ref[s] = grad_heads[:, s * HEAD : (s + 1) * HEAD]
    rights = [pick(core, v, False) for v in (dy, hidden_ref[...], upstream)]
    lefts = [heads, grad_before, active_ref[...]]
    pack_ref[...] = jnp.concatenate(lefts + rights, axis=1)


def last_grads_kernel(
    ids_ref, heads_ref, up_ref, hidden_ref, active_ref, before_ref, upstream_ref, got_ref, own
):
    core = ids_ref[0]
    lefts = heads_ref, before_ref, active_ref
    rights = up_ref, hidden_ref, upstream_ref
    for j in range(3):
        got_left = got_ref[:, j * D : (j + 1) * D]
        got_right = got_ref[:, 3 * D + j * WIDE : 3 * D + (j + 1) * WIDE]
        right = pick(core, rights[j][...], True).astype(bf16)
        store_grad(stacked(lefts[j][...], got_left), stacked(right, got_right), own, j, 3)


def heads_grads_kernel(ids_ref, all_ref, dq_ref, dk_ref, dv_ref, own, other):
    rows = all_ref[...].reshape(MP * LOCAL, D)
    for n, ref in enumerate((dq_ref, dk_ref, dv_ref)):
        grad = dot(ref[...].reshape(MP * LOCAL, HEAD).T, rows)
        store_blocks(ids_ref, grad, own, other, n)


def heads_back_kernel(
    got_ref,
    q_ref,
    k_ref,
    v_ref,
    log_ref,
    sent_ref,
    dq_ref,
    dk_ref,
    dv_ref,
):
    scale = HEAD**-0.5
    for i in range(ITEMS):
        q, k, v, g = (ref[:, i].reshape(NLAT, HEAD) for ref in (q_ref, k_ref, v_ref, got_ref))
        attention = jnp.exp(dot_t(k, q) * scale - log_ref[i : i + 1])
        grad_attention = dot_t(v, g)
        delta = jnp.sum(attention * grad_attention, axis=0, keepdims=True)
        dv = dot(attention.astype(bf16), g)
        grad_scores = (attention * (grad_attention - delta)).astype(bf16)
        dk = dot(grad_scores, q) * scale
        dq = dot(k.T, grad_scores).T * scale
        for ref, grad in ((dq_ref, dq), (dk_ref, dk), (dv_ref, dv)):
            ref[:, i] = grad.astype(bf16).reshape(MP, ROWS, HEAD)
    for s in range(MP):
        for n, ref in enumerate((dq_ref, dk_ref, dv_ref)):
            sent_ref[s, :, n * HEAD : (n + 1) * HEAD] = ref[s].reshape(LOCAL, HEAD)


def feed_back_kernel(
    ids_ref,
    got_ref,
    two_ref,
    one_ref,
    up_ref,
    slope_ref,
    mixed_ref,
    lse_ref,
    map_own,
    map_other,
    gain_feed,
    gain_self,
    *refs,
):
    pieces, self_pieces, refs = refs[: 2 * QUART], refs[2 * QUART : 2 * QUART + 2], refs[10:]
    sent_ref, down_ref, before_ref, branch_ref, grad_self_ref, grad_feed_ref = refs[:6]
    pack_ref, grad_pixel_ref, self_ref, self_sems, full_ref, sems = refs[6:]
    self_copies = fetch_all(ids_ref, self_pieces, self_ref, self_sems, 3)
    copies = fetch_steps(ids_ref, pieces, full_ref, sems)
    core = ids_ref[0]
    grad_hidden = 0.0
    for n in range(3):
        block = slice(n * HEAD, (n + 1) * HEAD)
        grad = jnp.concatenate([got_ref[s, :, block] for s in range(MP)], axis=1)
        arrive(self_copies, n)
        grad_hidden = grad_hidden + times_out(grad, self_ref, n)
    unit, scale = normal(two_ref[...])
    grad, grad_gain = normal_back(unit, scale, gain_self[...], grad_hidden)
    grad_self_ref[...] = grad_gain
    upstream = up_ref[...] + grad
    dy = upstream.astype(bf16)
    branch_ref[...] = dy
    arrive(copies, 1)
    grad_active = times_in(dy, full_ref, 1)
    grad_before = (grad_active * slope_ref[...]).astype(bf16)
    before_ref[...] = grad_before
    arrive(copies, 0)
    grad_hidden = times_out(grad_before, full_ref, 0)
    unit, scale = normal(one_ref[...])
    grad, grad_gain = normal_back(unit, scale, gain_feed[...], grad_hidden)
    grad_feed_ref[...] = grad_gain
    upstream = upstream + grad
    down_ref[...] = upstream
    dy = upstream.astype(bf16)
    pack_ref[...] = jnp.concatenate(
        [before_ref[...], pick(core, branch_ref[...], False), pick(core, dy, False)], axis=1
    )
    grad_mixed = halves(
        core, dot_t(side_by_side(map_own, HALF), dy), dot_t(side_by_side(map_other, HALF), dy), 0
    )[:CP]
    shared = grad_mixed * mixed_ref[...]
    delta = jnp.sum(shared, axis=0, keepdims=True)
    grad_pixel_ref[...] = as_row(jnp.sum(shared, axis=1, keepdims=True))
    sent = with_tail(grad_mixed, split3(lse_ref[...]) + split3(delta)).astype(bf16)
    for s in range(MP):
        sent_ref[s] = sent


def feed_grads_kernel(
    ids_ref,
    hidden_ref,
    active_ref,
    before_ref,
    branch_ref,
    down_ref,
    mixed_ref,
    got_mixed_ref,
    got_state_ref,
    got_ref,
    *refs,
):
    parts, mix_ref, right_ref = refs[:QUART], refs[QUART], refs[QUART + 1]
    core = ids_ref[0]
    own = pick(core, hidden_ref[...], True), pick(core, branch_ref[...], True)
    got = got_state_ref[:, D:], got_ref[:, D : D + WIDE]
    lefts = (before_ref, got_ref), (active_ref, got_state_ref)
    for j in range(2):
        left = stacked(lefts[j][0][...], lefts[j][1][:, :D])
        store_parts(ids_ref, left, stacked(own[j], got[j]), right_ref, parts, j, 2)
    right = stacked(pick(core, down_ref[...], True).astype(bf16), got_ref[:, D + WIDE :])
    mixed = jnp.concatenate([mixed_ref[...], got_mixed_ref[...]], axis=1)
    mix_ref[...] = dot(mixed, right)


def cross_back_kernel(
    ids_ref,
    rows_ref,
    flat_ref,
    items_ref,
    told_ref,
    normed_ref,
    gain_feed,
    gain_self,
    gain_last,
    gain_pixel,
    sent_ref,
    other_ref,
    own_ref,
    grad_ref,
):
    core = ids_ref[0]
    ids = lax.broadcasted_iota(jnp.int32, (CP, 1), 0)
    partials = []
    total, pixel = 0.0, 0.0
    for i, told in enumerate(to_items(told_ref)):
        slots = slice(i * SLOTS, (i + 1) * SLOTS)
        log, delta = join3(told, C + 1), join3(told, C + 4)
        told = jnp.where(ids < C, told, 0.0).astype(bf16)
        asked = items_ref[i]
        attention = jnp.exp(dot(rows_ref[slots], asked) - log)
        grad_attention = dot(rows_ref[slots], told)
        grad_scores = (attention * (grad_attention - delta)).astype(bf16)
        grad_ref[slots] = dot_t(grad_scores, asked) + dot_t(attention.astype(bf16), told)
        partial = dot(flat_ref[:, slots], grad_scores)
        partials.append(partial)
        normed = normed_ref[:, i * ROWS : (i + 1) * ROWS].reshape(NLAT, D)
        total = total + dot(partial.astype(bf16), normed)
        pixel = pixel + jnp.sum(partial * asked.astype(f32), axis=1, keepdims=True)
    store_by_peer(sent_ref, *partials)
    total = total * (D**-0.5)
    pixel = as_row(pixel) + gain_pixel[...]
    pixel = jnp.concatenate([pixel, jnp.zeros((1, D - CP), f32)], axis=1)
    gains = [gain_feed[...], gain_self[...], gain_last[...], pixel]
    ids = lax.broadcasted_iota(jnp.int32, (CP - 256, 1), 0) + 256
    for first, ref in ((True, own_ref), (False, other_ref)):
        half = pick(core, total, first)
        tail = half[256:]
        for n, gain in enumerate(gains):
            row = pick(core, gain, first)
            if not first:
                high = row.astype(bf16).astype(f32)
                tail = jnp.where(ids == C + 4 + n, row - high, tail)
                row = high
            tail = jnp.where(ids == C + n, row, tail)
        total_half = jnp.concatenate([half[:256], tail], axis=0)
        ref[...] = total_half if first else total_half.astype(bf16)


def pixel_back_kernel(pixel_ref, grad_ref, gain_ref, out_ref):
    unit, scale = normal(pixel_ref[...].astype(f32))
    grad, _ = normal_back(unit, scale, gain_ref[...], grad_ref[:, :C])
    out_ref[...] = grad


def latent_back_kernel(
    ids_ref, got_ref, latent_ref, gain_ref, map_own, map_other, down_ref, grad_ref
):
    core = ids_ref[0]
    asked = got_ref[0, :CP].astype(f32)
    for s in range(1, MP):
        asked = asked + got_ref[s, :CP].astype(f32)
    ids = lax.broadcasted_iota(jnp.int32, (CP, 1), 0)
    asked = jnp.where(ids < C, asked * (D**-0.5), 0.0)
    unit, scale = normal(latent_ref[...].astype(f32))
    padded = jnp.concatenate([asked, jnp.zeros((CH - CP, LOCAL), f32)], axis=0)
    grad_normed = 0.0
    for first, ref in ((True, map_own), (False, map_other)):
        part = pick_rows(core, padded, first)
        grad_normed = grad_normed + dot(part.T.astype(bf16), side_by_side(ref, 0))
    grad, _ = normal_back(unit, scale, gain_ref[...], grad_normed)
    grad_ref[...] = down_ref[...] + grad


def total_kernel(partial_ref, got_ref, own_ref, mix_ref, *refs):
    parts, sent_ref = refs[:QUART], refs[QUART]
    got = got_ref[...].astype(f32)
    score = own_ref[...] + got
    ids = lax.broadcasted_iota(jnp.int32, (CP - 256, 1), 0) + 256
    tail = score[256:]
    for n in range(4):
        row = C - 256 + n
        gain = tail[row : row + 1] + got[C + 4 + n : C + 5 + n]
        high = gain.astype(bf16).astype(f32)
        tail = jnp.where(ids == C + n, high, tail)
        tail = jnp.where(ids == C + 4 + n, gain - high, tail)
    rest = jnp.zeros((MP * PART - 2 * CP, WIDE), f32)
    total = jnp.concatenate([mix_ref[...], score[:256], tail, rest], axis=0)
    for s in range(MP):
        sent_ref[s, :CP] = partial_ref[s]
        rows = total[s * PART : (s + 1) * PART].astype(bf16)
        for q in range(QUART):
            start = CP + q * PART
            sent_ref[s, start : start + PART] = rows[:, q * HEAD : (q + 1) * HEAD]
        for j in range(2):
            value = parts[0][s * 2 + j].astype(f32)
            for part in parts[1:]:
                value = value + part[s * 2 + j].astype(f32)
            start = CP + QUART * PART + j * HEAD
            sent_ref[s, start : start + HEAD] = value.astype(bf16)


def spread_kernel(got_ref, sent_ref):
    total = got_ref[0, CP:].astype(f32)
    for s in range(1, MP):
        total = total + got_ref[s, CP:].astype(f32)
    total = total.astype(bf16)
    for s in range(MP):
        sent_ref[s] = total


def copies_kernel(got_ref, sent_ref, tiles_ref):
    total = got_ref[0, :SHARE].astype(f32)
    for s in range(1, MP):
        total = total + got_ref[s, :SHARE].astype(f32)
    total = total.astype(bf16)
    for s in range(MP):
        sent_ref[s] = total
    for q in range(QUART):
        for j in range(2):
            rows = slice(SHARE + j * HEAD, SHARE + (j + 1) * HEAD)
            tile = got_ref[q, rows].astype(f32) + got_ref[QUART + q, rows].astype(f32)
            tiles_ref[q, j] = tile.astype(bf16)


def cross_grads_kernel(
    ids_ref,
    own_ref,
    other_ref,
    key_ref,
    query_ref,
    value_own,
    value_other,
    rows_own,
    rows_other,
    map_own,
    map_other,
    gain_latent,
    gain_pixel,
    grad_query_ref,
    grad_key_ref,
    grad_value_ref,
    grad_out_ref,
    *refs,
):
    gain_refs, pad_ref, mix_ref = refs[:5], refs[5], refs[6]
    core, mine = ids_ref[0], ids_ref[2]
    pad_ref[...] = jnp.zeros(pad_ref.shape, f32)
    pad_ref[:C] = key_ref[...].astype(f32)
    key = pad_ref[...].astype(bf16)
    out_rows = [
        jnp.concatenate([ref[s] for s in range(MP)], axis=1) for ref in (rows_own, rows_other)
    ]
    out_rows = halves(core, out_rows[0], out_rows[1], 0)
    block = pl.ds(pl.multiple_of(lax.rem(mine, QUART) * HEAD, HEAD), HEAD)
    score_map = halves(core, side_by_side(map_own, 0), side_by_side(map_other, 0), 0)
    score_map = score_map[:CP].astype(f32)
    ids = lax.broadcasted_iota(jnp.int32, (CP, 1), 0)
    grad_key, grad_value = 0.0, 0.0
    gains, mixes = [], []
    for side, ref in enumerate((own_ref, other_ref)):
        half = core if side == 0 else 1 - core
        span = pl.ds(pl.multiple_of(half * WIDE, WIDE), WIDE)
        whole = jnp.concatenate(
            [
                jnp.concatenate([ref[s, q * PART : (q + 1) * PART] for q in range(QUART)], axis=1)
                for s in range(MP)
            ],
            axis=0,
        )
        mix, score = whole[:CP], whole[CP : 2 * CP]
        mixes.append(mix)
        grad_query_ref[span, :] = dot(score.T, key)
        grad_key = grad_key + dot(score, query_ref[span, :])
        grad_value = grad_value + dot_t(mix, pick(core, out_rows, side == 0))
        tail = score[256:].astype(f32)
        rows = tail[C - 256 : C - 252] + tail[C - 252 : C - 248]
        product = jnp.where(ids < C, score.astype(f32), 0.0) * pick(core, score_map, side == 0)
        first = jnp.sum(product, axis=0, keepdims=True)
        gains.append(jnp.concatenate([first, rows], axis=0))
    grad_key_ref[...] = grad_key[:C]
    grad_value_ref[...] = grad_value[:C]
    gains = halves(core, gains[0], gains[1], 1)
    gain_refs[0][...] = (gains[:1] / gain_latent[...])[0]
    for n in range(1, 4):
        gain_refs[n][...] = gains[n]
    gain_refs[4][...] = (gains[4:5, :C] / gain_pixel[...])[0]
    half = lax.div(mine, QUART)
    mix_ref[0], mix_ref[1] = mixes[0], mixes[1]
    mix = jnp.where(half == core, mix_ref[0, :, block], mix_ref[1, :, block])
    mix = jnp.concatenate([mix, jnp.zeros((CH - CP, HEAD), bf16)], axis=0)
    grad_out_ref[...] = dot(value_own[...].T, pick_rows(core, mix, True)) + dot(
        value_other[...].T, pick_rows(core, mix, False)
    )


def finish_kernel(turned_outs, ids_ref, own_ref, other_ref, feed_own, feed_other, *outs):
    core, depth = ids_ref[0], ids_ref[1]
    for side, pair in enumerate(((own_ref, feed_own), (other_ref, feed_other))):
        half = core if side == 0 else 1 - core
        for step in range(QUART):
            for j, out in enumerate(outs):
                late = j >= 6
                block = half * QUART + (step if late else lax.rem(depth + step, QUART))
                span = pl.ds(pl.multiple_of(block * HEAD, HEAD), HEAD)
                piece = pair[1][step, j - 6] if late else pair[0][step, j]
                piece = piece.astype(f32)
                if turned_outs[j]:
                    out[span, :] = piece.T
                else:
                    out[:, span] = piece


def body(
    latents,
    pixels,
    masks,
    cotangent,
    norm_latent,
    norm_pixel,
    norm_feed,
    norm_self,
    norm_last,
    cross_query,
    cross_key,
    cross_value,
    cross_out,
    feed_in,
    feed_out,
    self_query,
    self_key,
    self_value,
    self_out,
    last_in,
    last_out,
):
    core = lax.axis_index("dp") % 2
    mine = lax.axis_index("mp")
    depth = (lax.axis_index("dp") // 2) % QUART
    core_id = jnp.stack([core, depth, mine]).astype(jnp.int32)
    gain_latent, gain_pixel, gain_feed, gain_self, gain_last = (
        g[None, :] for g in (norm_latent, norm_pixel, norm_feed, norm_self, norm_last)
    )
    latent_rows = latents.reshape(LOCAL, D)
    pixel_rows = pixels.reshape(ITEMS * SLOTS, C)
    cotangent_rows = cotangent.reshape(LOCAL, D)
    row_f32, row_bf16 = ((LOCAL, D), f32), ((LOCAL, D), bf16)
    gain_row = ((1, D), f32)

    def come(x, step):
        return lax.ppermute(x, "dp", DEPTH[QUART - step])

    map_shape = ((MP, CH, HEAD), bf16)
    (sent,) = run(
        map_start_kernel,
        2,
        [((MP, CH + 2 * HEAD + ROWS, HEAD), bf16)],
        core_id,
        cross_key,
        cross_query,
        cross_value,
        feed_in,
        feed_out,
        cross_out,
        scratch=[pltpu.VMEM((2, CH, HEAD), f32)],
    )
    (tile,) = run(
        tiles_kernel,
        1,
        [((6, HEAD, HEAD), bf16)],
        core_id,
        self_out,
        last_in,
        last_out,
        self_query,
        self_key,
        self_value,
        hot_outs=(),
    )
    pixel_in, pixel_flat = run(
        pixel_kernel,
        2,
        [((ITEMS * SLOTS, CP), bf16), ((CP, ITEMS * SLOTS), bf16)],
        pixel_rows,
        masks,
        gain_pixel,
        scratch=[pltpu.VMEM((ITEMS * SLOTS, 384), f32)],
        hot_outs=(),
    )
    packs = lax.all_gather(tile, "mp")
    got, (pixel_in, pixel_flat) = after(exchange(sent), pixel_in, pixel_flat)

    def along(x):
        return lax.all_gather(x, "dp", axis_index_groups=ALONG_Z)

    sent, value_half, feed_pack, out_rows = run(
        map_sum_kernel,
        1,
        [
            map_shape,
            ((HALF, D), bf16),
            ((MP, 2, HEAD, HEAD), bf16),
            ((MP, ROWS, HEAD), bf16),
        ],
        got,
        cross_out,
        hot=(0,),
    )
    feed_pieces = [feed_pack, None, come(feed_pack, 2), None]
    map_own, (packs, feed_pieces[2]) = after(exchange(sent), packs, feed_pieces[2])
    map_other = core_swap(map_own)
    packs = along(packs)
    peer_shape = ((MP, CP, HEAD), bf16)
    sent, normed = run(
        asked_kernel,
        1,
        [peer_shape, row_bf16],
        core_id,
        map_own,
        map_other,
        latent_rows,
        gain_latent,
        hot=(1, 2),
        hot_outs=(),
    )
    feed_pieces[1], feed_pieces[3] = come(feed_pack, 1), come(feed_pack, 3)
    asked_all, (feed_pieces[1], feed_pieces[3]) = after(
        exchange(sent), feed_pieces[1], feed_pieces[3]
    )
    feed_pieces = feed_pieces + [core_swap(v) for v in feed_pieces]
    sent, asked_items = run(
        cross_kernel,
        3,
        [peer_shape, ((ITEMS, CP, NLAT), bf16)],
        pixel_in,
        pixel_flat,
        asked_all,
        hot=(2,),
        hot_outs=(),
    )
    sent, mixed, lse, state_one, feed_hidden, feed_active, feed_slope, state_two, mixed_low, state_pack = run(
        state_kernel,
        4,
        [
            ((MP, LOCAL, D), bf16),
            ((CP, LOCAL), f32),
            ((1, LOCAL), f32),
            row_f32,
            row_bf16,
            row_bf16,
            row_f32,
            row_f32,
            ((CP, LOCAL), bf16),
            ((LOCAL, D + WIDE), bf16),
        ],
        core_id,
        exchange(sent),
        latent_rows,
        map_own,
        map_other,
        gain_feed,
        gain_self,
        *feed_pieces,
        scratch=full_shape(2),
        far=range(7, 15),
        hot=(1,),
        hot_outs=(),
    )

    hidden_all, (packs, normed, got_mixed, got_state) = after(
        exchange(sent), packs, normed, core_swap(mixed_low), core_swap(state_pack)
    )
    other_packs = core_swap(packs)
    normed_all = lax.all_gather(normed, "mp")
    heads_shape = ((MP, ITEMS, ROWS, HEAD), bf16)
    sent, queries, keys, values, logs = run(
        heads_kernel,
        3,
        [heads_shape] * 4 + [((ITEMS, NLAT), f32)],
        hidden_all,
        self_query,
        self_key,
        self_value,
        hot=(0,),
    )
    got = exchange(sent)
    sent, up, result, heads_out, last_hidden, last_active, last_before, grad_last, back_pack = run(
        last_kernel,
        6,
        [
            ((MP, LOCAL, HEAD), bf16),
            row_f32,
            row_bf16,
            row_bf16,
            row_bf16,
            row_bf16,
            row_bf16,
            gain_row,
            ((LOCAL, 3 * (D + WIDE)), bf16),
        ],
        core_id,
        got.reshape(MP, LOCAL, HEAD),
        state_two,
        gain_last,
        cotangent_rows,
        packs,
        other_packs,
        scratch=full_shape(3) + [pltpu.VMEM((LOCAL, D), f32)],
        pinned=(5, 6),
        hot=(1,),
    )

    def tiles(count):
        return ((QUART, count, HEAD, HEAD), bf16)

    def along_sum(x):
        count = x.shape[1]
        x = x.reshape(QUART * count * HEAD, HEAD)
        x = lax.psum_scatter(x, "dp", axis_index_groups=ALONG_Z, tiled=True)
        return x.reshape(count, HEAD, HEAD)

    (last_own,) = run(
        last_grads_kernel,
        3,
        [tiles(3 * MP)],
        core_id,
        heads_out,
        up,
        last_hidden,
        last_active,
        last_before,
        cotangent_rows,
        core_swap(back_pack),
        hot=(7,),
        hot_outs=(),
    )
    grad_heads, (last_own,) = after(exchange(sent), last_own)

    def give(parts):
        return [lax.ppermute(parts[step], "dp", DEPTH[step]) for step in (1, 2, 3)]

    def all_of(first, *others):
        total = first.astype(f32)
        for other in others:
            total = total + other.astype(f32)
        return total.astype(bf16)

    grad_heads = grad_heads.reshape(MP, ITEMS, ROWS, HEAD)
    sent, dq, dk, dv = run(
        heads_back_kernel,
        4,
        [((MP, LOCAL, 3 * HEAD), bf16)] + [heads_shape] * 3,
        grad_heads,
        queries,
        keys,
        values,
        logs,
        hot=(0,),
    )
    last_own, (normed_all, _) = after(last_own, normed_all, dq)
    last_sum = along_sum(last_own)
    self_own, self_other = run(
        heads_grads_kernel, 2, [tiles(3)] * 2, core_id, hidden_all, dq, dk, dv, hot_outs=()
    )
    self_parts = (self_own.astype(f32) + core_swap(self_other).astype(f32)).astype(bf16)
    got, (self_parts,) = after(exchange(sent), self_parts)
    sent, down, feed_before, feed_branch, grad_self, grad_feed, feed_back, grad_pixel = run(
        feed_back_kernel,
        4,
        [peer_shape, row_f32, row_bf16, row_bf16, gain_row, gain_row, ((LOCAL, 2 * D), bf16), ((1, CP), f32)],
        core_id,
        got,
        state_two,
        state_one,
        up,
        feed_slope,
        mixed,
        lse,
        map_own,
        map_other,
        gain_feed,
        gain_self,
        *feed_pieces,
        packs,
        other_packs,
        scratch=full_shape(3) + full_shape(2),
        far=range(12, 20),
        pinned=(20, 21),
        hot=(1,),
    )
    *feed_parts, mix_own = run(
        feed_grads_kernel,
        2,
        [((2 * MP, HEAD, HEAD), bf16)] * QUART + [((CP, WIDE), f32)],
        core_id,
        feed_hidden,
        feed_active,
        feed_before,
        feed_branch,
        down,
        mixed_low,
        got_mixed,
        got_state,
        core_swap(feed_back),
        scratch=[pltpu.VMEM((2, 2 * LOCAL, WIDE), bf16)],
        loose=(7, 8),
        hot=(9,),
        hot_outs=(),
    )
    feed_got = give(feed_parts)
    last_sum, _ = after(last_sum, feed_parts[0])
    told_all, (self_parts, *_) = after(exchange(sent), self_parts, *feed_parts)
    self_got = give(self_parts)
    last_rows = last_sum.reshape(MP * 3 * HEAD, HEAD)
    last_piece = lax.psum_scatter(last_rows, "mp", tiled=True).reshape(3, HEAD, HEAD)
    partial, other, own, grad_pixel_in = run(
        cross_back_kernel,
        4,
        [peer_shape, ((CP, WIDE), bf16), ((CP, WIDE), f32), ((ITEMS * SLOTS, CP), f32)],
        core_id,
        pixel_in,
        pixel_flat,
        asked_items,
        told_all,
        normed_all,
        grad_feed,
        grad_self,
        grad_last,
        grad_pixel,
        hot=(4,),
        hot_outs=(0, 1, 2),
    )
    both = CP + SHARE + 2 * HEAD
    (sent,) = run(
        total_kernel,
        1,
        [((MP, both, HEAD), bf16)],
        partial,
        core_swap(other),
        own,
        mix_own,
        feed_parts[0],
        *feed_got,
        hot=(0, 1, 2),
        loose=(5, 6, 7),
    )
    (grad_pixels,) = run(
        pixel_back_kernel,
        2,
        [((ITEMS * SLOTS, C), f32)],
        pixel_rows,
        grad_pixel_in,
        gain_pixel,
        hot_outs=(),
    )
    grad_pixels = grad_pixels.reshape(ITEMS, SLOTS, C).transpose(2, 0, 1)
    pieces = jnp.concatenate([last_piece, all_of(self_parts[0], *self_got)], axis=0)
    far = lax.ppermute(pieces, "dp", FAR)
    got, (grad_pixels, pieces, far) = after(exchange(sent), grad_pixels, pieces, far)
    (sent,) = run(
        spread_kernel, 1, [((MP, SHARE + 2 * HEAD, HEAD), bf16)], got, hot=(0,)
    )
    (grad_latents,) = run(
        latent_back_kernel,
        2,
        [row_f32],
        core_id,
        got,
        latent_rows,
        gain_latent,
        map_own,
        map_other,
        down,
        hot=(1,),
        hot_outs=(),
    )
    x = all_of(pieces, far)
    got, (grad_latents, x) = after(grouped(sent, "dp", COPIES), grad_latents, x)
    sent, feed_own = run(
        copies_kernel,
        1,
        [((MP, SHARE, HEAD), bf16), ((QUART, 2, HEAD, HEAD), bf16)],
        got,
        hot=(0,),
    )
    own, pieces = after(exchange(sent), x, *(come(x, step) for step in (1, 2, 3)))
    pieces = jnp.stack(pieces)
    flips = (False, True, False, True, True, True, True, False)
    finished = run(
        functools.partial(finish_kernel, flips),
        2,
        [((D, HEAD) if flip else (HEAD, D), f32) for flip in flips],
        core_id,
        pieces,
        core_swap(pieces),
        feed_own,
        core_swap(feed_own),
        loose=(1, 2, 4),
        hot_outs=(),
    )
    grad_self_out, grad_last_in, grad_last_out, grad_sq, grad_sk, grad_sv = finished[:6]
    grad_feed_in, grad_feed_out = finished[6:]
    row_out, key_out = ((D, HEAD), f32), ((C, HEAD), f32)
    grad_cross_query, grad_cross_key, grad_cross_value, grad_cross_out, *gains = run(
        cross_grads_kernel,
        3,
        [row_out, key_out, key_out, row_out] + [((D,), f32)] * 4 + [((C,), f32)],
        core_id,
        own,
        core_swap(own),
        cross_key,
        cross_query,
        value_half,
        core_swap(value_half),
        out_rows,
        core_swap(out_rows),
        map_own,
        map_other,
        gain_latent,
        gain_pixel,
        scratch=[pltpu.VMEM((CP, HEAD), f32), pltpu.VMEM((2, CP, WIDE), bf16)],
        hot=(1, 2),
        loose=(6, 8),
        hot_outs=(),
    )

    shape = (ITEMS, ROWS, D)
    return (
        result.reshape(shape),
        grad_latents.reshape(shape),
        grad_pixels.transpose(1, 2, 0),
        gains[0],
        gains[4],
        gains[1],
        gains[2],
        gains[3],
        grad_cross_query,
        grad_cross_key,
        grad_cross_value,
        grad_cross_out,
        grad_feed_in,
        grad_feed_out,
        grad_sq,
        grad_sk,
        grad_sv,
        grad_self_out,
        grad_last_in,
        grad_last_out,
    )


def solution(mesh):
    rows = P("dp", "mp", None)
    columns = P(None, "mp")
    depth = P("mp", None)
    return jax.shard_map(
        body,
        mesh=mesh,
        in_specs=(rows, rows, P("dp", "mp"), rows)
        + (P(),) * 5
        + (columns,) * 5
        + (depth,)
        + (columns,) * 3
        + (depth, columns, depth),
        out_specs=(rows,) * 3
        + (P(),) * 5
        + (columns,) * 5
        + (depth,)
        + (columns,) * 3
        + (depth, columns, depth),
        check_vma=False,
    )
```

```python
import functools

import jax
import jax.numpy as jnp
from jax import lax
from jax.experimental import pallas as pl
from jax.experimental.pallas import tpu as pltpu
from jax.sharding import PartitionSpec as P

D = 1024
C = 261
CP = 272
CH = 288
HALF = 144
HEADS = 8
HEAD = 128
MP = 8
ITEMS = 2
ROWS = 64
LOCAL = ITEMS * ROWS
SLOTS = 512
NLAT = 512
WIDE = 512
MEMBERS = 64
PART = 80
QUART = 4
SHARE = QUART * PART
LIMIT = 24 << 20
EPS = 1e-05
MASKED = -1e30
GELU_A = 0.044715
GELU_K = 0.7978845608028654

bf16 = jnp.bfloat16
f32 = jnp.float32

SWAP = [(i, i ^ 1) for i in range(16)]
CHIPS = [
    [(d * 2 + core) * MP + m for d in range(8) for m in range(MP)] for core in range(2)
]
DEPTH = [
    [((y * 4 + z) * 2 + c, (y * 4 + (z + k) % 4) * 2 + c) for y in range(2) for z in range(4) for c in range(2)]
    for k in range(4)
]
FAR = [(i, i ^ 8) for i in range(16)]
NEAR = [(i, i ^ 4) for i in range(MP)]
OPPOSITE = [(i, i ^ 68) for i in range(128)]
ACROSS = [[(y * 4 + x, y * 4 + (x + k) % 4) for y in range(2) for x in range(4)] for k in range(4)]
COPIES = [[d * 2 + core for d in range(8)] for core in range(2)]
ALONG_Z = [[(y * 4 + z) * 2 + core for z in range(4)] for y in range(2) for core in range(2)]


def dot(a, b):
    return lax.dot_general(a, b, (((1,), (0,)), ((), ())), preferred_element_type=f32)


def dot_t(a, b):
    return lax.dot_general(a, b, (((1,), (1,)), ((), ())), preferred_element_type=f32)


def t_dot(a, b):
    return dot(a.T, b)


def cost(micros):
    return pl.CostEstimate(
        flops=int(micros * 1e7), bytes_accessed=int(micros * 2e4), transcendentals=0
    )


class Arriving:
    def __init__(self, ref, copy):
        self.ref, self.copy, self.shape = ref, copy, ref.shape

    def settle(self):
        if self.copy is not None:
            self.copy.wait()
        self.copy = None

    def __getitem__(self, index):
        self.settle()
        return self.ref[index]


class Leaving:
    def __init__(self, ref, copy):
        self.ref, self.copy, self.shape, self.left = ref, copy, ref.shape, False

    def leave(self):
        if not self.left:
            self.copy.start()
        self.left = True

    def __getitem__(self, index):
        return self.ref[index]

    def __setitem__(self, index, value):
        self.ref[index] = value
        if index is Ellipsis:
            self.leave()


def run(kernel, micros, outs, *args, scratch=(), far=(), pinned=(), loose=(), hot=(), hot_outs=(0,)):
    specs, homes = [], []
    for n, a in enumerate(args):
        if jnp.ndim(a) == 1 and a.dtype == jnp.int32:
            space = pltpu.SMEM
        elif n in hot:
            space = pltpu.VMEM
        elif n in far:
            space = pl.ANY
        elif n in pinned:
            space = pltpu.HBM
        else:
            space = pl.ANY if n in loose else pltpu.HBM
            homes.append(n)
        specs.append(pl.BlockSpec(memory_space=space))
    out_homes = [n for n in range(len(outs)) if n not in hot_outs]
    buffers = [pltpu.VMEM(args[n].shape, args[n].dtype) for n in homes]
    buffers += [pltpu.VMEM(*outs[n]) for n in out_homes]

    def wrapped(*refs):
        refs = list(refs)
        sems, refs = refs[-1], refs[:-1]
        given, refs = refs[: len(args)], refs[len(args) :]
        made, refs = refs[: len(outs)], refs[len(outs) :]
        own, refs = refs[: len(scratch)], refs[len(scratch) :]
        for k, n in enumerate(homes):
            copy = pltpu.make_async_copy(given[n], refs[k], sems.at[k])
            copy.start()
            given[n] = Arriving(refs[k], copy)
        for k, n in enumerate(out_homes, len(homes)):
            made[n] = Leaving(refs[k], pltpu.make_async_copy(refs[k], made[n], sems.at[k]))
        kernel(*given, *made, *own)
        for n in homes:
            given[n].settle()
        for n in out_homes:
            made[n].leave()
        for n in out_homes:
            made[n].copy.wait()

    return pl.pallas_call(
        wrapped,
        out_shape=[
            jax.ShapeDtypeStruct(*out) if n in hot_outs else pltpu.HBM(*out)
            for n, out in enumerate(outs)
        ],
        in_specs=specs,
        out_specs=[
            pl.BlockSpec(memory_space=pltpu.VMEM if n in hot_outs else pltpu.HBM)
            for n in range(len(outs))
        ],
        scratch_shapes=[
            *scratch,
            *buffers,
            pltpu.SemaphoreType.DMA((max(1, len(buffers)),)),
        ],
        compiler_params=pltpu.CompilerParams(vmem_limit_bytes=LIMIT),
        cost_estimate=cost(micros),
    )(
        *(
            pltpu.with_memory_space_constraint(a, pltpu.HBM)
            if n in pinned or (n in homes and n not in loose)
            else a
            for n, a in enumerate(args)
        )
    )


def after(x, *waits):
    x, *waits = lax.optimization_barrier((x, *waits))
    return x, waits


def core_swap(x):
    return lax.ppermute(x, "dp", SWAP)


def exchange(x):
    return lax.all_to_all(x, "mp", 0, 0, tiled=True)


def to_all(x):
    return exchange(jnp.broadcast_to(x[None], (MP,) + x.shape))


def grouped(x, axes, groups):
    return lax.all_to_all(x, axes, 0, 0, tiled=True, axis_index_groups=groups)


def grouped_all(x, axes, groups):
    return grouped(jnp.broadcast_to(x[None], (len(groups[0]),) + x.shape), axes, groups)


def added(x):
    return jnp.sum(x.astype(f32), axis=0).astype(bf16)


def normal(v):
    center = v - jnp.mean(v, axis=-1, keepdims=True)
    spread = jnp.mean(center * center, axis=-1, keepdims=True)
    scale = lax.rsqrt(spread + EPS)
    return center * scale, scale


def normal_back(unit, scale, gain, upstream):
    grad_gain = jnp.sum(upstream * unit, axis=0, keepdims=True)
    grad_unit = upstream * gain
    inner = jnp.mean(grad_unit * unit, axis=-1, keepdims=True)
    grad = scale * (grad_unit - jnp.mean(grad_unit, axis=-1, keepdims=True) - unit * inner)
    return grad, grad_gain


def gelu_parts(v):
    square = v * v
    t = jnp.tanh(GELU_K * v * (1.0 + GELU_A * square))
    value = 0.5 * v * (1.0 + t)
    slope = 0.5 * (1.0 + t) + 0.5 * v * (1.0 - t * t) * GELU_K * (1.0 + 3.0 * GELU_A * square)
    return value, slope


def split3(v):
    high = v.astype(bf16).astype(f32)
    middle = (v - high).astype(bf16).astype(f32)
    return [high, middle, v - high - middle]


def join3(rows, start):
    return rows[start : start + 1] + rows[start + 1 : start + 2] + rows[start + 2 : start + 3]


def halves(core, own, other, axis):
    first = jnp.where(core == 0, own, other)
    second = jnp.where(core == 0, other, own)
    return jnp.concatenate([first, second], axis=axis)


def pick(core, v, own):
    take_low = core == 0 if own else core != 0
    return jnp.where(take_low, v[:, :WIDE], v[:, WIDE:])


def pick_rows(core, v, own):
    take_low = core == 0 if own else core != 0
    return jnp.where(take_low, v[:HALF], v[HALF:])


def full_shape(count):
    return [
        pltpu.VMEM((count, MP, HEAD, D), bf16),
        pltpu.SemaphoreType.DMA((count, 2, QUART)),
    ]


def fetch_steps(ids_ref, pieces, full_ref, sems):
    core, depth = ids_ref[0], ids_ref[1]
    copies = []
    for j in range(full_ref.shape[0]):
        for n, ref in enumerate(pieces):
            side, step = n // QUART, n % QUART
            half = core if side == 0 else 1 - core
            block = half * QUART + lax.rem(depth + step, QUART)
            columns = pl.ds(pl.multiple_of(block * HEAD, HEAD), HEAD)
            copies.append(
                pltpu.make_async_copy(
                    ref.at[:, j], full_ref.at[j, :, :, columns], sems.at[j, side, step]
                )
            )
            copies[-1].start()
    return copies


def fetch_all(ids_ref, pieces, full_ref, sems, base):
    core = ids_ref[0]
    copies = []
    for j in range(full_ref.shape[0]):
        for side, ref in enumerate(pieces):
            half = core if side == 0 else 1 - core
            for q in range(QUART):
                columns = pl.ds(pl.multiple_of((half * QUART + q) * HEAD, HEAD), HEAD)
                copies.append(
                    pltpu.make_async_copy(
                        ref.at[q, :, base + j], full_ref.at[j, :, :, columns], sems.at[j, side, q]
                    )
                )
                copies[-1].start()
    return copies


def arrive(copies, j):
    for copy in copies[j * 2 * QUART : (j + 1) * 2 * QUART]:
        copy.wait()


def matrix(full_ref, j):
    return full_ref[j].reshape(D, D)


def times_in(x, full_ref, j):
    return dot_t(x, matrix(full_ref, j))


def times_out(x, full_ref, j):
    return dot(x, matrix(full_ref, j))


def store_blocks(ids_ref, grad, own_ref, other_ref, place):
    core, depth = ids_ref[0], ids_ref[1]
    for first, ref in ((True, own_ref), (False, other_ref)):
        half = pick(core, grad, first).astype(bf16)
        for q in range(QUART):
            step = lax.rem(q + QUART - depth, QUART)
            ref[step, place] = half[:, q * HEAD : (q + 1) * HEAD]


def stacked(own, got):
    return jnp.concatenate([own, got], axis=0)


def store_grad(left, right, own_ref, j, count):
    flipped = left.T
    for s in range(MP):
        grad = dot(flipped[s * HEAD : (s + 1) * HEAD], right).astype(bf16)
        for q in range(QUART):
            own_ref[q, s * count + j] = grad[:, q * HEAD : (q + 1) * HEAD]


def store_parts(ids_ref, left, right, right_ref, parts, j, count):
    right_ref[j] = right
    blocks = []
    for step in range(QUART):
        columns = pl.multiple_of(lax.rem(ids_ref[1] + step, QUART) * HEAD, HEAD)
        blocks.append(right_ref[j, :, pl.ds(columns, HEAD)])
    right = jnp.concatenate(blocks, axis=1)
    flipped = left.T
    for s in range(MP):
        grad = dot(flipped[s * HEAD : (s + 1) * HEAD], right).astype(bf16)
        for step, part in enumerate(parts):
            part[s * count + j] = grad[:, step * HEAD : (step + 1) * HEAD]


def as_row(column):
    return jnp.broadcast_to(column, (column.shape[0], HEAD)).T[:1]


def side_by_side(ref, start):
    return jnp.concatenate([ref[s, start : start + HALF] for s in range(MP)], axis=1)


def lane_halves():
    return lax.broadcasted_iota(jnp.int32, (1, HEAD), 1) < ROWS


def turned(x):
    return pltpu.roll(x, ROWS, 1)


def to_items(ref):
    low = lane_halves()
    items = [[], []]
    for p in range(0, MP, 2):
        a, b = ref[p].astype(f32), ref[p + 1].astype(f32)
        items[0].append(jnp.where(low, a, turned(b)))
        items[1].append(jnp.where(low, turned(a), b))
    return [jnp.concatenate(v, axis=1) for v in items]


def store_by_peer(ref, first, second):
    low = lane_halves()
    for p in range(0, MP, 2):
        x, y = (v[:, p * ROWS : (p + 2) * ROWS] for v in (first, second))
        ref[p] = jnp.where(low, x, turned(y)).astype(bf16)
        ref[p + 1] = jnp.where(low, turned(x), y).astype(bf16)


def with_tail(x, rows):
    ids = lax.broadcasted_iota(jnp.int32, (CP - 256, 1), 0) + 256
    tail = jnp.where(ids < C, x[256:CP], 0.0)
    for offset, row in enumerate(rows):
        tail = jnp.where(ids == C + 1 + offset, row, tail)
    return jnp.concatenate([x[:256], tail], axis=0)


def map_start_kernel(
    ids_ref,
    key_ref,
    query_ref,
    value_ref,
    feed_in_ref,
    feed_out_ref,
    self_out_ref,
    last_in_ref,
    last_out_ref,
    wq_ref,
    wk_ref,
    wv_ref,
    out_ref,
    sent_ref,
    tiles_ref,
    pad_ref,
):
    core = ids_ref[0]
    span = pl.ds(pl.multiple_of((core * QUART + ids_ref[1]) * HEAD, HEAD), HEAD)
    tiles_ref[0] = self_out_ref[:, span]
    tiles_ref[1] = last_in_ref[span, :].T
    tiles_ref[2] = last_out_ref[:, span]
    for n, ref in enumerate((wq_ref, wk_ref, wv_ref)):
        tiles_ref[3 + n] = ref[span, :].T
    tiles_ref.leave()
    tiles = [feed_in_ref[span, :].T, feed_out_ref[:, span]]
    pad_ref[...] = jnp.zeros(pad_ref.shape, f32)
    pad_ref[0, :C] = key_ref[...].astype(f32)
    pad_ref[1, :C] = value_ref[...].astype(f32)
    key = jnp.where(core == 0, pad_ref[0, :HALF], pad_ref[0, HALF:]).astype(bf16)
    value = jnp.where(core == 0, pad_ref[1, :HALF], pad_ref[1, HALF:]).astype(bf16)
    for s in range(MP):
        block = query_ref[s * HEAD : (s + 1) * HEAD]
        sent_ref[s, :HALF] = dot_t(key, block).astype(bf16)
        sent_ref[s, HALF:CH] = value
        for j, tile in enumerate(tiles):
            sent_ref[s, CH + j * HEAD : CH + (j + 1) * HEAD] = tile
        rows = pl.ds(pl.multiple_of(s * HEAD + core * ROWS, ROWS), ROWS)
        sent_ref[s, CH + 2 * HEAD :] = out_ref[rows, :]


def map_sum_kernel(got_ref, out_ref, sent_ref, value_ref, feed_ref, rows_ref):
    for s in range(MP):
        for j in range(2):
            feed_ref[s, j] = got_ref[s, CH + j * HEAD : CH + (j + 1) * HEAD]
        rows_ref[s] = got_ref[s, CH + 2 * HEAD :]
    feed_ref.leave()
    score = got_ref[0, :HALF].astype(f32)
    for s in range(1, MP):
        score = score + got_ref[s, :HALF].astype(f32)
    value = side_by_side(got_ref, HALF)
    value_ref[...] = value
    score = score.astype(bf16)
    mix = dot(value, out_ref[...]).astype(bf16)
    for s in range(MP):
        sent_ref[s, :HALF] = score
        sent_ref[s, HALF:] = mix


def asked_kernel(core_ref, own_ref, other_ref, latent_ref, gain_ref, sent_ref, normed_ref):
    core = core_ref[0]
    unit, _ = normal(latent_ref[...].astype(f32))
    normed = (unit * gain_ref[...]).astype(bf16)
    normed_ref[...] = normed
    asked = halves(
        core, dot_t(side_by_side(own_ref, 0), normed), dot_t(side_by_side(other_ref, 0), normed), 0
    )
    ids = lax.broadcasted_iota(jnp.int32, (CP, 1), 0)
    asked = jnp.where(ids < C, asked[:CP] * (D**-0.5), jnp.where(ids == C, 1.0, 0.0))
    asked = asked.astype(bf16)
    for s in range(MP):
        sent_ref[s] = asked


def pixel_kernel(pixel_ref, mask_ref, gain_ref, rows_ref, flat_ref, pad_ref):
    unit, _ = normal(pixel_ref[...].astype(f32))
    pad_ref[...] = jnp.zeros(pad_ref.shape, f32)
    pad_ref[:, :C] = unit * gain_ref[...]
    flat = pad_ref[...].T[:CP]
    bias = jnp.where(mask_ref[...] > 0, 0.0, MASKED)
    bias = jnp.concatenate([bias[i : i + 1] for i in range(ITEMS)], axis=1)
    ids = lax.broadcasted_iota(jnp.int32, (CP, 1), 0)
    flat = jnp.where(ids == C, bias, flat)
    flat_ref[...] = flat.astype(bf16)
    lanes = lax.broadcasted_iota(jnp.int32, (1, CP), 1)
    rows_ref[...] = flat.T.astype(bf16)


def cross_kernel(rows_ref, flat_ref, asked_ref, sent_ref, items_ref):
    sums = []
    for i, asked in enumerate(to_items(asked_ref)):
        asked = asked.astype(bf16)
        items_ref[i] = asked
        slots = slice(i * SLOTS, (i + 1) * SLOTS)
        scores = dot(rows_ref[slots], asked)
        peak = jnp.max(scores, axis=0, keepdims=True)
        weight = jnp.exp(scores - peak)
        total = jnp.sum(weight, axis=0, keepdims=True)
        mixed = dot(flat_ref[:, slots], weight.astype(bf16))
        sums.append(with_tail(mixed, split3(peak) + split3(total)))
    store_by_peer(sent_ref, *sums)


def feed_forward(stream, gain, copies, full_ref, j, hidden_ref, active_ref, slope_ref):
    unit, _ = normal(stream)
    hidden = (unit * gain).astype(bf16)
    hidden_ref[...] = hidden
    arrive(copies, j)
    active, slope = gelu_parts(times_in(hidden, full_ref, j))
    active = active.astype(bf16)
    active_ref[...] = active
    slope_ref[...] = slope
    arrive(copies, j + 1)
    return times_out(active, full_ref, j + 1)


def state_kernel(ids_ref, got_ref, latent_ref, map_own, map_other, gain_feed, gain_self, *refs):
    pieces, refs = refs[: 2 * QUART], refs[2 * QUART :]
    sent_ref, mixed_ref, lse_ref, one_ref, hidden_ref, active_ref, slope_ref, two_ref = refs[:8]
    low_ref, pack_ref, full_ref, sems = refs[8:]
    copies = fetch_steps(ids_ref, pieces, full_ref, sems)
    core = ids_ref[0]
    got = [got_ref[s].astype(f32) for s in range(MP)]
    peaks = [join3(g, C + 1) for g in got]
    totals = [join3(g, C + 4) for g in got]
    peak = peaks[0]
    for s in range(1, MP):
        peak = jnp.maximum(peak, peaks[s])
    shares = [jnp.exp(p - peak) for p in peaks]
    total = shares[0] * totals[0]
    mixed = shares[0] * got[0]
    for s in range(1, MP):
        total = total + shares[s] * totals[s]
        mixed = mixed + shares[s] * got[s]
    ids = lax.broadcasted_iota(jnp.int32, (CP, 1), 0)
    mixed = jnp.where(ids < C, mixed / total, 0.0)
    lse_ref[...] = peak + jnp.log(total)
    mixed_ref[...] = mixed
    low_ref[...] = mixed.astype(bf16)
    mixed = jnp.concatenate([mixed, jnp.zeros((CH - CP, LOCAL), f32)], axis=0)
    one = latent_ref[...].astype(f32)
    for first, ref in ((True, map_own), (False, map_other)):
        part = pick_rows(core, mixed, first)
        one = one + dot(part.T.astype(bf16), side_by_side(ref, HALF))
    one_ref[...] = one
    two = one + feed_forward(
        one, gain_feed[...], copies, full_ref, 0, hidden_ref, active_ref, slope_ref
    )
    two_ref[...] = two
    pack_ref[...] = jnp.concatenate([active_ref[...], pick(core, hidden_ref[...], False)], axis=1)
    unit, _ = normal(two)
    hidden = (unit * gain_self[...]).astype(bf16)
    for s in range(MP):
        sent_ref[s] = hidden


def heads_kernel(all_ref, wq_ref, wk_ref, wv_ref, sent_ref, q_ref, k_ref, v_ref, log_ref):
    weight = jnp.concatenate([wq_ref[...], wk_ref[...], wv_ref[...]], axis=1)
    for s in range(MP):
        rows = dot(all_ref[s], weight).astype(bf16)
        for n, ref in enumerate((q_ref, k_ref, v_ref)):
            ref[s] = rows[:, n * HEAD : (n + 1) * HEAD].reshape(ITEMS, ROWS, HEAD)
    for i in range(ITEMS):
        q, k, v = (ref[:, i].reshape(NLAT, HEAD) for ref in (q_ref, k_ref, v_ref))
        scores = dot_t(k, q) * HEAD**-0.5
        top = jnp.max(scores, axis=0, keepdims=True)
        log = top + jnp.log(jnp.sum(jnp.exp(scores - top), axis=0, keepdims=True))
        log_ref[i : i + 1] = log
        attention = jnp.exp(scores - log).astype(bf16)
        out = dot(v.T, attention).T.astype(bf16)
        sent_ref[:, i] = out.reshape(MP, ROWS, HEAD)


def last_kernel(ids_ref, got_ref, two_ref, gain_ref, cotangent_ref, *refs):
    pieces, refs = refs[:2], refs[2:]
    sent_ref, up_ref, result_ref, heads_ref, hidden_ref, active_ref, before_ref = refs[:7]
    grad_gain_ref, pack_ref, full_ref, sems, slope_ref = refs[7:]
    core = ids_ref[0]
    copies = fetch_all(ids_ref, pieces, full_ref, sems, 0)
    heads = jnp.concatenate([got_ref[s] for s in range(MP)], axis=1)
    heads_ref[...] = heads
    arrive(copies, 0)
    three = two_ref[...] + times_out(heads, full_ref, 0)
    branch = feed_forward(
        three, gain_ref[...], copies, full_ref, 1, hidden_ref, active_ref, slope_ref
    )
    result_ref[...] = (three + branch).astype(bf16)
    upstream = cotangent_ref[...]
    grad_active = times_in(upstream, full_ref, 2)
    grad_before = (grad_active * slope_ref[...]).astype(bf16)
    before_ref[...] = grad_before
    grad_hidden = times_out(grad_before, full_ref, 1)
    unit, scale = normal(three)
    grad, grad_gain = normal_back(unit, scale, gain_ref[...], grad_hidden)
    grad_gain_ref[...] = grad_gain
    up = upstream.astype(f32) + grad
    up_ref[...] = up
    dy = up.astype(bf16)
    grad_heads = times_in(dy, full_ref, 0).astype(bf16)
    for s in range(MP):
        sent_ref[s] = grad_heads[:, s * HEAD : (s + 1) * HEAD]
    rights = [pick(core, v, False) for v in (dy, hidden_ref[...], upstream)]
    lefts = [heads, grad_before, active_ref[...]]
    pack_ref[...] = jnp.concatenate(lefts + rights, axis=1)


def last_grads_kernel(
    ids_ref, heads_ref, up_ref, hidden_ref, active_ref, before_ref, upstream_ref, got_ref, own
):
    core = ids_ref[0]
    lefts = heads_ref, before_ref, active_ref
    rights = up_ref, hidden_ref, upstream_ref
    for j in range(3):
        got_left = got_ref[:, j * D : (j + 1) * D]
        got_right = got_ref[:, 3 * D + j * WIDE : 3 * D + (j + 1) * WIDE]
        right = pick(core, rights[j][...], True).astype(bf16)
        store_grad(stacked(lefts[j][...], got_left), stacked(right, got_right), own, j, 3)


def heads_grads_kernel(ids_ref, all_ref, dq_ref, dk_ref, dv_ref, own, other):
    rows = all_ref[...].reshape(MP * LOCAL, D)
    for n, ref in enumerate((dq_ref, dk_ref, dv_ref)):
        grad = dot(ref[...].reshape(MP * LOCAL, HEAD).T, rows)
        store_blocks(ids_ref, grad, own, other, n)


def heads_back_kernel(
    got_ref,
    q_ref,
    k_ref,
    v_ref,
    log_ref,
    sent_ref,
    dq_ref,
    dk_ref,
    dv_ref,
):
    scale = HEAD**-0.5
    for i in range(ITEMS):
        q, k, v, g = (ref[:, i].reshape(NLAT, HEAD) for ref in (q_ref, k_ref, v_ref, got_ref))
        attention = jnp.exp(dot_t(k, q) * scale - log_ref[i : i + 1])
        grad_attention = dot_t(v, g)
        delta = jnp.sum(attention * grad_attention, axis=0, keepdims=True)
        dv = dot(attention.astype(bf16), g)
        grad_scores = (attention * (grad_attention - delta)).astype(bf16)
        dk = dot(grad_scores, q) * scale
        dq = dot(k.T, grad_scores).T * scale
        for ref, grad in ((dq_ref, dq), (dk_ref, dk), (dv_ref, dv)):
            ref[:, i] = grad.astype(bf16).reshape(MP, ROWS, HEAD)
    for s in range(MP):
        for n, ref in enumerate((dq_ref, dk_ref, dv_ref)):
            sent_ref[s, :, n * HEAD : (n + 1) * HEAD] = ref[s].reshape(LOCAL, HEAD)


def feed_back_kernel(
    ids_ref,
    got_ref,
    two_ref,
    one_ref,
    up_ref,
    slope_ref,
    mixed_ref,
    lse_ref,
    map_own,
    map_other,
    gain_feed,
    gain_self,
    *refs,
):
    pieces, self_pieces, refs = refs[: 2 * QUART], refs[2 * QUART : 2 * QUART + 2], refs[10:]
    sent_ref, down_ref, before_ref, branch_ref, grad_self_ref, grad_feed_ref = refs[:6]
    pack_ref, grad_pixel_ref, self_ref, self_sems, full_ref, sems = refs[6:]
    self_copies = fetch_all(ids_ref, self_pieces, self_ref, self_sems, 3)
    copies = fetch_steps(ids_ref, pieces, full_ref, sems)
    core = ids_ref[0]
    grad_hidden = 0.0
    for n in range(3):
        block = slice(n * HEAD, (n + 1) * HEAD)
        grad = jnp.concatenate([got_ref[s, :, block] for s in range(MP)], axis=1)
        arrive(self_copies, n)
        grad_hidden = grad_hidden + times_out(grad, self_ref, n)
    unit, scale = normal(two_ref[...])
    grad, grad_gain = normal_back(unit, scale, gain_self[...], grad_hidden)
    grad_self_ref[...] = grad_gain
    upstream = up_ref[...] + grad
    dy = upstream.astype(bf16)
    branch_ref[...] = dy
    arrive(copies, 1)
    grad_active = times_in(dy, full_ref, 1)
    grad_before = (grad_active * slope_ref[...]).astype(bf16)
    before_ref[...] = grad_before
    arrive(copies, 0)
    grad_hidden = times_out(grad_before, full_ref, 0)
    unit, scale = normal(one_ref[...])
    grad, grad_gain = normal_back(unit, scale, gain_feed[...], grad_hidden)
    grad_feed_ref[...] = grad_gain
    upstream = upstream + grad
    down_ref[...] = upstream
    dy = upstream.astype(bf16)
    pack_ref[...] = jnp.concatenate(
        [before_ref[...], pick(core, branch_ref[...], False), pick(core, dy, False)], axis=1
    )
    grad_mixed = halves(
        core, dot_t(side_by_side(map_own, HALF), dy), dot_t(side_by_side(map_other, HALF), dy), 0
    )[:CP]
    shared = grad_mixed * mixed_ref[...]
    delta = jnp.sum(shared, axis=0, keepdims=True)
    grad_pixel_ref[...] = as_row(jnp.sum(shared, axis=1, keepdims=True))
    sent = with_tail(grad_mixed, split3(lse_ref[...]) + split3(delta)).astype(bf16)
    for s in range(MP):
        sent_ref[s] = sent


def feed_grads_kernel(
    ids_ref,
    hidden_ref,
    active_ref,
    before_ref,
    branch_ref,
    down_ref,
    mixed_ref,
    got_mixed_ref,
    got_state_ref,
    got_ref,
    *refs,
):
    parts, mix_ref, right_ref = refs[:QUART], refs[QUART], refs[QUART + 1]
    core = ids_ref[0]
    own = pick(core, hidden_ref[...], True), pick(core, branch_ref[...], True)
    got = got_state_ref[:, D:], got_ref[:, D : D + WIDE]
    lefts = (before_ref, got_ref), (active_ref, got_state_ref)
    for j in range(2):
        left = stacked(lefts[j][0][...], lefts[j][1][:, :D])
        store_parts(ids_ref, left, stacked(own[j], got[j]), right_ref, parts, j, 2)
    right = stacked(pick(core, down_ref[...], True).astype(bf16), got_ref[:, D + WIDE :])
    mixed = jnp.concatenate([mixed_ref[...], got_mixed_ref[...]], axis=1)
    mix_ref[...] = dot(mixed, right)


def cross_back_kernel(
    ids_ref,
    rows_ref,
    flat_ref,
    items_ref,
    told_ref,
    normed_ref,
    gain_feed,
    gain_self,
    gain_last,
    gain_pixel,
    sent_ref,
    other_ref,
    own_ref,
    grad_ref,
):
    core = ids_ref[0]
    ids = lax.broadcasted_iota(jnp.int32, (CP, 1), 0)
    partials = []
    total, pixel = 0.0, 0.0
    for i, told in enumerate(to_items(told_ref)):
        slots = slice(i * SLOTS, (i + 1) * SLOTS)
        log, delta = join3(told, C + 1), join3(told, C + 4)
        told = jnp.where(ids < C, told, 0.0).astype(bf16)
        asked = items_ref[i]
        attention = jnp.exp(dot(rows_ref[slots], asked) - log)
        grad_attention = dot(rows_ref[slots], told)
        grad_scores = (attention * (grad_attention - delta)).astype(bf16)
        grad_ref[slots] = dot_t(grad_scores, asked) + dot_t(attention.astype(bf16), told)
        partial = dot(flat_ref[:, slots], grad_scores)
        partials.append(partial)
        normed = normed_ref[:, i * ROWS : (i + 1) * ROWS].reshape(NLAT, D)
        total = total + dot(partial.astype(bf16), normed)
        pixel = pixel + jnp.sum(partial * asked.astype(f32), axis=1, keepdims=True)
    store_by_peer(sent_ref, *partials)
    total = total * (D**-0.5)
    pixel = as_row(pixel) + gain_pixel[...]
    pixel = jnp.concatenate([pixel, jnp.zeros((1, D - CP), f32)], axis=1)
    gains = [gain_feed[...], gain_self[...], gain_last[...], pixel]
    ids = lax.broadcasted_iota(jnp.int32, (CP - 256, 1), 0) + 256
    for first, ref in ((True, own_ref), (False, other_ref)):
        half = pick(core, total, first)
        tail = half[256:]
        for n, gain in enumerate(gains):
            row = pick(core, gain, first)
            if not first:
                high = row.astype(bf16).astype(f32)
                tail = jnp.where(ids == C + 4 + n, row - high, tail)
                row = high
            tail = jnp.where(ids == C + n, row, tail)
        total_half = jnp.concatenate([half[:256], tail], axis=0)
        ref[...] = total_half if first else total_half.astype(bf16)


def pixel_back_kernel(pixel_ref, grad_ref, gain_ref, out_ref):
    unit, scale = normal(pixel_ref[...].astype(f32))
    grad, _ = normal_back(unit, scale, gain_ref[...], grad_ref[:, :C])
    out_ref[...] = grad


def latent_back_kernel(
    ids_ref, got_ref, latent_ref, gain_ref, map_own, map_other, down_ref, grad_ref
):
    core = ids_ref[0]
    asked = got_ref[0, :CP].astype(f32)
    for s in range(1, MP):
        asked = asked + got_ref[s, :CP].astype(f32)
    ids = lax.broadcasted_iota(jnp.int32, (CP, 1), 0)
    asked = jnp.where(ids < C, asked * (D**-0.5), 0.0)
    unit, scale = normal(latent_ref[...].astype(f32))
    padded = jnp.concatenate([asked, jnp.zeros((CH - CP, LOCAL), f32)], axis=0)
    grad_normed = 0.0
    for first, ref in ((True, map_own), (False, map_other)):
        part = pick_rows(core, padded, first)
        grad_normed = grad_normed + dot(part.T.astype(bf16), side_by_side(ref, 0))
    grad, _ = normal_back(unit, scale, gain_ref[...], grad_normed)
    grad_ref[...] = down_ref[...] + grad


def total_kernel(partial_ref, got_ref, own_ref, mix_ref, sent_ref):
    got = got_ref[...].astype(f32)
    score = own_ref[...] + got
    ids = lax.broadcasted_iota(jnp.int32, (CP - 256, 1), 0) + 256
    tail = score[256:]
    for n in range(4):
        row = C - 256 + n
        gain = tail[row : row + 1] + got[C + 4 + n : C + 5 + n]
        high = gain.astype(bf16).astype(f32)
        tail = jnp.where(ids == C + n, high, tail)
        tail = jnp.where(ids == C + 4 + n, gain - high, tail)
    rest = jnp.zeros((MP * PART - 2 * CP, WIDE), f32)
    total = jnp.concatenate([mix_ref[...], score[:256], tail, rest], axis=0)
    for s in range(MP):
        sent_ref[s, :CP] = partial_ref[s]
        rows = total[s * PART : (s + 1) * PART].astype(bf16)
        for q in range(QUART):
            start = CP + q * PART
            sent_ref[s, start : start + PART] = rows[:, q * HEAD : (q + 1) * HEAD]


def peer_sum(ref, rows):
    total = ref[0, rows].astype(f32)
    for s in range(1, MP):
        total = total + ref[s, rows].astype(f32)
    return total.astype(bf16)


def spread_kernel(got_ref, sent_ref):
    total = peer_sum(got_ref, slice(CP, CP + SHARE))
    for s in range(MP):
        sent_ref[s] = total


def feed_kernel(got_ref, *refs):
    parts, sent_ref = refs[:QUART], refs[QUART]
    total = peer_sum(got_ref, slice(0, SHARE))
    for s in range(MP):
        sent_ref[s, :SHARE] = total
        for j in range(2):
            value = parts[0][s * 2 + j].astype(f32)
            for part in parts[1:]:
                value = value + part[s * 2 + j].astype(f32)
            start = SHARE + j * HEAD
            sent_ref[s, start : start + HEAD] = value.astype(bf16)


def tiles_out_kernel(got_ref, kept_ref, far_ref, sent_ref):
    total = peer_sum(got_ref, slice(SHARE, SHARE + 2 * HEAD))
    tiles = [(kept_ref[j].astype(f32) + far_ref[j].astype(f32)).astype(bf16) for j in range(3)]
    for s in range(MP):
        sent_ref[s, : 2 * HEAD] = total
        for j, tile in enumerate(tiles):
            sent_ref[s, (2 + j) * HEAD : (3 + j) * HEAD] = tile


def cross_grads_kernel(
    ids_ref,
    own_ref,
    other_ref,
    key_ref,
    query_ref,
    value_own,
    value_other,
    rows_own,
    rows_other,
    map_own,
    map_other,
    gain_latent,
    gain_pixel,
    grad_query_ref,
    grad_key_ref,
    grad_value_ref,
    grad_out_ref,
    *refs,
):
    gain_refs, pad_ref, mix_ref = refs[:5], refs[5], refs[6]
    core, mine = ids_ref[0], ids_ref[2]
    pad_ref[...] = jnp.zeros(pad_ref.shape, f32)
    pad_ref[:C] = key_ref[...].astype(f32)
    key = pad_ref[...].astype(bf16)
    out_rows = [
        jnp.concatenate([ref[s] for s in range(MP)], axis=1) for ref in (rows_own, rows_other)
    ]
    out_rows = halves(core, out_rows[0], out_rows[1], 0)
    block = pl.ds(pl.multiple_of(lax.rem(mine, QUART) * HEAD, HEAD), HEAD)
    score_map = halves(core, side_by_side(map_own, 0), side_by_side(map_other, 0), 0)
    score_map = score_map[:CP].astype(f32)
    ids = lax.broadcasted_iota(jnp.int32, (CP, 1), 0)
    grad_key, grad_value = 0.0, 0.0
    gains, mixes = [], []
    for side, ref in enumerate((own_ref, other_ref)):
        half = core if side == 0 else 1 - core
        span = pl.ds(pl.multiple_of(half * WIDE, WIDE), WIDE)
        whole = jnp.concatenate(
            [
                jnp.concatenate([ref[s, q * PART : (q + 1) * PART] for q in range(QUART)], axis=1)
                for s in range(MP)
            ],
            axis=0,
        )
        mix, score = whole[:CP], whole[CP : 2 * CP]
        mixes.append(mix)
        grad_query_ref[span, :] = dot(score.T, key)
        grad_key = grad_key + dot(score, query_ref[span, :])
        grad_value = grad_value + dot_t(mix, pick(core, out_rows, side == 0))
        tail = score[256:].astype(f32)
        rows = tail[C - 256 : C - 252] + tail[C - 252 : C - 248]
        product = jnp.where(ids < C, score.astype(f32), 0.0) * pick(core, score_map, side == 0)
        first = jnp.sum(product, axis=0, keepdims=True)
        gains.append(jnp.concatenate([first, rows], axis=0))
    grad_key_ref[...] = grad_key[:C]
    grad_value_ref[...] = grad_value[:C]
    gains = halves(core, gains[0], gains[1], 1)
    gain_refs[0][...] = (gains[:1] / gain_latent[...])[0]
    for n in range(1, 4):
        gain_refs[n][...] = gains[n]
    gain_refs[4][...] = (gains[4:5, :C] / gain_pixel[...])[0]
    half = lax.div(mine, QUART)
    mix_ref[0], mix_ref[1] = mixes[0], mixes[1]
    mix = jnp.where(half == core, mix_ref[0, :, block], mix_ref[1, :, block])
    mix = jnp.concatenate([mix, jnp.zeros((CH - CP, HEAD), bf16)], axis=0)
    grad_out_ref[...] = dot(value_own[...].T, pick_rows(core, mix, True)) + dot(
        value_other[...].T, pick_rows(core, mix, False)
    )


def finish_kernel(turned_outs, ids_ref, own_ref, other_ref, *outs):
    core = ids_ref[0]
    for side, ref in enumerate((own_ref, other_ref)):
        half = core if side == 0 else 1 - core
        for q in range(QUART):
            span = pl.ds(pl.multiple_of((half * QUART + q) * HEAD, HEAD), HEAD)
            for j, out in enumerate(outs):
                if j >= 6:
                    rows = slice((j - 6) * HEAD, (j - 5) * HEAD)
                    piece = ref[q, rows].astype(f32) + ref[QUART + q, rows].astype(f32)
                else:
                    rows = slice((2 + j % 3) * HEAD, (3 + j % 3) * HEAD)
                    piece = ref[q + QUART * (j // 3), rows].astype(f32)
                if turned_outs[j]:
                    out[span, :] = piece.T
                else:
                    out[:, span] = piece


def body(
    latents,
    pixels,
    masks,
    cotangent,
    norm_latent,
    norm_pixel,
    norm_feed,
    norm_self,
    norm_last,
    cross_query,
    cross_key,
    cross_value,
    cross_out,
    feed_in,
    feed_out,
    self_query,
    self_key,
    self_value,
    self_out,
    last_in,
    last_out,
):
    core = lax.axis_index("dp") % 2
    mine = lax.axis_index("mp")
    depth = (lax.axis_index("dp") // 2) % QUART
    core_id = jnp.stack([core, depth, mine]).astype(jnp.int32)
    gain_latent, gain_pixel, gain_feed, gain_self, gain_last = (
        g[None, :] for g in (norm_latent, norm_pixel, norm_feed, norm_self, norm_last)
    )
    latent_rows = latents.reshape(LOCAL, D)
    pixel_rows = pixels.reshape(ITEMS * SLOTS, C)
    cotangent_rows = cotangent.reshape(LOCAL, D)
    row_f32, row_bf16 = ((LOCAL, D), f32), ((LOCAL, D), bf16)
    gain_row = ((1, D), f32)

    def come(x, step):
        return lax.ppermute(x, "dp", DEPTH[QUART - step])

    map_shape = ((MP, CH, HEAD), bf16)
    sent, tile = run(
        map_start_kernel,
        2,
        [((MP, CH + 2 * HEAD + ROWS, HEAD), bf16), ((6, HEAD, HEAD), bf16)],
        core_id,
        cross_key,
        cross_query,
        cross_value,
        feed_in,
        feed_out,
        self_out,
        last_in,
        last_out,
        self_query,
        self_key,
        self_value,
        cross_out,
        scratch=[pltpu.VMEM((2, CH, HEAD), f32)],
    )
    pixel_in, pixel_flat = run(
        pixel_kernel,
        2,
        [((ITEMS * SLOTS, CP), bf16), ((CP, ITEMS * SLOTS), bf16)],
        pixel_rows,
        masks,
        gain_pixel,
        scratch=[pltpu.VMEM((ITEMS * SLOTS, 384), f32)],
        hot_outs=(),
    )
    packs = lax.all_gather(tile, "mp")
    got, (pixel_in, pixel_flat) = after(exchange(sent), pixel_in, pixel_flat)

    def along(x):
        return lax.all_gather(x, "dp", axis_index_groups=ALONG_Z)

    sent, value_half, feed_pack, out_rows = run(
        map_sum_kernel,
        1,
        [
            map_shape,
            ((HALF, D), bf16),
            ((MP, 2, HEAD, HEAD), bf16),
            ((MP, ROWS, HEAD), bf16),
        ],
        got,
        cross_out,
        hot=(0,),
    )
    feed_pieces = [feed_pack, None, come(feed_pack, 2), None]
    map_own, (packs, feed_pieces[2]) = after(exchange(sent), packs, feed_pieces[2])
    map_other = core_swap(map_own)
    packs = along(packs)
    peer_shape = ((MP, CP, HEAD), bf16)
    sent, normed = run(
        asked_kernel,
        1,
        [peer_shape, row_bf16],
        core_id,
        map_own,
        map_other,
        latent_rows,
        gain_latent,
        hot=(1, 2),
        hot_outs=(),
    )
    feed_pieces[1], feed_pieces[3] = come(feed_pack, 1), come(feed_pack, 3)
    asked_all, (feed_pieces[1], feed_pieces[3]) = after(
        exchange(sent), feed_pieces[1], feed_pieces[3]
    )
    feed_pieces = feed_pieces + [core_swap(v) for v in feed_pieces]
    sent, asked_items = run(
        cross_kernel,
        3,
        [peer_shape, ((ITEMS, CP, NLAT), bf16)],
        pixel_in,
        pixel_flat,
        asked_all,
        hot=(2,),
        hot_outs=(),
    )
    sent, mixed, lse, state_one, feed_hidden, feed_active, feed_slope, state_two, mixed_low, state_pack = run(
        state_kernel,
        4,
        [
            ((MP, LOCAL, D), bf16),
            ((CP, LOCAL), f32),
            ((1, LOCAL), f32),
            row_f32,
            row_bf16,
            row_bf16,
            row_f32,
            row_f32,
            ((CP, LOCAL), bf16),
            ((LOCAL, D + WIDE), bf16),
        ],
        core_id,
        exchange(sent),
        latent_rows,
        map_own,
        map_other,
        gain_feed,
        gain_self,
        *feed_pieces,
        scratch=full_shape(2),
        far=range(7, 15),
        hot=(1,),
        hot_outs=(),
    )

    hidden_all, (packs, normed, got_mixed, got_state) = after(
        exchange(sent), packs, normed, core_swap(mixed_low), core_swap(state_pack)
    )
    other_packs = core_swap(packs)
    normed_all = lax.all_gather(normed, "mp")
    heads_shape = ((MP, ITEMS, ROWS, HEAD), bf16)
    sent, queries, keys, values, logs = run(
        heads_kernel,
        3,
        [heads_shape] * 4 + [((ITEMS, NLAT), f32)],
        hidden_all,
        self_query,
        self_key,
        self_value,
        hot=(0,),
    )
    got = exchange(sent)
    sent, up, result, heads_out, last_hidden, last_active, last_before, grad_last, back_pack = run(
        last_kernel,
        6,
        [
            ((MP, LOCAL, HEAD), bf16),
            row_f32,
            row_bf16,
            row_bf16,
            row_bf16,
            row_bf16,
            row_bf16,
            gain_row,
            ((LOCAL, 3 * (D + WIDE)), bf16),
        ],
        core_id,
        got.reshape(MP, LOCAL, HEAD),
        state_two,
        gain_last,
        cotangent_rows,
        packs,
        other_packs,
        scratch=full_shape(3) + [pltpu.VMEM((LOCAL, D), f32)],
        pinned=(5, 6),
        hot=(1,),
    )

    def tiles(count):
        return ((QUART, count, HEAD, HEAD), bf16)

    def along_sum(x):
        count = x.shape[1]
        x = x.reshape(QUART * count * HEAD, HEAD)
        x = lax.psum_scatter(x, "dp", axis_index_groups=ALONG_Z, tiled=True)
        return x.reshape(count, HEAD, HEAD)

    (last_own,) = run(
        last_grads_kernel,
        3,
        [tiles(3 * MP)],
        core_id,
        heads_out,
        up,
        last_hidden,
        last_active,
        last_before,
        cotangent_rows,
        core_swap(back_pack),
        hot=(7,),
        hot_outs=(),
    )
    grad_heads, (last_own,) = after(exchange(sent), last_own)

    def give(parts):
        return [lax.ppermute(parts[step], "dp", DEPTH[step]) for step in (1, 2, 3)]

    def all_of(first, *others):
        total = first.astype(f32)
        for other in others:
            total = total + other.astype(f32)
        return total.astype(bf16)

    grad_heads = grad_heads.reshape(MP, ITEMS, ROWS, HEAD)
    sent, dq, dk, dv = run(
        heads_back_kernel,
        4,
        [((MP, LOCAL, 3 * HEAD), bf16)] + [heads_shape] * 3,
        grad_heads,
        queries,
        keys,
        values,
        logs,
        hot=(0,),
    )
    last_own, (normed_all, _) = after(last_own, normed_all, dq)
    last_sum = along_sum(last_own)
    self_own, self_other = run(
        heads_grads_kernel, 2, [tiles(3)] * 2, core_id, hidden_all, dq, dk, dv, hot_outs=()
    )
    self_parts = (self_own.astype(f32) + core_swap(self_other).astype(f32)).astype(bf16)
    got, (self_parts,) = after(exchange(sent), self_parts)
    sent, down, feed_before, feed_branch, grad_self, grad_feed, feed_back, grad_pixel = run(
        feed_back_kernel,
        4,
        [peer_shape, row_f32, row_bf16, row_bf16, gain_row, gain_row, ((LOCAL, 2 * D), bf16), ((1, CP), f32)],
        core_id,
        got,
        state_two,
        state_one,
        up,
        feed_slope,
        mixed,
        lse,
        map_own,
        map_other,
        gain_feed,
        gain_self,
        *feed_pieces,
        packs,
        other_packs,
        scratch=full_shape(3) + full_shape(2),
        far=range(12, 20),
        pinned=(20, 21),
        hot=(1,),
    )
    *feed_parts, mix_own = run(
        feed_grads_kernel,
        2,
        [((2 * MP, HEAD, HEAD), bf16)] * QUART + [((CP, WIDE), f32)],
        core_id,
        feed_hidden,
        feed_active,
        feed_before,
        feed_branch,
        down,
        mixed_low,
        got_mixed,
        got_state,
        core_swap(feed_back),
        scratch=[pltpu.VMEM((2, 2 * LOCAL, WIDE), bf16)],
        loose=(7, 8),
        hot=(9,),
        hot_outs=(),
    )
    feed_got = give(feed_parts)
    last_sum, _ = after(last_sum, feed_parts[0])
    self_got = give(self_parts)
    self_sum = all_of(self_parts[0], *self_got)
    told_all, (self_sum, *_) = after(exchange(sent), self_sum, *feed_parts)
    last_rows = last_sum.reshape(MP * 3 * HEAD, HEAD)
    last_piece = lax.psum_scatter(last_rows, "mp", tiled=True).reshape(3, HEAD, HEAD)
    partial, other, own, grad_pixel_in = run(
        cross_back_kernel,
        4,
        [peer_shape, ((CP, WIDE), bf16), ((CP, WIDE), f32), ((ITEMS * SLOTS, CP), f32)],
        core_id,
        pixel_in,
        pixel_flat,
        asked_items,
        told_all,
        normed_all,
        grad_feed,
        grad_self,
        grad_last,
        grad_pixel,
        hot=(4,),
        hot_outs=(0, 1, 2),
    )
    other, (feed_got[0], feed_got[2]) = after(core_swap(other), feed_got[0], feed_got[2])
    (sent,) = run(
        total_kernel,
        1,
        [((MP, CP + SHARE, HEAD), bf16)],
        partial,
        other,
        own,
        mix_own,
        hot=(0, 1, 2),
    )
    (grad_pixels,) = run(
        pixel_back_kernel,
        2,
        [((ITEMS * SLOTS, C), f32)],
        pixel_rows,
        grad_pixel_in,
        gain_pixel,
        hot_outs=(),
    )
    grad_pixels = grad_pixels.reshape(ITEMS, SLOTS, C).transpose(2, 0, 1)
    got, (grad_pixels, feed_got[1]) = after(exchange(sent), grad_pixels, feed_got[1])
    share_shape = ((MP, SHARE, HEAD), bf16)
    (sent,) = run(spread_kernel, 1, [share_shape], got, hot=(0,))
    (grad_latents,) = run(
        latent_back_kernel,
        2,
        [row_f32],
        core_id,
        got,
        latent_rows,
        gain_latent,
        map_own,
        map_other,
        down,
        hot=(1,),
        hot_outs=(),
    )
    got, (grad_latents,) = after(grouped(sent, "dp", COPIES), grad_latents)
    (sent,) = run(
        feed_kernel,
        1,
        [((MP, SHARE + 2 * HEAD, HEAD), bf16)],
        got,
        feed_parts[0],
        *feed_got,
        hot=(0,),
        loose=(2, 3, 4),
    )
    row = lax.axis_index("dp") // 8
    kept = jnp.where(row == 0, last_piece, self_sum)
    far = lax.ppermute(jnp.where(row == 0, self_sum, last_piece), "dp", FAR)
    own, (kept, far) = after(exchange(sent), kept, far)
    (sent,) = run(
        tiles_out_kernel,
        1,
        [((MP, 5 * HEAD, HEAD), bf16)],
        own,
        kept,
        far,
        hot=(0,),
        hot_outs=(),
        loose=(1, 2),
    )
    other = core_swap(own)
    row_out, key_out = ((D, HEAD), f32), ((C, HEAD), f32)
    cross = run(
        cross_grads_kernel,
        3,
        [row_out, key_out, key_out, row_out] + [((D,), f32)] * 4 + [((C,), f32)],
        core_id,
        own,
        other,
        cross_key,
        cross_query,
        value_half,
        core_swap(value_half),
        out_rows,
        core_swap(out_rows),
        map_own,
        map_other,
        gain_latent,
        gain_pixel,
        scratch=[pltpu.VMEM((CP, HEAD), f32), pltpu.VMEM((2, CP, WIDE), bf16)],
        hot=(1, 2),
        loose=(6, 8),
        hot_outs=(),
    )
    own, cross = after(grouped(sent, "dp", COPIES), *cross)
    grad_cross_query, grad_cross_key, grad_cross_value, grad_cross_out, *gains = cross
    flips = (False, True, False, True, True, True, True, False)
    finished = run(
        functools.partial(finish_kernel, flips),
        2,
        [((D, HEAD) if flip else (HEAD, D), f32) for flip in flips],
        core_id,
        own,
        core_swap(own),
        hot=(1, 2),
        hot_outs=(),
    )
    grad_self_out, grad_last_in, grad_last_out, grad_sq, grad_sk, grad_sv = finished[:6]
    grad_feed_in, grad_feed_out = finished[6:]
    shape = (ITEMS, ROWS, D)
    return (
        result.reshape(shape),
        grad_latents.reshape(shape),
        grad_pixels.transpose(1, 2, 0),
        gains[0],
        gains[4],
        gains[1],
        gains[2],
        gains[3],
        grad_cross_query,
        grad_cross_key,
        grad_cross_value,
        grad_cross_out,
        grad_feed_in,
        grad_feed_out,
        grad_sq,
        grad_sk,
        grad_sv,
        grad_self_out,
        grad_last_in,
        grad_last_out,
    )


def solution(mesh):
    rows = P("dp", "mp", None)
    columns = P(None, "mp")
    depth = P("mp", None)
    return jax.shard_map(
        body,
        mesh=mesh,
        in_specs=(rows, rows, P("dp", "mp"), rows)
        + (P(),) * 5
        + (columns,) * 5
        + (depth,)
        + (columns,) * 3
        + (depth, columns, depth),
        out_specs=(rows,) * 3
        + (P(),) * 5
        + (columns,) * 5
        + (depth,)
        + (columns,) * 3
        + (depth, columns, depth),
        check_vma=False,
    )
```

```python
import functools

import jax
import jax.numpy as jnp
from jax import lax
from jax.experimental import pallas as pl
from jax.experimental.pallas import tpu as pltpu
from jax.sharding import PartitionSpec as P

D = 1024
C = 261
CP = 272
CH = 288
HALF = 144
HEADS = 8
HEAD = 128
MP = 8
ITEMS = 2
ROWS = 64
LOCAL = ITEMS * ROWS
SLOTS = 512
NLAT = 512
WIDE = 512
MEMBERS = 64
PART = 80
QUART = 4
SHARE = QUART * PART
LIMIT = 24 << 20
EPS = 1e-05
MASKED = -1e30
GELU_A = 0.044715
GELU_K = 0.7978845608028654

bf16 = jnp.bfloat16
f32 = jnp.float32

SWAP = [(i, i ^ 1) for i in range(16)]
CHIPS = [
    [(d * 2 + core) * MP + m for d in range(8) for m in range(MP)] for core in range(2)
]
DEPTH = [
    [((y * 4 + z) * 2 + c, (y * 4 + (z + k) % 4) * 2 + c) for y in range(2) for z in range(4) for c in range(2)]
    for k in range(4)
]
FAR = [(i, i ^ 8) for i in range(16)]
NEAR = [(i, i ^ 4) for i in range(MP)]
OPPOSITE = [(i, i ^ 68) for i in range(128)]
ACROSS = [[(y * 4 + x, y * 4 + (x + k) % 4) for y in range(2) for x in range(4)] for k in range(4)]
COPIES = [[d * 2 + core for d in range(8)] for core in range(2)]
ALONG_Z = [[(y * 4 + z) * 2 + core for z in range(4)] for y in range(2) for core in range(2)]


def dot(a, b):
    return lax.dot_general(a, b, (((1,), (0,)), ((), ())), preferred_element_type=f32)


def dot_t(a, b):
    return lax.dot_general(a, b, (((1,), (1,)), ((), ())), preferred_element_type=f32)


def t_dot(a, b):
    return dot(a.T, b)


def cost(micros):
    return pl.CostEstimate(
        flops=int(micros * 1e7), bytes_accessed=int(micros * 2e4), transcendentals=0
    )


class Arriving:
    def __init__(self, ref, copy):
        self.ref, self.copy, self.shape = ref, copy, ref.shape

    def settle(self):
        if self.copy is not None:
            self.copy.wait()
        self.copy = None

    def __getitem__(self, index):
        self.settle()
        return self.ref[index]


class Leaving:
    def __init__(self, ref, copy):
        self.ref, self.copy, self.shape, self.left = ref, copy, ref.shape, False

    def leave(self):
        if not self.left:
            self.copy.start()
        self.left = True

    def __getitem__(self, index):
        return self.ref[index]

    def __setitem__(self, index, value):
        self.ref[index] = value
        if index is Ellipsis:
            self.leave()


def run(kernel, micros, outs, *args, scratch=(), far=(), pinned=(), loose=(), hot=(), hot_outs=(0,)):
    specs, homes = [], []
    for n, a in enumerate(args):
        if jnp.ndim(a) == 1 and a.dtype == jnp.int32:
            space = pltpu.SMEM
        elif n in hot:
            space = pltpu.VMEM
        elif n in far:
            space = pl.ANY
        elif n in pinned:
            space = pltpu.HBM
        else:
            space = pl.ANY if n in loose else pltpu.HBM
            homes.append(n)
        specs.append(pl.BlockSpec(memory_space=space))
    out_homes = [n for n in range(len(outs)) if n not in hot_outs]
    buffers = [pltpu.VMEM(args[n].shape, args[n].dtype) for n in homes]
    buffers += [pltpu.VMEM(*outs[n]) for n in out_homes]

    def wrapped(*refs):
        refs = list(refs)
        sems, refs = refs[-1], refs[:-1]
        given, refs = refs[: len(args)], refs[len(args) :]
        made, refs = refs[: len(outs)], refs[len(outs) :]
        own, refs = refs[: len(scratch)], refs[len(scratch) :]
        for k, n in enumerate(homes):
            copy = pltpu.make_async_copy(given[n], refs[k], sems.at[k])
            copy.start()
            given[n] = Arriving(refs[k], copy)
        for k, n in enumerate(out_homes, len(homes)):
            made[n] = Leaving(refs[k], pltpu.make_async_copy(refs[k], made[n], sems.at[k]))
        kernel(*given, *made, *own)
        for n in homes:
            given[n].settle()
        for n in out_homes:
            made[n].leave()
        for n in out_homes:
            made[n].copy.wait()

    return pl.pallas_call(
        wrapped,
        out_shape=[
            jax.ShapeDtypeStruct(*out) if n in hot_outs else pltpu.HBM(*out)
            for n, out in enumerate(outs)
        ],
        in_specs=specs,
        out_specs=[
            pl.BlockSpec(memory_space=pltpu.VMEM if n in hot_outs else pltpu.HBM)
            for n in range(len(outs))
        ],
        scratch_shapes=[
            *scratch,
            *buffers,
            pltpu.SemaphoreType.DMA((max(1, len(buffers)),)),
        ],
        compiler_params=pltpu.CompilerParams(vmem_limit_bytes=LIMIT),
        cost_estimate=cost(micros),
    )(
        *(
            pltpu.with_memory_space_constraint(a, pltpu.HBM)
            if n in pinned or (n in homes and n not in loose)
            else a
            for n, a in enumerate(args)
        )
    )


def after(x, *waits):
    x, *waits = lax.optimization_barrier((x, *waits))
    return x, waits


def core_swap(x):
    return lax.ppermute(x, "dp", SWAP)


def exchange(x):
    return lax.all_to_all(x, "mp", 0, 0, tiled=True)


def to_all(x):
    return exchange(jnp.broadcast_to(x[None], (MP,) + x.shape))


def grouped(x, axes, groups):
    return lax.all_to_all(x, axes, 0, 0, tiled=True, axis_index_groups=groups)


def grouped_all(x, axes, groups):
    return grouped(jnp.broadcast_to(x[None], (len(groups[0]),) + x.shape), axes, groups)


def added(x):
    return jnp.sum(x.astype(f32), axis=0).astype(bf16)


def normal(v):
    center = v - jnp.mean(v, axis=-1, keepdims=True)
    spread = jnp.mean(center * center, axis=-1, keepdims=True)
    scale = lax.rsqrt(spread + EPS)
    return center * scale, scale


def normal_back(unit, scale, gain, upstream):
    grad_gain = jnp.sum(upstream * unit, axis=0, keepdims=True)
    grad_unit = upstream * gain
    inner = jnp.mean(grad_unit * unit, axis=-1, keepdims=True)
    grad = scale * (grad_unit - jnp.mean(grad_unit, axis=-1, keepdims=True) - unit * inner)
    return grad, grad_gain


def gelu_parts(v):
    square = v * v
    t = jnp.tanh(GELU_K * v * (1.0 + GELU_A * square))
    value = 0.5 * v * (1.0 + t)
    slope = 0.5 * (1.0 + t) + 0.5 * v * (1.0 - t * t) * GELU_K * (1.0 + 3.0 * GELU_A * square)
    return value, slope


def split3(v):
    high = v.astype(bf16).astype(f32)
    middle = (v - high).astype(bf16).astype(f32)
    return [high, middle, v - high - middle]


def join3(rows, start):
    return rows[start : start + 1] + rows[start + 1 : start + 2] + rows[start + 2 : start + 3]


def halves(core, own, other, axis):
    first = jnp.where(core == 0, own, other)
    second = jnp.where(core == 0, other, own)
    return jnp.concatenate([first, second], axis=axis)


def pick(core, v, own):
    take_low = core == 0 if own else core != 0
    return jnp.where(take_low, v[:, :WIDE], v[:, WIDE:])


def pick_rows(core, v, own):
    take_low = core == 0 if own else core != 0
    return jnp.where(take_low, v[:HALF], v[HALF:])


def full_shape(count):
    return [
        pltpu.VMEM((count, MP, HEAD, D), bf16),
        pltpu.SemaphoreType.DMA((count, 2, QUART)),
    ]


def fetch_steps(ids_ref, pieces, full_ref, sems):
    core, depth = ids_ref[0], ids_ref[1]
    copies = []
    for j in range(full_ref.shape[0]):
        for n, ref in enumerate(pieces):
            side, step = n // QUART, n % QUART
            half = core if side == 0 else 1 - core
            block = half * QUART + lax.rem(depth + step, QUART)
            columns = pl.ds(pl.multiple_of(block * HEAD, HEAD), HEAD)
            copies.append(
                pltpu.make_async_copy(
                    ref.at[:, j], full_ref.at[j, :, :, columns], sems.at[j, side, step]
                )
            )
            copies[-1].start()
    return copies


def fetch_all(ids_ref, pieces, full_ref, sems, base):
    core = ids_ref[0]
    copies = []
    for j in range(full_ref.shape[0]):
        for side, ref in enumerate(pieces):
            half = core if side == 0 else 1 - core
            for q in range(QUART):
                columns = pl.ds(pl.multiple_of((half * QUART + q) * HEAD, HEAD), HEAD)
                copies.append(
                    pltpu.make_async_copy(
                        ref.at[q, :, base + j], full_ref.at[j, :, :, columns], sems.at[j, side, q]
                    )
                )
                copies[-1].start()
    return copies


def arrive(copies, j):
    for copy in copies[j * 2 * QUART : (j + 1) * 2 * QUART]:
        copy.wait()


def matrix(full_ref, j):
    return full_ref[j].reshape(D, D)


def times_in(x, full_ref, j):
    return dot_t(x, matrix(full_ref, j))


def times_out(x, full_ref, j):
    return dot(x, matrix(full_ref, j))


def store_blocks(ids_ref, grad, own_ref, other_ref, place):
    core, depth = ids_ref[0], ids_ref[1]
    for first, ref in ((True, own_ref), (False, other_ref)):
        half = pick(core, grad, first).astype(bf16)
        for q in range(QUART):
            step = lax.rem(q + QUART - depth, QUART)
            ref[step, place] = half[:, q * HEAD : (q + 1) * HEAD]


def stacked(own, got):
    return jnp.concatenate([own, got], axis=0)


def store_grad(left, right, own_ref, j, count):
    flipped = left.T
    for s in range(MP):
        grad = dot(flipped[s * HEAD : (s + 1) * HEAD], right).astype(bf16)
        for q in range(QUART):
            own_ref[q, s * count + j] = grad[:, q * HEAD : (q + 1) * HEAD]


def store_parts(ids_ref, left, right, right_ref, parts, j, count):
    right_ref[j] = right
    blocks = []
    for step in range(QUART):
        columns = pl.multiple_of(lax.rem(ids_ref[1] + step, QUART) * HEAD, HEAD)
        blocks.append(right_ref[j, :, pl.ds(columns, HEAD)])
    right = jnp.concatenate(blocks, axis=1)
    flipped = left.T
    for s in range(MP):
        grad = dot(flipped[s * HEAD : (s + 1) * HEAD], right).astype(bf16)
        for step, part in enumerate(parts):
            part[s * count + j] = grad[:, step * HEAD : (step + 1) * HEAD]


def as_row(column):
    return jnp.broadcast_to(column, (column.shape[0], HEAD)).T[:1]


def side_by_side(ref, start):
    return jnp.concatenate([ref[s, start : start + HALF] for s in range(MP)], axis=1)


def lane_halves():
    return lax.broadcasted_iota(jnp.int32, (1, HEAD), 1) < ROWS


def turned(x):
    return pltpu.roll(x, ROWS, 1)


def to_items(ref):
    low = lane_halves()
    items = [[], []]
    for p in range(0, MP, 2):
        a, b = ref[p].astype(f32), ref[p + 1].astype(f32)
        items[0].append(jnp.where(low, a, turned(b)))
        items[1].append(jnp.where(low, turned(a), b))
    return [jnp.concatenate(v, axis=1) for v in items]


def store_by_peer(ref, first, second):
    low = lane_halves()
    for p in range(0, MP, 2):
        x, y = (v[:, p * ROWS : (p + 2) * ROWS] for v in (first, second))
        ref[p] = jnp.where(low, x, turned(y)).astype(bf16)
        ref[p + 1] = jnp.where(low, turned(x), y).astype(bf16)


def with_tail(x, rows):
    ids = lax.broadcasted_iota(jnp.int32, (CP - 256, 1), 0) + 256
    tail = jnp.where(ids < C, x[256:CP], 0.0)
    for offset, row in enumerate(rows):
        tail = jnp.where(ids == C + 1 + offset, row, tail)
    return jnp.concatenate([x[:256], tail], axis=0)


def map_start_kernel(
    ids_ref,
    key_ref,
    query_ref,
    value_ref,
    feed_in_ref,
    feed_out_ref,
    self_out_ref,
    last_in_ref,
    last_out_ref,
    wq_ref,
    wk_ref,
    wv_ref,
    out_ref,
    sent_ref,
    tiles_ref,
    pad_ref,
):
    core = ids_ref[0]
    span = pl.ds(pl.multiple_of((core * QUART + ids_ref[1]) * HEAD, HEAD), HEAD)
    tiles_ref[0] = self_out_ref[:, span]
    tiles_ref[1] = last_in_ref[span, :].T
    tiles_ref[2] = last_out_ref[:, span]
    for n, ref in enumerate((wq_ref, wk_ref, wv_ref)):
        tiles_ref[3 + n] = ref[span, :].T
    tiles_ref.leave()
    tiles = [feed_in_ref[span, :].T, feed_out_ref[:, span]]
    pad_ref[...] = jnp.zeros(pad_ref.shape, f32)
    pad_ref[0, :C] = key_ref[...].astype(f32)
    pad_ref[1, :C] = value_ref[...].astype(f32)
    key = jnp.where(core == 0, pad_ref[0, :HALF], pad_ref[0, HALF:]).astype(bf16)
    value = jnp.where(core == 0, pad_ref[1, :HALF], pad_ref[1, HALF:]).astype(bf16)
    for s in range(MP):
        block = query_ref[s * HEAD : (s + 1) * HEAD]
        sent_ref[s, :HALF] = dot_t(key, block).astype(bf16)
        sent_ref[s, HALF:CH] = value
        for j, tile in enumerate(tiles):
            sent_ref[s, CH + j * HEAD : CH + (j + 1) * HEAD] = tile
        rows = pl.ds(pl.multiple_of(s * HEAD + core * ROWS, ROWS), ROWS)
        sent_ref[s, CH + 2 * HEAD :] = out_ref[rows, :]


def map_sum_kernel(got_ref, out_ref, sent_ref, value_ref, feed_ref, rows_ref):
    for s in range(MP):
        for j in range(2):
            feed_ref[s, j] = got_ref[s, CH + j * HEAD : CH + (j + 1) * HEAD]
        rows_ref[s] = got_ref[s, CH + 2 * HEAD :]
    feed_ref.leave()
    score = got_ref[0, :HALF].astype(f32)
    for s in range(1, MP):
        score = score + got_ref[s, :HALF].astype(f32)
    value = side_by_side(got_ref, HALF)
    value_ref[...] = value
    score = score.astype(bf16)
    mix = dot(value, out_ref[...]).astype(bf16)
    for s in range(MP):
        sent_ref[s, :HALF] = score
        sent_ref[s, HALF:] = mix


def asked_kernel(core_ref, own_ref, other_ref, latent_ref, gain_ref, sent_ref, normed_ref):
    core = core_ref[0]
    unit, _ = normal(latent_ref[...].astype(f32))
    normed = (unit * gain_ref[...]).astype(bf16)
    normed_ref[...] = normed
    asked = halves(
        core, dot_t(side_by_side(own_ref, 0), normed), dot_t(side_by_side(other_ref, 0), normed), 0
    )
    ids = lax.broadcasted_iota(jnp.int32, (CP, 1), 0)
    asked = jnp.where(ids < C, asked[:CP] * (D**-0.5), jnp.where(ids == C, 1.0, 0.0))
    asked = asked.astype(bf16)
    for s in range(MP):
        sent_ref[s] = asked


def pixel_kernel(pixel_ref, mask_ref, gain_ref, rows_ref, flat_ref, pad_ref):
    unit, _ = normal(pixel_ref[...].astype(f32))
    pad_ref[...] = jnp.zeros(pad_ref.shape, f32)
    pad_ref[:, :C] = unit * gain_ref[...]
    flat = pad_ref[...].T[:CP]
    bias = jnp.where(mask_ref[...] > 0, 0.0, MASKED)
    bias = jnp.concatenate([bias[i : i + 1] for i in range(ITEMS)], axis=1)
    ids = lax.broadcasted_iota(jnp.int32, (CP, 1), 0)
    flat = jnp.where(ids == C, bias, flat)
    flat_ref[...] = flat.astype(bf16)
    lanes = lax.broadcasted_iota(jnp.int32, (1, CP), 1)
    rows_ref[...] = flat.T.astype(bf16)


def cross_kernel(rows_ref, flat_ref, asked_ref, sent_ref, items_ref):
    sums = []
    for i, asked in enumerate(to_items(asked_ref)):
        asked = asked.astype(bf16)
        items_ref[i] = asked
        slots = slice(i * SLOTS, (i + 1) * SLOTS)
        scores = dot(rows_ref[slots], asked)
        peak = jnp.max(scores, axis=0, keepdims=True)
        weight = jnp.exp(scores - peak)
        total = jnp.sum(weight, axis=0, keepdims=True)
        mixed = dot(flat_ref[:, slots], weight.astype(bf16))
        sums.append(with_tail(mixed, split3(peak) + split3(total)))
    store_by_peer(sent_ref, *sums)


def feed_forward(stream, gain, copies, full_ref, j, hidden_ref, active_ref, slope_ref):
    unit, _ = normal(stream)
    hidden = (unit * gain).astype(bf16)
    hidden_ref[...] = hidden
    arrive(copies, j)
    active, slope = gelu_parts(times_in(hidden, full_ref, j))
    active = active.astype(bf16)
    active_ref[...] = active
    slope_ref[...] = slope
    arrive(copies, j + 1)
    return times_out(active, full_ref, j + 1)


def state_kernel(ids_ref, got_ref, latent_ref, map_own, map_other, gain_feed, gain_self, *refs):
    pieces, refs = refs[: 2 * QUART], refs[2 * QUART :]
    sent_ref, mixed_ref, lse_ref, one_ref, hidden_ref, active_ref, slope_ref, two_ref = refs[:8]
    low_ref, pack_ref, full_ref, sems = refs[8:]
    copies = fetch_steps(ids_ref, pieces, full_ref, sems)
    core = ids_ref[0]
    got = [got_ref[s].astype(f32) for s in range(MP)]
    peaks = [join3(g, C + 1) for g in got]
    totals = [join3(g, C + 4) for g in got]
    peak = peaks[0]
    for s in range(1, MP):
        peak = jnp.maximum(peak, peaks[s])
    shares = [jnp.exp(p - peak) for p in peaks]
    total = shares[0] * totals[0]
    mixed = shares[0] * got[0]
    for s in range(1, MP):
        total = total + shares[s] * totals[s]
        mixed = mixed + shares[s] * got[s]
    ids = lax.broadcasted_iota(jnp.int32, (CP, 1), 0)
    mixed = jnp.where(ids < C, mixed / total, 0.0)
    lse_ref[...] = peak + jnp.log(total)
    mixed_ref[...] = mixed
    low_ref[...] = mixed.astype(bf16)
    mixed = jnp.concatenate([mixed, jnp.zeros((CH - CP, LOCAL), f32)], axis=0)
    one = latent_ref[...].astype(f32)
    for first, ref in ((True, map_own), (False, map_other)):
        part = pick_rows(core, mixed, first)
        one = one + dot(part.T.astype(bf16), side_by_side(ref, HALF))
    one_ref[...] = one
    two = one + feed_forward(
        one, gain_feed[...], copies, full_ref, 0, hidden_ref, active_ref, slope_ref
    )
    two_ref[...] = two
    pack_ref[...] = jnp.concatenate([active_ref[...], pick(core, hidden_ref[...], False)], axis=1)
    unit, _ = normal(two)
    hidden = (unit * gain_self[...]).astype(bf16)
    for s in range(MP):
        sent_ref[s] = hidden


def heads_kernel(all_ref, wq_ref, wk_ref, wv_ref, sent_ref, q_ref, k_ref, v_ref, log_ref):
    weight = jnp.concatenate([wq_ref[...], wk_ref[...], wv_ref[...]], axis=1)
    for s in range(MP):
        rows = dot(all_ref[s], weight).astype(bf16)
        for n, ref in enumerate((q_ref, k_ref, v_ref)):
            ref[s] = rows[:, n * HEAD : (n + 1) * HEAD].reshape(ITEMS, ROWS, HEAD)
    for i in range(ITEMS):
        q, k, v = (ref[:, i].reshape(NLAT, HEAD) for ref in (q_ref, k_ref, v_ref))
        scores = dot_t(k, q) * HEAD**-0.5
        top = jnp.max(scores, axis=0, keepdims=True)
        log = top + jnp.log(jnp.sum(jnp.exp(scores - top), axis=0, keepdims=True))
        log_ref[i : i + 1] = log
        attention = jnp.exp(scores - log).astype(bf16)
        out = dot(v.T, attention).T.astype(bf16)
        sent_ref[:, i] = out.reshape(MP, ROWS, HEAD)


def last_kernel(ids_ref, got_ref, two_ref, gain_ref, cotangent_ref, *refs):
    pieces, refs = refs[:2], refs[2:]
    sent_ref, up_ref, result_ref, heads_ref, hidden_ref, active_ref, before_ref = refs[:7]
    grad_gain_ref, pack_ref, full_ref, sems, slope_ref = refs[7:]
    core = ids_ref[0]
    copies = fetch_all(ids_ref, pieces, full_ref, sems, 0)
    heads = jnp.concatenate([got_ref[s] for s in range(MP)], axis=1)
    heads_ref[...] = heads
    arrive(copies, 0)
    three = two_ref[...] + times_out(heads, full_ref, 0)
    branch = feed_forward(
        three, gain_ref[...], copies, full_ref, 1, hidden_ref, active_ref, slope_ref
    )
    result_ref[...] = (three + branch).astype(bf16)
    upstream = cotangent_ref[...]
    grad_active = times_in(upstream, full_ref, 2)
    grad_before = (grad_active * slope_ref[...]).astype(bf16)
    before_ref[...] = grad_before
    grad_hidden = times_out(grad_before, full_ref, 1)
    unit, scale = normal(three)
    grad, grad_gain = normal_back(unit, scale, gain_ref[...], grad_hidden)
    grad_gain_ref[...] = grad_gain
    up = upstream.astype(f32) + grad
    up_ref[...] = up
    dy = up.astype(bf16)
    grad_heads = times_in(dy, full_ref, 0).astype(bf16)
    for s in range(MP):
        sent_ref[s] = grad_heads[:, s * HEAD : (s + 1) * HEAD]
    rights = [pick(core, v, False) for v in (dy, hidden_ref[...], upstream)]
    lefts = [heads, grad_before, active_ref[...]]
    pack_ref[...] = jnp.concatenate(lefts + rights, axis=1)


def last_grads_kernel(
    ids_ref, heads_ref, up_ref, hidden_ref, active_ref, before_ref, upstream_ref, got_ref, own
):
    core = ids_ref[0]
    lefts = heads_ref, before_ref, active_ref
    rights = up_ref, hidden_ref, upstream_ref
    for j in range(3):
        got_left = got_ref[:, j * D : (j + 1) * D]
        got_right = got_ref[:, 3 * D + j * WIDE : 3 * D + (j + 1) * WIDE]
        right = pick(core, rights[j][...], True).astype(bf16)
        store_grad(stacked(lefts[j][...], got_left), stacked(right, got_right), own, j, 3)


def heads_grads_kernel(ids_ref, all_ref, dq_ref, dk_ref, dv_ref, own, other):
    rows = all_ref[...].reshape(MP * LOCAL, D)
    for n, ref in enumerate((dq_ref, dk_ref, dv_ref)):
        grad = dot(ref[...].reshape(MP * LOCAL, HEAD).T, rows)
        store_blocks(ids_ref, grad, own, other, n)


def heads_back_kernel(
    got_ref,
    q_ref,
    k_ref,
    v_ref,
    log_ref,
    sent_ref,
    dq_ref,
    dk_ref,
    dv_ref,
):
    scale = HEAD**-0.5
    for i in range(ITEMS):
        q, k, v, g = (ref[:, i].reshape(NLAT, HEAD) for ref in (q_ref, k_ref, v_ref, got_ref))
        attention = jnp.exp(dot_t(k, q) * scale - log_ref[i : i + 1])
        grad_attention = dot_t(v, g)
        delta = jnp.sum(attention * grad_attention, axis=0, keepdims=True)
        dv = dot(attention.astype(bf16), g)
        grad_scores = (attention * (grad_attention - delta)).astype(bf16)
        dk = dot(grad_scores, q) * scale
        dq = dot(k.T, grad_scores).T * scale
        for ref, grad in ((dq_ref, dq), (dk_ref, dk), (dv_ref, dv)):
            ref[:, i] = grad.astype(bf16).reshape(MP, ROWS, HEAD)
    for s in range(MP):
        for n, ref in enumerate((dq_ref, dk_ref, dv_ref)):
            sent_ref[s, :, n * HEAD : (n + 1) * HEAD] = ref[s].reshape(LOCAL, HEAD)


def feed_back_kernel(
    ids_ref,
    got_ref,
    two_ref,
    one_ref,
    up_ref,
    slope_ref,
    mixed_ref,
    lse_ref,
    map_own,
    map_other,
    gain_feed,
    gain_self,
    *refs,
):
    pieces, self_pieces, refs = refs[: 2 * QUART], refs[2 * QUART : 2 * QUART + 2], refs[10:]
    sent_ref, down_ref, before_ref, branch_ref, grad_self_ref, grad_feed_ref = refs[:6]
    pack_ref, grad_pixel_ref, self_ref, self_sems, full_ref, sems = refs[6:]
    self_copies = fetch_all(ids_ref, self_pieces, self_ref, self_sems, 3)
    copies = fetch_steps(ids_ref, pieces, full_ref, sems)
    core = ids_ref[0]
    grad_hidden = 0.0
    for n in range(3):
        block = slice(n * HEAD, (n + 1) * HEAD)
        grad = jnp.concatenate([got_ref[s, :, block] for s in range(MP)], axis=1)
        arrive(self_copies, n)
        grad_hidden = grad_hidden + times_out(grad, self_ref, n)
    unit, scale = normal(two_ref[...])
    grad, grad_gain = normal_back(unit, scale, gain_self[...], grad_hidden)
    grad_self_ref[...] = grad_gain
    upstream = up_ref[...] + grad
    dy = upstream.astype(bf16)
    branch_ref[...] = dy
    arrive(copies, 1)
    grad_active = times_in(dy, full_ref, 1)
    grad_before = (grad_active * slope_ref[...]).astype(bf16)
    before_ref[...] = grad_before
    arrive(copies, 0)
    grad_hidden = times_out(grad_before, full_ref, 0)
    unit, scale = normal(one_ref[...])
    grad, grad_gain = normal_back(unit, scale, gain_feed[...], grad_hidden)
    grad_feed_ref[...] = grad_gain
    upstream = upstream + grad
    down_ref[...] = upstream
    dy = upstream.astype(bf16)
    pack_ref[...] = jnp.concatenate(
        [before_ref[...], pick(core, branch_ref[...], False), pick(core, dy, False)], axis=1
    )
    grad_mixed = halves(
        core, dot_t(side_by_side(map_own, HALF), dy), dot_t(side_by_side(map_other, HALF), dy), 0
    )[:CP]
    shared = grad_mixed * mixed_ref[...]
    delta = jnp.sum(shared, axis=0, keepdims=True)
    grad_pixel_ref[...] = as_row(jnp.sum(shared, axis=1, keepdims=True))
    sent = with_tail(grad_mixed, split3(lse_ref[...]) + split3(delta)).astype(bf16)
    for s in range(MP):
        sent_ref[s] = sent


def feed_grads_kernel(
    ids_ref,
    hidden_ref,
    active_ref,
    before_ref,
    branch_ref,
    down_ref,
    mixed_ref,
    got_mixed_ref,
    got_state_ref,
    got_ref,
    *refs,
):
    parts, mix_ref, right_ref = refs[:QUART], refs[QUART], refs[QUART + 1]
    core = ids_ref[0]
    own = pick(core, hidden_ref[...], True), pick(core, branch_ref[...], True)
    got = got_state_ref[:, D:], got_ref[:, D : D + WIDE]
    lefts = (before_ref, got_ref), (active_ref, got_state_ref)
    for j in range(2):
        left = stacked(lefts[j][0][...], lefts[j][1][:, :D])
        store_parts(ids_ref, left, stacked(own[j], got[j]), right_ref, parts, j, 2)
    right = stacked(pick(core, down_ref[...], True).astype(bf16), got_ref[:, D + WIDE :])
    mixed = jnp.concatenate([mixed_ref[...], got_mixed_ref[...]], axis=1)
    mix_ref[...] = dot(mixed, right)


def cross_back_kernel(
    ids_ref,
    rows_ref,
    flat_ref,
    items_ref,
    told_ref,
    normed_ref,
    gain_feed,
    gain_self,
    gain_last,
    gain_pixel,
    sent_ref,
    other_ref,
    own_ref,
    grad_ref,
):
    core = ids_ref[0]
    ids = lax.broadcasted_iota(jnp.int32, (CP, 1), 0)
    partials = []
    total, pixel = 0.0, 0.0
    for i, told in enumerate(to_items(told_ref)):
        slots = slice(i * SLOTS, (i + 1) * SLOTS)
        log, delta = join3(told, C + 1), join3(told, C + 4)
        told = jnp.where(ids < C, told, 0.0).astype(bf16)
        asked = items_ref[i]
        attention = jnp.exp(dot(rows_ref[slots], asked) - log)
        grad_attention = dot(rows_ref[slots], told)
        grad_scores = (attention * (grad_attention - delta)).astype(bf16)
        grad_ref[slots] = dot_t(grad_scores, asked) + dot_t(attention.astype(bf16), told)
        partial = dot(flat_ref[:, slots], grad_scores)
        partials.append(partial)
        normed = normed_ref[:, i * ROWS : (i + 1) * ROWS].reshape(NLAT, D)
        total = total + dot(partial.astype(bf16), normed)
        pixel = pixel + jnp.sum(partial * asked.astype(f32), axis=1, keepdims=True)
    store_by_peer(sent_ref, *partials)
    total = total * (D**-0.5)
    pixel = as_row(pixel) + gain_pixel[...]
    pixel = jnp.concatenate([pixel, jnp.zeros((1, D - CP), f32)], axis=1)
    gains = [gain_feed[...], gain_self[...], gain_last[...], pixel]
    ids = lax.broadcasted_iota(jnp.int32, (CP - 256, 1), 0) + 256
    for first, ref in ((True, own_ref), (False, other_ref)):
        half = pick(core, total, first)
        tail = half[256:]
        for n, gain in enumerate(gains):
            row = pick(core, gain, first)
            if not first:
                high = row.astype(bf16).astype(f32)
                tail = jnp.where(ids == C + 4 + n, row - high, tail)
                row = high
            tail = jnp.where(ids == C + n, row, tail)
        total_half = jnp.concatenate([half[:256], tail], axis=0)
        ref[...] = total_half if first else total_half.astype(bf16)


def pixel_back_kernel(pixel_ref, grad_ref, gain_ref, out_ref):
    unit, scale = normal(pixel_ref[...].astype(f32))
    grad, _ = normal_back(unit, scale, gain_ref[...], grad_ref[:, :C])
    out_ref[...] = grad


def latent_back_kernel(
    ids_ref, got_ref, latent_ref, gain_ref, map_own, map_other, down_ref, grad_ref
):
    core = ids_ref[0]
    asked = got_ref[0, :CP].astype(f32)
    for s in range(1, MP):
        asked = asked + got_ref[s, :CP].astype(f32)
    ids = lax.broadcasted_iota(jnp.int32, (CP, 1), 0)
    asked = jnp.where(ids < C, asked * (D**-0.5), 0.0)
    unit, scale = normal(latent_ref[...].astype(f32))
    padded = jnp.concatenate([asked, jnp.zeros((CH - CP, LOCAL), f32)], axis=0)
    grad_normed = 0.0
    for first, ref in ((True, map_own), (False, map_other)):
        part = pick_rows(core, padded, first)
        grad_normed = grad_normed + dot(part.T.astype(bf16), side_by_side(ref, 0))
    grad, _ = normal_back(unit, scale, gain_ref[...], grad_normed)
    grad_ref[...] = down_ref[...] + grad


def total_kernel(partial_ref, got_ref, own_ref, mix_ref, sent_ref):
    got = got_ref[...].astype(f32)
    score = own_ref[...] + got
    ids = lax.broadcasted_iota(jnp.int32, (CP - 256, 1), 0) + 256
    tail = score[256:]
    for n in range(4):
        row = C - 256 + n
        gain = tail[row : row + 1] + got[C + 4 + n : C + 5 + n]
        high = gain.astype(bf16).astype(f32)
        tail = jnp.where(ids == C + n, high, tail)
        tail = jnp.where(ids == C + 4 + n, gain - high, tail)
    rest = jnp.zeros((MP * PART - 2 * CP, WIDE), f32)
    total = jnp.concatenate([mix_ref[...], score[:256], tail, rest], axis=0)
    for s in range(MP):
        sent_ref[s, :CP] = partial_ref[s]
        rows = total[s * PART : (s + 1) * PART].astype(bf16)
        for q in range(QUART):
            start = CP + q * PART
            sent_ref[s, start : start + PART] = rows[:, q * HEAD : (q + 1) * HEAD]


def peer_sum(ref, rows):
    total = ref[0, rows].astype(f32)
    for s in range(1, MP):
        total = total + ref[s, rows].astype(f32)
    return total.astype(bf16)


def spread_kernel(got_ref, sent_ref):
    total = peer_sum(got_ref, slice(CP, CP + SHARE))
    for s in range(MP):
        sent_ref[s] = total


def feed_kernel(got_ref, *refs):
    parts, sent_ref = refs[:QUART], refs[QUART]
    total = peer_sum(got_ref, slice(0, SHARE))
    for s in range(MP):
        sent_ref[s, :SHARE] = total
        for j in range(2):
            value = parts[0][s * 2 + j].astype(f32)
            for part in parts[1:]:
                value = value + part[s * 2 + j].astype(f32)
            start = SHARE + j * HEAD
            sent_ref[s, start : start + HEAD] = value.astype(bf16)


def tiles_out_kernel(got_ref, kept_ref, far_ref, sent_ref):
    total = peer_sum(got_ref, slice(SHARE, SHARE + 2 * HEAD))
    tiles = [(kept_ref[j].astype(f32) + far_ref[j].astype(f32)).astype(bf16) for j in range(3)]
    for s in range(MP):
        sent_ref[s, : 2 * HEAD] = total
        for j, tile in enumerate(tiles):
            sent_ref[s, (2 + j) * HEAD : (3 + j) * HEAD] = tile


def cross_grads_kernel(
    ids_ref,
    own_ref,
    other_ref,
    key_ref,
    query_ref,
    value_own,
    value_other,
    rows_own,
    rows_other,
    map_own,
    map_other,
    gain_latent,
    gain_pixel,
    grad_query_ref,
    grad_key_ref,
    grad_value_ref,
    grad_out_ref,
    *refs,
):
    gain_refs, pad_ref, mix_ref = refs[:5], refs[5], refs[6]
    core, mine = ids_ref[0], ids_ref[2]
    pad_ref[...] = jnp.zeros(pad_ref.shape, f32)
    pad_ref[:C] = key_ref[...].astype(f32)
    key = pad_ref[...].astype(bf16)
    out_rows = [
        jnp.concatenate([ref[s] for s in range(MP)], axis=1) for ref in (rows_own, rows_other)
    ]
    out_rows = halves(core, out_rows[0], out_rows[1], 0)
    block = pl.ds(pl.multiple_of(lax.rem(mine, QUART) * HEAD, HEAD), HEAD)
    score_map = halves(core, side_by_side(map_own, 0), side_by_side(map_other, 0), 0)
    score_map = score_map[:CP].astype(f32)
    ids = lax.broadcasted_iota(jnp.int32, (CP, 1), 0)
    grad_key, grad_value = 0.0, 0.0
    gains, mixes = [], []
    for side, ref in enumerate((own_ref, other_ref)):
        half = core if side == 0 else 1 - core
        span = pl.ds(pl.multiple_of(half * WIDE, WIDE), WIDE)
        whole = jnp.concatenate(
            [
                jnp.concatenate([ref[s, q * PART : (q + 1) * PART] for q in range(QUART)], axis=1)
                for s in range(MP)
            ],
            axis=0,
        )
        mix, score = whole[:CP], whole[CP : 2 * CP]
        mixes.append(mix)
        grad_query_ref[span, :] = dot(score.T, key)
        grad_key = grad_key + dot(score, query_ref[span, :])
        grad_value = grad_value + dot_t(mix, pick(core, out_rows, side == 0))
        tail = score[256:].astype(f32)
        rows = tail[C - 256 : C - 252] + tail[C - 252 : C - 248]
        product = jnp.where(ids < C, score.astype(f32), 0.0) * pick(core, score_map, side == 0)
        first = jnp.sum(product, axis=0, keepdims=True)
        gains.append(jnp.concatenate([first, rows], axis=0))
    grad_key_ref[...] = grad_key[:C]
    grad_value_ref[...] = grad_value[:C]
    gains = halves(core, gains[0], gains[1], 1)
    gain_refs[0][...] = (gains[:1] / gain_latent[...])[0]
    for n in range(1, 4):
        gain_refs[n][...] = gains[n]
    gain_refs[4][...] = (gains[4:5, :C] / gain_pixel[...])[0]
    half = lax.div(mine, QUART)
    mix_ref[0], mix_ref[1] = mixes[0], mixes[1]
    mix = jnp.where(half == core, mix_ref[0, :, block], mix_ref[1, :, block])
    mix = jnp.concatenate([mix, jnp.zeros((CH - CP, HEAD), bf16)], axis=0)
    grad_out_ref[...] = dot(value_own[...].T, pick_rows(core, mix, True)) + dot(
        value_other[...].T, pick_rows(core, mix, False)
    )


def finish_kernel(turned_outs, ids_ref, own_ref, other_ref, *outs):
    core = ids_ref[0]
    for side, ref in enumerate((own_ref, other_ref)):
        half = core if side == 0 else 1 - core
        for q in range(QUART):
            span = pl.ds(pl.multiple_of((half * QUART + q) * HEAD, HEAD), HEAD)
            for j, out in enumerate(outs):
                if j >= 6:
                    rows = slice((j - 6) * HEAD, (j - 5) * HEAD)
                    piece = ref[q, rows].astype(f32) + ref[QUART + q, rows].astype(f32)
                else:
                    rows = slice((2 + j % 3) * HEAD, (3 + j % 3) * HEAD)
                    piece = ref[q + QUART * (j // 3), rows].astype(f32)
                if turned_outs[j]:
                    out[span, :] = piece.T
                else:
                    out[:, span] = piece


def body(
    latents,
    pixels,
    masks,
    cotangent,
    norm_latent,
    norm_pixel,
    norm_feed,
    norm_self,
    norm_last,
    cross_query,
    cross_key,
    cross_value,
    cross_out,
    feed_in,
    feed_out,
    self_query,
    self_key,
    self_value,
    self_out,
    last_in,
    last_out,
):
    core = lax.axis_index("dp") % 2
    mine = lax.axis_index("mp")
    depth = (lax.axis_index("dp") // 2) % QUART
    core_id = jnp.stack([core, depth, mine]).astype(jnp.int32)
    gain_latent, gain_pixel, gain_feed, gain_self, gain_last = (
        g[None, :] for g in (norm_latent, norm_pixel, norm_feed, norm_self, norm_last)
    )
    latent_rows = latents.reshape(LOCAL, D)
    pixel_rows = pixels.reshape(ITEMS * SLOTS, C)
    cotangent_rows = cotangent.reshape(LOCAL, D)
    row_f32, row_bf16 = ((LOCAL, D), f32), ((LOCAL, D), bf16)
    gain_row = ((1, D), f32)

    def come(x, step):
        return lax.ppermute(x, "dp", DEPTH[QUART - step])

    map_shape = ((MP, CH, HEAD), bf16)
    sent, tile = run(
        map_start_kernel,
        2,
        [((MP, CH + 2 * HEAD + ROWS, HEAD), bf16), ((6, HEAD, HEAD), bf16)],
        core_id,
        cross_key,
        cross_query,
        cross_value,
        feed_in,
        feed_out,
        self_out,
        last_in,
        last_out,
        self_query,
        self_key,
        self_value,
        cross_out,
        scratch=[pltpu.VMEM((2, CH, HEAD), f32)],
    )
    pixel_in, pixel_flat = run(
        pixel_kernel,
        2,
        [((ITEMS * SLOTS, CP), bf16), ((CP, ITEMS * SLOTS), bf16)],
        pixel_rows,
        masks,
        gain_pixel,
        scratch=[pltpu.VMEM((ITEMS * SLOTS, 384), f32)],
        hot_outs=(),
    )
    packs = lax.all_gather(tile, "mp")
    got, (pixel_in, pixel_flat) = after(exchange(sent), pixel_in, pixel_flat)

    def along(x):
        return lax.all_gather(x, "dp", axis_index_groups=ALONG_Z)

    sent, value_half, feed_pack, out_rows = run(
        map_sum_kernel,
        1,
        [
            map_shape,
            ((HALF, D), bf16),
            ((MP, 2, HEAD, HEAD), bf16),
            ((MP, ROWS, HEAD), bf16),
        ],
        got,
        cross_out,
        hot=(0,),
    )
    feed_pieces = [feed_pack, None, come(feed_pack, 2), None]
    map_own, (packs, feed_pieces[2]) = after(exchange(sent), packs, feed_pieces[2])
    map_other = core_swap(map_own)
    packs = along(packs)
    peer_shape = ((MP, CP, HEAD), bf16)
    sent, normed = run(
        asked_kernel,
        1,
        [peer_shape, row_bf16],
        core_id,
        map_own,
        map_other,
        latent_rows,
        gain_latent,
        hot=(1, 2),
        hot_outs=(),
    )
    feed_pieces[1], feed_pieces[3] = come(feed_pack, 1), come(feed_pack, 3)
    asked_all, (feed_pieces[1], feed_pieces[3]) = after(
        exchange(sent), feed_pieces[1], feed_pieces[3]
    )
    feed_pieces = feed_pieces + [core_swap(v) for v in feed_pieces]
    sent, asked_items = run(
        cross_kernel,
        3,
        [peer_shape, ((ITEMS, CP, NLAT), bf16)],
        pixel_in,
        pixel_flat,
        asked_all,
        hot=(2,),
        hot_outs=(),
    )
    sent, mixed, lse, state_one, feed_hidden, feed_active, feed_slope, state_two, mixed_low, state_pack = run(
        state_kernel,
        4,
        [
            ((MP, LOCAL, D), bf16),
            ((CP, LOCAL), f32),
            ((1, LOCAL), f32),
            row_f32,
            row_bf16,
            row_bf16,
            row_f32,
            row_f32,
            ((CP, LOCAL), bf16),
            ((LOCAL, D + WIDE), bf16),
        ],
        core_id,
        exchange(sent),
        latent_rows,
        map_own,
        map_other,
        gain_feed,
        gain_self,
        *feed_pieces,
        scratch=full_shape(2),
        far=range(7, 15),
        hot=(1,),
        hot_outs=(),
    )

    hidden_all, (packs, normed, got_mixed, got_state) = after(
        exchange(sent), packs, normed, core_swap(mixed_low), core_swap(state_pack)
    )
    other_packs = core_swap(packs)
    normed_all = lax.all_gather(normed, "mp")
    heads_shape = ((MP, ITEMS, ROWS, HEAD), bf16)
    sent, queries, keys, values, logs = run(
        heads_kernel,
        3,
        [heads_shape] * 4 + [((ITEMS, NLAT), f32)],
        hidden_all,
        self_query,
        self_key,
        self_value,
        hot=(0,),
    )
    got = exchange(sent)
    sent, up, result, heads_out, last_hidden, last_active, last_before, grad_last, back_pack = run(
        last_kernel,
        6,
        [
            ((MP, LOCAL, HEAD), bf16),
            row_f32,
            row_bf16,
            row_bf16,
            row_bf16,
            row_bf16,
            row_bf16,
            gain_row,
            ((LOCAL, 3 * (D + WIDE)), bf16),
        ],
        core_id,
        got.reshape(MP, LOCAL, HEAD),
        state_two,
        gain_last,
        cotangent_rows,
        packs,
        other_packs,
        scratch=full_shape(3) + [pltpu.VMEM((LOCAL, D), f32)],
        pinned=(5, 6),
        hot=(1,),
    )

    def tiles(count):
        return ((QUART, count, HEAD, HEAD), bf16)

    def along_sum(x):
        count = x.shape[1]
        x = x.reshape(QUART * count * HEAD, HEAD)
        x = lax.psum_scatter(x, "dp", axis_index_groups=ALONG_Z, tiled=True)
        return x.reshape(count, HEAD, HEAD)

    (last_own,) = run(
        last_grads_kernel,
        3,
        [tiles(3 * MP)],
        core_id,
        heads_out,
        up,
        last_hidden,
        last_active,
        last_before,
        cotangent_rows,
        core_swap(back_pack),
        hot=(7,),
        hot_outs=(),
    )
    grad_heads, (last_own,) = after(exchange(sent), last_own)

    def give(parts):
        return [lax.ppermute(parts[step], "dp", DEPTH[step]) for step in (1, 2, 3)]

    def all_of(first, *others):
        total = first.astype(f32)
        for other in others:
            total = total + other.astype(f32)
        return total.astype(bf16)

    grad_heads = grad_heads.reshape(MP, ITEMS, ROWS, HEAD)
    sent, dq, dk, dv = run(
        heads_back_kernel,
        4,
        [((MP, LOCAL, 3 * HEAD), bf16)] + [heads_shape] * 3,
        grad_heads,
        queries,
        keys,
        values,
        logs,
        hot=(0,),
    )
    last_own, (normed_all, _) = after(last_own, normed_all, dq)
    last_sum = along_sum(last_own)
    self_own, self_other = run(
        heads_grads_kernel, 2, [tiles(3)] * 2, core_id, hidden_all, dq, dk, dv, hot_outs=()
    )
    self_parts = (self_own.astype(f32) + core_swap(self_other).astype(f32)).astype(bf16)
    got, (self_parts,) = after(exchange(sent), self_parts)
    sent, down, feed_before, feed_branch, grad_self, grad_feed, feed_back, grad_pixel = run(
        feed_back_kernel,
        4,
        [peer_shape, row_f32, row_bf16, row_bf16, gain_row, gain_row, ((LOCAL, 2 * D), bf16), ((1, CP), f32)],
        core_id,
        got,
        state_two,
        state_one,
        up,
        feed_slope,
        mixed,
        lse,
        map_own,
        map_other,
        gain_feed,
        gain_self,
        *feed_pieces,
        packs,
        other_packs,
        scratch=full_shape(3) + full_shape(2),
        far=range(12, 20),
        pinned=(20, 21),
        hot=(1,),
    )
    *feed_parts, mix_own = run(
        feed_grads_kernel,
        2,
        [((2 * MP, HEAD, HEAD), bf16)] * QUART + [((CP, WIDE), f32)],
        core_id,
        feed_hidden,
        feed_active,
        feed_before,
        feed_branch,
        down,
        mixed_low,
        got_mixed,
        got_state,
        core_swap(feed_back),
        scratch=[pltpu.VMEM((2, 2 * LOCAL, WIDE), bf16)],
        loose=(7, 8),
        hot=(9,),
        hot_outs=(),
    )
    feed_got = give(feed_parts)
    last_sum, _ = after(last_sum, feed_parts[0])
    told_all, (self_parts, *_) = after(exchange(sent), self_parts, *feed_parts)
    self_got = give(self_parts)
    last_rows = last_sum.reshape(MP * 3 * HEAD, HEAD)
    last_piece = lax.psum_scatter(last_rows, "mp", tiled=True).reshape(3, HEAD, HEAD)
    partial, other, own, grad_pixel_in = run(
        cross_back_kernel,
        4,
        [peer_shape, ((CP, WIDE), bf16), ((CP, WIDE), f32), ((ITEMS * SLOTS, CP), f32)],
        core_id,
        pixel_in,
        pixel_flat,
        asked_items,
        told_all,
        normed_all,
        grad_feed,
        grad_self,
        grad_last,
        grad_pixel,
        hot=(4,),
        hot_outs=(0, 1, 2),
    )
    other, (feed_got[0], feed_got[2]) = after(core_swap(other), feed_got[0], feed_got[2])
    (sent,) = run(
        total_kernel,
        1,
        [((MP, CP + SHARE, HEAD), bf16)],
        partial,
        other,
        own,
        mix_own,
        hot=(0, 1, 2),
    )
    (grad_pixels,) = run(
        pixel_back_kernel,
        2,
        [((ITEMS * SLOTS, C), f32)],
        pixel_rows,
        grad_pixel_in,
        gain_pixel,
        hot_outs=(),
    )
    grad_pixels = grad_pixels.reshape(ITEMS, SLOTS, C).transpose(2, 0, 1)
    self_sum = all_of(self_parts[0], *self_got)
    got, (grad_pixels, self_sum, feed_got[1]) = after(
        exchange(sent), grad_pixels, self_sum, feed_got[1]
    )
    share_shape = ((MP, SHARE, HEAD), bf16)
    (sent,) = run(spread_kernel, 1, [share_shape], got, hot=(0,))
    (grad_latents,) = run(
        latent_back_kernel,
        2,
        [row_f32],
        core_id,
        got,
        latent_rows,
        gain_latent,
        map_own,
        map_other,
        down,
        hot=(1,),
        hot_outs=(),
    )
    got, (grad_latents,) = after(grouped(sent, "dp", COPIES), grad_latents)
    (sent,) = run(
        feed_kernel,
        1,
        [((MP, SHARE + 2 * HEAD, HEAD), bf16)],
        got,
        feed_parts[0],
        *feed_got,
        hot=(0,),
        loose=(2, 3, 4),
    )
    row = lax.axis_index("dp") // 8
    kept = jnp.where(row == 0, last_piece, self_sum)
    far = lax.ppermute(jnp.where(row == 0, self_sum, last_piece), "dp", FAR)
    own, (kept, far) = after(exchange(sent), kept, far)
    (sent,) = run(
        tiles_out_kernel,
        1,
        [((MP, 5 * HEAD, HEAD), bf16)],
        own,
        kept,
        far,
        hot=(0,),
        hot_outs=(),
        loose=(1, 2),
    )
    other = core_swap(own)
    row_out, key_out = ((D, HEAD), f32), ((C, HEAD), f32)
    cross = run(
        cross_grads_kernel,
        3,
        [row_out, key_out, key_out, row_out] + [((D,), f32)] * 4 + [((C,), f32)],
        core_id,
        own,
        other,
        cross_key,
        cross_query,
        value_half,
        core_swap(value_half),
        out_rows,
        core_swap(out_rows),
        map_own,
        map_other,
        gain_latent,
        gain_pixel,
        scratch=[pltpu.VMEM((CP, HEAD), f32), pltpu.VMEM((2, CP, WIDE), bf16)],
        hot=(1, 2),
        loose=(6, 8),
        hot_outs=(),
    )
    own, cross = after(grouped(sent, "dp", COPIES), *cross)
    grad_cross_query, grad_cross_key, grad_cross_value, grad_cross_out, *gains = cross
    flips = (False, True, False, True, True, True, True, False)
    finished = run(
        functools.partial(finish_kernel, flips),
        2,
        [((D, HEAD) if flip else (HEAD, D), f32) for flip in flips],
        core_id,
        own,
        core_swap(own),
        hot=(1, 2),
        hot_outs=(),
    )
    grad_self_out, grad_last_in, grad_last_out, grad_sq, grad_sk, grad_sv = finished[:6]
    grad_feed_in, grad_feed_out = finished[6:]
    shape = (ITEMS, ROWS, D)
    return (
        result.reshape(shape),
        grad_latents.reshape(shape),
        grad_pixels.transpose(1, 2, 0),
        gains[0],
        gains[4],
        gains[1],
        gains[2],
        gains[3],
        grad_cross_query,
        grad_cross_key,
        grad_cross_value,
        grad_cross_out,
        grad_feed_in,
        grad_feed_out,
        grad_sq,
        grad_sk,
        grad_sv,
        grad_self_out,
        grad_last_in,
        grad_last_out,
    )


def solution(mesh):
    rows = P("dp", "mp", None)
    columns = P(None, "mp")
    depth = P("mp", None)
    return jax.shard_map(
        body,
        mesh=mesh,
        in_specs=(rows, rows, P("dp", "mp"), rows)
        + (P(),) * 5
        + (columns,) * 5
        + (depth,)
        + (columns,) * 3
        + (depth, columns, depth),
        out_specs=(rows,) * 3
        + (P(),) * 5
        + (columns,) * 5
        + (depth,)
        + (columns,) * 3
        + (depth, columns, depth),
        check_vma=False,
    )
```
